32 devices in a mesh: dp: 4 (over y, x), tensor: 8 (over z, core).
Axes of the slice: x: 2, y: 2, z: 4, core: 2. Of those that a mesh axis runs over, the one named last changes fastest.
Arguments:
- tokens: float32 [13824, 1024], P(('dp', 'tensor')), may hold values from -6 to 6
- cotangent: float32 [13824, 1024], P(('dp', 'tensor')), may hold values from -6 to 6
- vectors: float32 [6, 1024], replicated, may hold values from -0.9 to 1.9, as said below
- vectors_m: float32 [6, 1024], replicated, may hold values from -80 to 80
- vectors_v: float32 [6, 1024], replicated, may hold values from 6.912 to 110.592
- w_qkv: float32 [1024, 3072], P('dp', 'tensor'), may hold values from -0.25 to 0.25
- qkv_m: float32 [1024, 3072], P('dp', 'tensor'), may hold values from -80 to 80
- qkv_v: float32 [1024, 3072], P('dp', 'tensor'), may hold values from 6.912 to 110.592
- w_out: float32 [1024, 1024], P('tensor', 'dp'), may hold values from -0.5 to 0.5
- out_m: float32 [1024, 1024], P('tensor', 'dp'), may hold values from -32 to 32
- out_v: float32 [1024, 1024], P('tensor', 'dp'), may hold values from 1.10592 to 17.69472
- w_up: float32 [1024, 4096], P('dp', 'tensor'), may hold values from -0.1875 to 0.1875
- up_m: float32 [1024, 4096], P('dp', 'tensor'), may hold values from -24 to 24
- up_v: float32 [1024, 4096], P('dp', 'tensor'), may hold values from 0.62208 to 9.95328
- hidden_bias: float32 [4096], P('tensor'), may hold values from -3 to 3
- bias_m: float32 [4096], P('tensor'), may hold values from -24 to 24
- bias_v: float32 [4096], P('tensor'), may hold values from 0.62208 to 9.95328
- w_down: float32 [4096, 1024], P('tensor', 'dp'), may hold values from -0.09375 to 0.09375
- down_m: float32 [4096, 1024], P('tensor', 'dp'), may hold values from -48 to 48
- down_v: float32 [4096, 1024], P('tensor', 'dp'), may hold values from 2.48832 to 39.81312
Outputs:
- output: float32 [13824, 1024], P(('dp', 'tensor'))
- input_grad: float32 [13824, 1024], P(('dp', 'tensor'))
- vectors_grad: float32 [6, 1024], replicated
- vectors_m_new: float32 [6, 1024], replicated
- vectors_v_new: float32 [6, 1024], replicated
- vectors_new: float32 [6, 1024], replicated
- qkv_grad: float32 [1024, 3072], P('dp', 'tensor')
- qkv_m_new: float32 [1024, 3072], P('dp', 'tensor')
- qkv_v_new: float32 [1024, 3072], P('dp', 'tensor')
- qkv_new: float32 [1024, 3072], P('dp', 'tensor')
- out_grad: float32 [1024, 1024], P('tensor', 'dp')
- out_m_new: float32 [1024, 1024], P('tensor', 'dp')
- out_v_new: float32 [1024, 1024], P('tensor', 'dp')
- out_new: float32 [1024, 1024], P('tensor', 'dp')
- up_grad: float32 [1024, 4096], P('dp', 'tensor')
- up_m_new: float32 [1024, 4096], P('dp', 'tensor')
- up_v_new: float32 [1024, 4096], P('dp', 'tensor')
- up_new: float32 [1024, 4096], P('dp', 'tensor')
- bias_grad: float32 [4096], P('tensor')
- bias_m_new: float32 [4096], P('tensor')
- bias_v_new: float32 [4096], P('tensor')
- bias_new: float32 [4096], P('tensor')
- down_grad: float32 [4096, 1024], P('tensor', 'dp')
- down_m_new: float32 [4096, 1024], P('tensor', 'dp')
- down_v_new: float32 [4096, 1024], P('tensor', 'dp')
- down_new: float32 [4096, 1024], P('tensor', 'dp')
The draws below stay inside these ranges and needn't reach their ends.
Inputs may be any that keep to these rules, and one draw needn't show every extreme that they name: `vectors`: rows 0 and 2 lie within 1 - 0.9 to 1 + 0.9, the other rows within -0.9 to 0.9.
All inputs are finite; a program needn't handle non-finite values.
Results may differ from the reference program's by a relative error of at most 0.018.
Values may be sent and summed in bfloat16 or wider, within the bound.
No kernel may reach another device: no remote copies, remote signals or barrier semaphores. Data moves between devices by JAX's collectives and lax.ppermute only.
A program may use at most 192 MiB of HBM per device.

```python
import math
import jax
import jax.numpy as jnp
from jax import lax

D = 1024
H = 16
HD = 64
FF = 4096
SEQ = 576
IMG_DEV = 6
STEP = 10
IMAGES = 24
TOKENS = 13824
N_DP = 4


def draw_vectors(key, part):
    key = jax.random.fold_in(key, 7)
    noise = jnp.clip(jax.random.normal(key, (6, D), jnp.float32), -3.0, 3.0)
    row_ids = lax.broadcasted_iota(jnp.int32, (6, D), 0)
    centre = jnp.where((row_ids == 0) | (row_ids == 2), 1.0, 0.0).astype(jnp.float32)
    return centre + 0.3 * noise


def levels(own_key, shape, split, low, top_value):
    def one(dim, shards_of):
        heights = jax.random.uniform(jax.random.fold_in(jax.random.fold_in(own_key, 6), dim), (shards_of,), jnp.float32, low / len(split), top_value / len(split))
        return jnp.repeat(jnp.exp(heights), shape[dim] // shards_of).reshape((-1,) + (1,) * (len(shape) - dim - 1))

    loudness = one(*split[0])
    for cut in split[1:]:
        loudness = loudness * one(*cut)
    return loudness


def bell_draw(key, extent, width, bound, split=(), kind=jnp.bfloat16):
    array = width * jax.random.normal(key, extent, jnp.float32)
    if split:
        array = array * levels(key, extent, split, -0.22, 0.18)
    return jnp.clip(array, -bound, bound).astype(kind)


def setup_inputs(seed: int = 0) -> dict:
    key_list = jax.random.split(jax.random.key(seed), 21)
    return {
        "tokens": bell_draw(key_list[0], (TOKENS, D), 1.0, 6.0, ((0, 32),), jnp.float32),
        "cotangent": bell_draw(key_list[1], (TOKENS, D), 1.0, 6.0, ((0, 32),), jnp.float32),
        "vectors": draw_vectors(jax.random.fold_in(key_list[20], 71), 0),
        "vectors_m": bell_draw(key_list[3], (6, D), (0.111 * (IMAGES * SEQ) ** 0.5), 80.0, (), jnp.float32),
        "vectors_v": jnp.clip(jnp.exp(jax.random.uniform(key_list[4], (6, D), jnp.float32, math.log(6.912), math.log(110.592))), 6.912, 110.592),
        "w_qkv": bell_draw(key_list[5], (D, 3 * D), (D // 2) ** -0.5, 0.25, ((0, 4), (1, 8)), jnp.float32),
        "qkv_m": bell_draw(key_list[6], (D, 3 * D), (0.111 * (IMAGES * SEQ) ** 0.5), 80.0, ((0, 4), (1, 8)), jnp.float32),
        "qkv_v": jnp.clip(jnp.exp(math.log(110.592) - 2.7725887 * jax.random.uniform(key_list[7], (D, 3 * D), jnp.float32) ** levels(key_list[7], (D, 3 * D), ((0, 4), (1, 8)), -0.2, 0.2)), 6.912, 110.592),
        "w_out": bell_draw(key_list[8], (D, D), (D // 8) ** -0.5, 0.5, ((0, 8), (1, 4)), jnp.float32),
        "out_m": bell_draw(key_list[9], (D, D), (0.044 * (IMAGES * SEQ) ** 0.5), 32.0, ((0, 8), (1, 4)), jnp.float32),
        "out_v": jnp.clip(jnp.exp(math.log(17.69472) - 2.7725887 * jax.random.uniform(key_list[10], (D, D), jnp.float32) ** levels(key_list[10], (D, D), ((0, 8), (1, 4)), -0.2, 0.2)), 1.10592, 17.69472),
        "w_up": bell_draw(key_list[11], (D, FF), D ** -0.5, 0.1875, ((0, 4), (1, 8)), jnp.float32),
        "up_m": bell_draw(key_list[12], (D, FF), (0.033 * (IMAGES * SEQ) ** 0.5), 24.0, ((0, 4), (1, 8)), jnp.float32),
        "up_v": jnp.clip(jnp.exp(math.log(9.95328) - 2.7725887 * jax.random.uniform(key_list[13], (D, FF), jnp.float32) ** levels(key_list[13], (D, FF), ((0, 4), (1, 8)), -0.2, 0.2)), 0.62208, 9.95328),
        "hidden_bias": bell_draw(key_list[14], (FF,), 0.5, 3.0, ((0, 8),), jnp.float32),
        "bias_m": bell_draw(key_list[15], (FF,), (0.033 * (IMAGES * SEQ) ** 0.5), 24.0, ((0, 8),), jnp.float32),
        "bias_v": jnp.clip(jnp.exp(math.log(9.95328) - 2.7725887 * jax.random.uniform(key_list[16], (FF,), jnp.float32) ** levels(key_list[16], (FF,), ((0, 8),), -0.2, 0.2)), 0.62208, 9.95328),
        "w_down": bell_draw(key_list[17], (FF, D), FF ** -0.5, 0.09375, ((0, 8), (1, 4)), jnp.float32),
        "down_m": bell_draw(key_list[18], (FF, D), (0.067 * (IMAGES * SEQ) ** 0.5), 48.0, ((0, 8), (1, 4)), jnp.float32),
        "down_v": jnp.clip(jnp.exp(math.log(39.81312) - 2.7725887 * jax.random.uniform(key_list[19], (FF, D), jnp.float32) ** levels(key_list[19], (FF, D), ((0, 8), (1, 4)), -0.2, 0.2)), 2.48832, 39.81312),
    }


@jax.custom_vjp
def low(v):
    return lax.optimization_barrier(v.astype(jnp.bfloat16)).astype(jnp.float32)

@jax.custom_vjp
def low_back(v):
    return v

def low_keep(v):
    return (low(v), None)

def low_pass(kept, grad):
    return (grad,)

def back_keep(v):
    return (v, None)

def back_low(kept, grad):
    return (low(grad),)
low.defvjp(low_keep, low_pass)
low_back.defvjp(back_keep, back_low)

def layer_norm(rows_in, gain, shift):
    centred = rows_in - lax.optimization_barrier(jnp.mean(rows_in, axis=-1, keepdims=True))
    spread = lax.optimization_barrier(jnp.mean(centred * centred, axis=-1, keepdims=True))
    return centred * lax.rsqrt(spread + 1e-06) * gain + shift

def one_image(qkv_image):
    parts = qkv_image.reshape(SEQ, H, 3, HD)
    scale = 1.0 / math.sqrt(HD)
    scores = jnp.einsum('qhd,khd->hqk', parts[:, :, 0], parts[:, :, 1], precision=lax.Precision.HIGHEST)
    scores = low_back(scores * scale)
    weights_soft = low(jax.nn.softmax(scores, axis=-1))
    mixed_out = jnp.einsum('hqk,khd->qhd', weights_soft, parts[:, :, 2], precision=lax.Precision.HIGHEST)
    return mixed_out.reshape(SEQ, D)

def forward(group_tokens, vectors, w_qkv, w_out, w_up, hidden_bias, w_down):
    highest = lax.Precision.HIGHEST
    row_total = group_tokens.shape[0]
    normed_one = low(layer_norm(group_tokens, vectors[0], vectors[1]))
    qkv_rows = low(low_back(jnp.dot(normed_one, low(w_qkv), precision=highest)))
    attended = lax.map(jax.checkpoint(one_image), qkv_rows.reshape(row_total // SEQ, SEQ, 3 * D))
    attended = low(low_back(attended.reshape(row_total, D)))
    middle = group_tokens + low_back(jnp.dot(attended, low(w_out), precision=highest)) + vectors[4]
    normed_two = low(layer_norm(middle, vectors[2], vectors[3]))
    hidden_pre = low_back(jnp.dot(normed_two, low(w_up), precision=highest)) + hidden_bias
    hidden_act = low(jax.nn.gelu(hidden_pre, approximate=False))
    return middle + low_back(jnp.dot(hidden_act, low(w_down), precision=highest)) + vectors[5]

def adam_step(weight, gradient, first, second, rate, decay):
    first = 0.9 * first + 0.1 * gradient
    second = 0.999 * second + 0.001 * gradient * gradient
    first_fix = 1.0 - 0.9 ** STEP
    second_fix = 1.0 - 0.999 ** STEP
    update = first / first_fix / (jnp.sqrt(second / second_fix) + 1e-08) + decay * weight
    return (gradient, first, second, weight - rate * update)

def reference(tokens, cotangent, vectors, vectors_m, vectors_v, w_qkv, qkv_m, qkv_v, w_out, out_m, out_v, w_up, up_m, up_v, hidden_bias, bias_m, bias_v, w_down, down_m, down_v):
    params = (vectors, w_qkv, w_out, w_up, hidden_bias, w_down)
    group_size = IMG_DEV * SEQ
    token_groups = tokens.reshape(N_DP, group_size, D)
    cot_groups = cotangent.reshape(N_DP, group_size, D)

    def one_group(totals, item_parts):
        group_tokens, group_cot = item_parts
        result, pull_back = jax.vjp(forward, group_tokens, *params)
        gradients = pull_back(group_cot)
        new_totals = tuple((t + g for t, g in zip(totals, gradients[1:])))
        return (new_totals, (result, gradients[0]))
    empty_sums = tuple((jnp.zeros_like(p) for p in params))
    totals, (outputs, input_grads) = lax.scan(one_group, empty_sums, (token_groups, cot_groups))
    g_vec, g_qkv, g_out, g_up, g_bias, g_down = totals
    vec_res = adam_step(vectors, g_vec, vectors_m, vectors_v, 0.3, 0.0)
    qkv_res = adam_step(w_qkv, g_qkv, qkv_m, qkv_v, 0.1, 0.05)
    out_res = adam_step(w_out, g_out, out_m, out_v, 0.2, 0.05)
    up_res = adam_step(w_up, g_up, up_m, up_v, 0.1, 0.05)
    bias_res = adam_step(hidden_bias, g_bias, bias_m, bias_v, 0.3, 0.0)
    down_res = adam_step(w_down, g_down, down_m, down_v, 0.05, 0.05)
    return (outputs.reshape(TOKENS, D), input_grads.reshape(TOKENS, D), vec_res[0], vec_res[1], vec_res[2], vec_res[3], qkv_res[0], qkv_res[1], qkv_res[2], qkv_res[3], out_res[0], out_res[1], out_res[2], out_res[3], up_res[0], up_res[1], up_res[2], up_res[3], bias_res[0], bias_res[1], bias_res[2], bias_res[3], down_res[0], down_res[1], down_res[2], down_res[3])
```

```python
import math

import jax
import jax.numpy as jnp
from jax import lax
from jax.experimental import pallas as pl
from jax.experimental.pallas import tpu as pltpu
from jax.sharding import PartitionSpec as P

HD = 64
SEQ = 576
STEP = 10
NZ = 4
BIAS_ROWS = 16
AXES = ("dp", "tensor")
F32 = jnp.float32
BF16 = jnp.bfloat16
VMEM_LIMIT = 63 * 1024 * 1024
TIMES = {"first_norm": 5, "attend_whole_back": 1000}


def nn(left, right):
    return jnp.dot(left, right, preferred_element_type=F32)


def nt(left, right):
    return lax.dot_general(left, right, (((1,), (1,)), ((), ())), preferred_element_type=F32)


def tn(left, right):
    return lax.dot_general(left, right, (((0,), (0,)), ((), ())), preferred_element_type=F32)


def cost(name, nbytes):
    return pl.CostEstimate(flops=int(5e8 * TIMES.get(name, 0)), bytes_accessed=int(nbytes), transcendentals=0)


def call(body, name, grid, scalars, in_specs, out_specs, out_shape, args, scratch=(), after=(), hold=(), nbytes=0):
    given, extra = len(args), len(after) + len(hold)
    single = not isinstance(out_shape, (list, tuple))
    out_specs, out_shape = ([out_specs], [out_shape]) if single else (list(out_specs), list(out_shape))
    made = len(out_shape)

    def run(sc, *refs):
        rest = refs[given + extra :]
        body(sc, *refs[:given], *rest[:made], *rest[made + len(hold) :])

    anywhere = pl.BlockSpec(memory_space=pltpu.HBM)
    first = 1 + given + len(after)
    out = pl.pallas_call(
        run,
        name=name,
        grid_spec=pltpu.PrefetchScalarGridSpec(
            num_scalar_prefetch=1,
            grid=grid,
            in_specs=list(in_specs) + [anywhere] * extra,
            out_specs=out_specs + [anywhere] * len(hold),
            scratch_shapes=list(scratch),
        ),
        out_shape=out_shape + [shape(h.shape, h.dtype) for h in hold],
        input_output_aliases={first + i: made + i for i in range(len(hold))},
        compiler_params=pltpu.CompilerParams(vmem_limit_bytes=VMEM_LIMIT),
        cost_estimate=cost(name, nbytes),
    )(scalars, *args, *after, *hold)
    return out[0] if single and not hold else tuple(out)


def shape(dims, dtype):
    return jax.ShapeDtypeStruct(dims, dtype)


def whole(dims):
    return pl.BlockSpec(dims, lambda *_: (0,) * len(dims))


def slot(dims):
    return pl.BlockSpec((1,) + dims, lambda s, *_: (s, 0, 0))


def lower_slots(dims):
    return pl.BlockSpec((1,) + dims, lambda s, *_: (jnp.minimum(s, NZ // 2 - 1), 0, 0))


def upper_slots(dims):
    return pl.BlockSpec((1,) + dims, lambda s, *_: (jnp.maximum(s - NZ // 2, 0), 0, 0))


class Copies:
    def __init__(self, sems):
        self.sems, self.used = sems, 0

    def start(self, source, target):
        copy = pltpu.make_async_copy(source, target, self.sems.at[self.used])
        self.used += 1
        copy.start()
        return copy


def wait(copies):
    for copy in copies:
        copy.wait()


def manual(body, name, scalars, args, out_shape, scratch, copies, after=(), hold=()):
    given, extra = len(args), len(after) + len(hold)
    nbytes = sum(math.prod(a.shape) * a.dtype.itemsize for a in list(args) + list(out_shape))

    def run(sc, *refs):
        rest = refs[given + extra :]
        body(sc, refs[:given], rest[: len(out_shape)], rest[len(out_shape) + len(hold) : -1], Copies(rest[-1]))

    anywhere = pl.BlockSpec(memory_space=pltpu.HBM)
    first = 1 + given + len(after)
    return pl.pallas_call(
        run,
        name=name,
        in_specs=[pl.BlockSpec(memory_space=pltpu.SMEM)] + [anywhere] * (given + extra),
        out_specs=[anywhere] * (len(out_shape) + len(hold)),
        out_shape=list(out_shape) + [shape(h.shape, h.dtype) for h in hold],
        input_output_aliases={first + i: len(out_shape) + i for i in range(len(hold))},
        scratch_shapes=list(scratch) + [pltpu.SemaphoreType.DMA((copies,))],
        compiler_params=pltpu.CompilerParams(vmem_limit_bytes=VMEM_LIMIT),
        cost_estimate=cost(name, nbytes),
    )(scalars, *args, *after, *hold)


def vmem(dims, dtype=BF16):
    return pltpu.VMEM(dims, dtype)


class Weights:
    def __init__(self, arrays, blocks, block, col, cols):
        full = arrays[0].shape[2]
        if (col % 128 or cols % 128) and cols != full:
            arrays, col, full = [a[:, :, col : col + cols] for a in arrays], 0, cols
        self.args, self.blocks, self.block = list(arrays), blocks, block
        self.col, self.cols, self.full = col, cols, full
        self.depth = block * len(blocks)
        self.flat = cols % 128 == 0
        self.scratch = vmem((self.depth, NZ * cols) if self.flat else (NZ, self.depth, cols))
        self.copies = len(blocks) * NZ

    def load(self, copies, refs, target, sc):
        by_slot = [[] for _ in range(NZ)]
        for z in range(NZ):
            for k, (row, places) in enumerate(self.blocks):
                number, place = places[z]
                source = refs[number].at[sc[3] ^ z if place is None else place, pl.ds(row, self.block), :]
                if self.cols != self.full:
                    source = source.at[:, pl.ds(self.col, self.cols)]
                rows = pl.ds(k * self.block, self.block)
                goal = target.at[rows, pl.ds(z * self.cols, self.cols)] if self.flat else target.at[z, rows, :]
                by_slot[z].append(copies.start(source, goal))
        return by_slot

    def slots(self, target, first, count):
        if self.flat:
            return target[:, first * self.cols : (first + count) * self.cols]
        assert count == 1
        return target[first]


def slots_at_once(cols):
    for step in (1, 2, 4):
        if cols * step % 512 == 0 and cols % 128 == 0:
            return step
    return 1


class Rows:
    def __init__(self, parts, ordered, swapped=0):
        self.ordered, self.swapped = ordered, swapped
        self.part = parts[0].shape[0]
        self.args = list(parts)
        self.count = self.part * len(parts)
        self.width = parts[0].shape[1]
        self.copies = len(parts) * max(1, swapped)

    def load(self, copies, refs, target, sc, first=0):
        started = []
        for j, ref in enumerate(refs):
            at = first + j * self.part
            if self.ordered and len(refs) > 1:
                at = pl.multiple_of((sc[1] ^ j) * self.part, 16)
            rows = pl.ds(at, self.part)
            if not self.swapped:
                started.append(copies.start(ref, target.at[rows, :]))
                continue
            block = self.width // self.swapped
            for k in range(self.swapped):
                source = ref.at[:, pl.ds((k ^ 1) * block, block)]
                started.append(copies.start(source, target.at[rows, pl.ds(k * block, block)]))
        return started


class Slots:
    def __init__(self, array):
        self.args, self.copies = [array], NZ
        _, self.count, self.cols = array.shape

    def load(self, copies, refs, target, sc, first=0):
        return [[copies.start(refs[0].at[z], target.at[z, pl.ds(first, self.count), :])] for z in range(NZ)]


class SplitSlots:
    def __init__(self, full, mine, theirs):
        self.args, self.copies = [full, mine, theirs], 2 * NZ
        self.count, self.cols = full.shape[1] + mine.shape[1], full.shape[2]

    def load(self, copies, refs, target, sc, first=0):
        full, mine, theirs = refs
        by_slot = [[copies.start(full.at[z], target.at[z, whole_image(sc), :])] for z in range(NZ)]
        for z in range(NZ):
            source = (theirs if z % 2 else mine).at[z // 2]
            by_slot[z].append(copies.start(source, target.at[z, split_rows(sc), :]))
        return by_slot


def take(items, count):
    return items[:count], items[count:]


def store_parts(total, out_scratch, parts, copies, outs, sc, ordered, swapped):
    part = out_scratch.shape[1]
    started = []
    for j in range(parts):
        rows = pl.ds(pl.multiple_of((sc[1] ^ j) * part, 8) if ordered else j * part, part)
        if swapped:
            block = total.shape[1] // swapped
            for k in range(swapped):
                piece = total[rows, k * block : (k + 1) * block]
                out_scratch[j, :, (k ^ 1) * block : ((k ^ 1) + 1) * block] = piece.astype(BF16)
        else:
            out_scratch[j] = total[rows, :].astype(BF16)
        started.append(copies.start(out_scratch.at[j], outs[j]))
    return started


def gate(scalars, after, hold):
    def body(sc, ins, outs, scratch, copies):
        pass

    return manual(body, "gate", scalars, [], [], [], 1, after, hold)


def pack(scalars, pieces, after=(), hold=()):
    def body(sc, ins, outs, scratch, copies):
        arriving = [copies.start(ref, scratch[0].at[i]) for i, ref in enumerate(ins)]
        leaving = []
        for i, copy in enumerate(arriving):
            copy.wait()
            leaving.append(copies.start(scratch[0].at[i], outs[0].at[i]))
        wait(leaving)

    dims = (len(pieces),) + pieces[0].shape
    return manual(
        body, "pack", scalars, pieces, [shape(dims, BF16)], [vmem(dims)], 2 * len(pieces), after, hold
    )


def add(scalars, arrays, after=(), hold=()):
    out, *held = add_groups(scalars, [arrays], False, after, hold)
    return (out, *held)


def add_groups(scalars, groups, apart, after=(), hold=()):
    dims, terms = groups[0][0].shape, len(groups[0])
    three = len(dims) == 3
    count = dims[0] if three else 3 if dims[0] % 48 == 0 else 1
    rows = 0 if three else dims[0] // count
    place = (lambda ref, i: ref.at[i]) if three else (lambda ref, i: ref.at[pl.ds(i * rows, rows), :])
    at = (lambda i: i) if three else (lambda i: slice(i * rows, (i + 1) * rows))

    def body(sc, ins, outs, scratch, copies):
        arriving = []
        for g in range(len(groups)):
            for i in range(count):
                arriving.append([
                    copies.start(place(ins[g * terms + t], i), place(scratch[g * terms + t], i)) for t in range(terms)
                ])
        leaving = []
        for g in range(len(groups)):
            total_ref = scratch[len(groups) * terms + g]
            for i in range(count):
                wait(arriving[g * count + i])
                total = scratch[g * terms][at(i)].astype(F32)
                for t in range(1, terms):
                    total += scratch[g * terms + t][at(i)].astype(F32)
                total_ref[at(i)] = total.astype(BF16)
                goal = outs[g * count + i] if apart else place(outs[g], i)
                leaving.append(copies.start(place(total_ref, i), goal))
        wait(leaving)

    made = [shape(dims[1:], BF16)] * (count * len(groups)) if apart else [shape(dims, BF16)] * len(groups)
    return manual(
        body, "add", scalars, [a for g in groups for a in g], made, [vmem(dims)] * ((terms + 1) * len(groups)),
        (terms + 1) * count * len(groups), after, hold,
    )


def project(scalars, rows, weights, name, after=(), hold=()):
    count, cols = rows.count, weights.cols
    half = SEQ // 2

    def body(sc, ins, outs, scratch, copies):
        x, w, y = scratch
        row_refs, weight_refs = take(ins, len(rows.args))
        started = rows.load(copies, row_refs, x, sc)
        by_slot = weights.load(copies, weight_refs, w, sc)
        wait(started)
        step, leaving = slots_at_once(cols), []
        for z in range(0, NZ, step):
            for s in range(z, z + step):
                wait(by_slot[s])
            value = nn(x[...], weights.slots(w, z, step))
            for s in range(step):
                y[z + s] = value[:, s * cols : (s + 1) * cols].astype(BF16)
                leaving.append(copies.start(y.at[z + s], outs[0].at[z + s]))
                if (z + s) % 2:
                    leaving.append(copies.start(y.at[z + s, split_rows(sc), :], outs[1].at[(z + s) // 2]))
        wait(leaving)

    return manual(
        body, name, scalars, rows.args + weights.args,
        [shape((NZ, count, cols), BF16), shape((NZ // 2, half, cols), BF16)],
        [vmem((count, rows.width)), weights.scratch, vmem((NZ, count, cols))],
        rows.copies + weights.copies + NZ + NZ // 2, after, hold,
    )


def project_back(scalars, slots, weights, nodes, name, after=(), hold=()):
    count, cols, width = slots.count, weights.cols, weights.depth

    def body(sc, ins, outs, scratch, copies):
        y, w, total, parts = scratch
        slot_refs, weight_refs = take(ins, len(slots.args))
        for started in slots.load(copies, slot_refs, y, sc) + weights.load(copies, weight_refs, w, sc):
            wait(started)
        if weights.flat:
            total[...] = nt(jnp.concatenate([y[z] for z in range(NZ)], axis=1), w[...])
        else:
            value = nt(y[0], w[0])
            for z in range(1, NZ):
                value += nt(y[z], w[z])
            total[...] = value
        wait(store_parts(total, parts, nodes, copies, outs, sc, True, 0))

    return manual(
        body, name, scalars, slots.args + weights.args, [shape((count // nodes, width), BF16)] * nodes,
        [vmem((NZ, count, cols)), weights.scratch, vmem((count, width), F32), vmem((nodes, count // nodes, width))],
        slots.copies + weights.copies + nodes, after, hold,
    )


def weight_grads(scalars, products, dps, out_shape, goal, side, name, after=(), hold=()):
    counts = [sum(g.count for g in rows) for rows, _ in products]
    widths = [slots[0].cols for _, slots in products]
    width = products[0][0][0].width
    block = width // dps
    parts = 1 if side else len(products)
    cols = sum(widths) if side else widths[0]
    step = max(slots_at_once(c) for c in widths)
    args, scratch, copies_needed = [], [vmem((parts, NZ, width, cols))], parts * NZ * dps
    for (rows, slots), count, own in zip(products, counts, widths):
        args += [a for g in rows + slots for a in g.args]
        scratch += [vmem((count, width)), vmem((NZ, count, own)), vmem((width, count))]
        copies_needed += sum(g.copies for g in rows + slots)

    def body(sc, ins, outs, scratch, copies):
        result = scratch[0]
        loaded = []
        for i, (rows, slots) in enumerate(products):
            x, y, flipped = scratch[1 + 3 * i : 4 + 3 * i]
            started, at = [], 0
            for g in rows:
                refs, ins = take(ins, len(g.args))
                started += g.load(copies, refs, x, sc, at)
                at += g.count
            by_slot, at = [[] for _ in range(NZ)], 0
            for g in slots:
                refs, ins = take(ins, len(g.args))
                for z, some in enumerate(g.load(copies, refs, y, sc, at)):
                    by_slot[z] += some
                at += g.count
            loaded.append((started, by_slot))
        leaving = []

        def send(part, z):
            for k in range(dps):
                rows = pl.ds(k * block, block)
                leaving.append(copies.start(result.at[part, z, rows, :], goal(sc, outs, part, k, z)))

        def multiply(i, z, at, part):
            y, flipped, own = scratch[2 + 3 * i], scratch[3 + 3 * i], widths[i]
            for s in range(z, z + step):
                wait(loaded[i][1][s])
            whole_y = jnp.concatenate([y[z + s] for s in range(step)], axis=1) if step > 1 else y[z]
            value = nn(flipped[...], whole_y)
            for s in range(step):
                result[part, z + s, :, at : at + own] = value[:, s * own : (s + 1) * own].astype(BF16)

        def flip(i):
            wait(loaded[i][0])
            scratch[3 + 3 * i][...] = scratch[1 + 3 * i][...].T

        if side:
            for i in range(len(products)):
                flip(i)
            for z in range(0, NZ, step):
                for i in range(len(products)):
                    multiply(i, z, sum(widths[:i]), 0)
                for s in range(z, z + step):
                    send(0, s)
        else:
            for i in range(len(products)):
                flip(i)
                for z in range(0, NZ, step):
                    multiply(i, z, 0, i)
                    for s in range(z, z + step):
                        send(i, s)
        wait(leaving)

    return list(manual(body, name, scalars, args, out_shape, scratch, copies_needed, after, hold))


def feed_forward(scalars, rows, weights, bias_row, name, after=(), hold=()):
    count, cols = rows.count, weights.cols

    def body(sc, ins, outs, scratch, copies):
        x, w, b, hidden, slope = scratch
        row_refs, weight_refs = take(ins, len(rows.args))
        started = rows.load(copies, row_refs, x, sc)
        for z in range(NZ):
            started.append(copies.start(weight_refs[0].at[sc[3] ^ z, pl.ds(bias_row, BIAS_ROWS), :], b.at[z]))
        by_slot = weights.load(copies, weight_refs, w, sc)
        wait(started)
        leaving = []
        step = slots_at_once(cols)
        for z in range(0, NZ, step):
            for s in range(z, z + step):
                wait(by_slot[s])
            value = nn(x[...], weights.slots(w, z, step))
            for s in range(step):
                terms = b[z + s].astype(F32)
                u = value[:, s * cols : (s + 1) * cols] + (terms[0:1] + terms[1:2] + terms[2:3])
                cdf = 0.5 + 0.5 * lax.erf(u * math.sqrt(0.5))
                hidden[z + s] = (u * cdf).astype(BF16)
                slope[z + s] = (cdf + u * (jnp.exp(-0.5 * u * u) * (1.0 / math.sqrt(2.0 * math.pi)))).astype(BF16)
                leaving.append(copies.start(hidden.at[z + s], outs[0].at[z + s]))
                leaving.append(copies.start(slope.at[z + s], outs[1].at[z + s]))
        wait(leaving)

    return manual(
        body, name, scalars, rows.args + weights.args, [shape((NZ, count, cols), BF16)] * 2,
        [vmem((count, rows.width)), weights.scratch, vmem((NZ, BIAS_ROWS, cols)), vmem((NZ, count, cols)), vmem((NZ, count, cols))],
        rows.copies + NZ + weights.copies + 2 * NZ, after, hold,
    )


def feed_back(scalars, rows, slope, down, up, nodes, swapped, name, after=(), hold=()):
    count, cols, width = rows.count, down.cols, rows.width

    def body(sc, ins, outs, scratch, copies):
        x, wd, wu, steep, du, gb, total, parts = scratch
        row_refs, ins = take(ins, len(rows.args))
        slope_ref, ins = ins[0], ins[1:]
        down_refs, up_refs = take(ins, len(down.args))
        started = rows.load(copies, row_refs, x, sc)
        down_slots = down.load(copies, down_refs, wd, sc)
        steep_slots = [copies.start(slope_ref.at[z], steep.at[z]) for z in range(NZ)]
        up_slots = up.load(copies, up_refs, wu, sc)
        wait(started)
        leaving = []
        step = slots_at_once(cols)
        for z in range(0, NZ, step):
            for s in range(z, z + step):
                wait(down_slots[s])
                steep_slots[s].wait()
            value = nn(x[...], down.slots(wd, z, step))
            for s in range(step):
                grad = value[:, s * cols : (s + 1) * cols] * steep[z + s].astype(F32)
                gb[z + s : z + s + 1, :] = jnp.sum(grad, axis=0, keepdims=True)
                du[z + s] = grad.astype(BF16)
                leaving.append(copies.start(du.at[z + s], outs[0].at[z + s]))
        leaving.append(copies.start(gb, outs[1]))
        for z in range(NZ):
            wait(up_slots[z])
        total[...] = nt(jnp.concatenate([du[z] for z in range(NZ)], axis=1), wu[...])
        wait(leaving + store_parts(total, parts, nodes, copies, outs[2:], sc, False, swapped))

    out = manual(
        body, name, scalars, rows.args + [slope] + down.args + up.args,
        [shape((NZ, count, cols), BF16), shape((NZ, cols), F32)] + [shape((count // nodes, width), BF16)] * nodes,
        [vmem((count, width)), down.scratch, up.scratch, vmem((NZ, count, cols)), vmem((NZ, count, cols)),
         vmem((NZ, cols), F32), vmem((count, width), F32), vmem((nodes, count // nodes, width))],
        rows.copies + down.copies + up.copies + 2 * NZ + 1 + nodes, after, hold,
    )
    return out[0], out[1], list(out[2 : 2 + nodes]), out[2 + nodes :]


def feed_out(scalars, hidden, down, nodes, swapped, name, after=(), hold=()):
    _, count, cols = hidden.shape
    width = down.depth

    def body(sc, ins, outs, scratch, copies):
        y, w, total, parts = scratch
        started = [copies.start(ins[0].at[z], y.at[z]) for z in range(NZ)]
        by_slot = down.load(copies, ins[1:], w, sc)
        wait(started)
        for z in range(NZ):
            wait(by_slot[z])
        total[...] = nt(jnp.concatenate([y[z] for z in range(NZ)], axis=1), w[...])
        wait(store_parts(total, parts, nodes, copies, outs, sc, False, swapped))

    return manual(
        body, name, scalars, [hidden] + down.args, [shape((count // nodes, width), BF16)] * nodes,
        [vmem((NZ, count, cols)), down.scratch, vmem((count, width), F32), vmem((nodes, count // nodes, width))],
        NZ + down.copies + nodes, after, hold,
    )


def head_mask(cols, head):
    lane = lax.broadcasted_iota(jnp.int32, (1, cols), 1)
    return (lane >= head * HD) & (lane < (head + 1) * HD)


def attend(q, k, v):
    cols = q.shape[1]
    q = q * (1.0 / math.sqrt(HD))
    total = None
    for head in range(cols // HD):
        mask = head_mask(cols, head)
        scores = nt(jnp.where(mask, q, 0).astype(BF16), k)
        raised = jnp.exp(scores - jnp.max(scores, axis=1, keepdims=True))
        soft = raised * (1.0 / jnp.sum(raised, axis=1, keepdims=True))
        mixed = nn(soft.astype(BF16), jnp.where(mask, v, 0).astype(BF16))
        total = mixed if total is None else total + mixed
    return total.astype(BF16)


def attend_back(q, k, v, do):
    cols = q.shape[1]
    q = (q * (1.0 / math.sqrt(HD))).astype(BF16)
    dq = dk = dv = None
    for head in range(cols // HD):
        mask = head_mask(cols, head)
        qh = jnp.where(mask, q, 0).astype(BF16)
        doh = jnp.where(mask, do, 0).astype(BF16)
        kh = jnp.where(mask, k, 0).astype(BF16)
        scores = nt(k, qh)
        raised = jnp.exp(scores - jnp.max(scores, axis=0, keepdims=True))
        soft = raised * (1.0 / jnp.sum(raised, axis=0, keepdims=True))
        dsoft = nt(v, doh)
        dot = jnp.sum(dsoft * soft, axis=0, keepdims=True)
        dscores = (soft * (dsoft - dot)).astype(BF16)
        dvh = nn(soft.astype(BF16), doh)
        dkh = nn(dscores, qh)
        dqh = tn(dscores, kh)
        dq = dqh if dq is None else dq + dqh
        dk = dkh if dk is None else dk + dkh
        dv = dvh if dv is None else dv + dvh
    return (dq * (1.0 / math.sqrt(HD))).astype(BF16), dk.astype(BF16), dv.astype(BF16)


def whole_image(sc):
    return pl.ds(pl.multiple_of(sc[2] * (SEQ // 2), 32), SEQ)


def split_rows(sc):
    return pl.ds(pl.multiple_of((1 - sc[2]) * SEQ, 32), SEQ // 2)


def own_slot(dims):
    return pl.BlockSpec((1,) + dims, lambda s, *_: (2 * s, 0, 0))


def attend_whole(scalars, qkv, after=(), hold=()):
    slots, count, triple = qkv.shape
    cols = triple // 3

    def body(sc, qkv_ref, o_ref):
        rows = whole_image(sc)
        q, k, v = (qkv_ref[0, rows, j * cols : (j + 1) * cols] for j in range(3))
        o_ref[0] = attend(q, k, v)

    return call(
        body, "attend_whole", (slots,), scalars, [slot((count, triple))], slot((SEQ, cols)),
        shape((slots, SEQ, cols), BF16), [qkv],
        after=after, hold=hold, nbytes=2 * slots * count * 4 * cols,
    )


def attend_split(scalars, qkv, partner, after=(), hold=()):
    slots, half, triple = partner.shape
    count = qkv.shape[1]
    cols = triple // 3

    def body(sc, qkv_ref, partner_ref, mine_ref, theirs_ref, joined):
        joined[:half, :] = qkv_ref[0, split_rows(sc), :]
        joined[half:, :] = partner_ref[0]
        q, k, v = (joined[:, j * cols : (j + 1) * cols] for j in range(3))
        mixed = attend(q, k, v)
        mine_ref[0] = mixed[:half]
        theirs_ref[0] = mixed[half:]

    return call(
        body, "attend_split", (slots,), scalars, [own_slot((count, triple)), slot((half, triple))],
        [slot((half, cols))] * 2, [shape((slots, half, cols), BF16)] * 2, [qkv, partner],
        scratch=[pltpu.VMEM((2 * half, triple), BF16)],
        after=after, hold=hold, nbytes=2 * slots * count * 4 * cols,
    )


def attend_whole_back(scalars, qkv, do, after=(), hold=()):
    slots, count, triple = qkv.shape
    cols = triple // 3

    def body(sc, qkv_ref, do_ref, out_ref):
        rows = whole_image(sc)
        q, k, v = (qkv_ref[0, rows, j * cols : (j + 1) * cols] for j in range(3))
        grads = attend_back(q, k, v, do_ref[0, rows, :])
        for j in range(3):
            out_ref[0, :, j * cols : (j + 1) * cols] = grads[j]

    return call(
        body, "attend_whole_back", (slots,), scalars, [slot((count, triple)), slot((count, cols))],
        slot((SEQ, triple)), shape((slots, SEQ, triple), BF16), [qkv, do],
        after=after, hold=hold, nbytes=2 * slots * count * 7 * cols,
    )


def attend_split_back(scalars, qkv, partner, do, do_partner, after=(), hold=()):
    slots, half, triple = partner.shape
    count = qkv.shape[1]
    cols = triple // 3

    def body(sc, qkv_ref, partner_ref, do_ref, do_partner_ref, mine_ref, theirs_ref, joined, joined_do):
        joined[:half, :] = qkv_ref[0, split_rows(sc), :]
        joined[half:, :] = partner_ref[0]
        joined_do[:half, :] = do_ref[0, split_rows(sc), :]
        joined_do[half:, :] = do_partner_ref[0]
        q, k, v = (joined[:, j * cols : (j + 1) * cols] for j in range(3))
        grads = attend_back(q, k, v, joined_do[...])
        for j in range(3):
            mine_ref[0, :, j * cols : (j + 1) * cols] = grads[j][:half]
            theirs_ref[0, :, j * cols : (j + 1) * cols] = grads[j][half:]

    return call(
        body, "attend_split_back", (slots,), scalars,
        [own_slot((count, triple)), slot((half, triple)), own_slot((count, cols)), slot((half, cols))],
        [slot((half, triple))] * 2, [shape((slots, half, triple), BF16)] * 2, [qkv, partner, do, do_partner],
        scratch=[pltpu.VMEM((2 * half, triple), BF16), pltpu.VMEM((2 * half, cols), BF16)],
        after=after, hold=hold, nbytes=2 * slots * count * 7 * cols,
    )


def row_tile(count):
    return count // 3 if (count // 3) % 16 == 0 else count


def tiles(rows, width):
    return pl.BlockSpec((rows, width), lambda i, *_: (i, 0))


def to_relative(sc, scratch, out_ref, block):
    dps = scratch.shape[1] // block
    for k in range(dps):
        out_ref[:, k * block : (k + 1) * block] = scratch[
            :, pl.ds(pl.multiple_of((sc[0] ^ k) * block, block), block)
        ].astype(out_ref.dtype)


def from_relative(sc, refs, scratch, block):
    dps = scratch.shape[1] // block
    for k in range(dps):
        here = slice(k * block, (k + 1) * block)
        piece = refs[0][:, here].astype(F32)
        for ref in refs[1:]:
            piece += ref[:, here].astype(F32)
        scratch[:, pl.ds(pl.multiple_of((sc[0] ^ k) * block, block), block)] = piece


def normed(rows):
    centred = rows - jnp.mean(rows, axis=-1, keepdims=True)
    inverse = lax.rsqrt(jnp.mean(centred * centred, axis=-1, keepdims=True) + 1e-06)
    return centred * inverse, inverse


def norm_back(hat, inverse, grad, gain):
    scaled = grad * gain
    return inverse * (
        scaled - jnp.mean(scaled, axis=-1, keepdims=True) - hat * jnp.mean(scaled * hat, axis=-1, keepdims=True)
    )


def first_norm(scalars, tokens, cotangent, vectors, dps, after=(), hold=()):
    count, width = tokens.shape
    rows, block = row_tile(count), width // dps

    def body(sc, x_ref, cot_ref, vec_ref, a_ref, g_ref, scratch):
        hat, _ = normed(x_ref[...])
        scratch[...] = hat * vec_ref[0:1] + vec_ref[1:2]
        to_relative(sc, scratch, a_ref, block)
        to_relative(sc, cot_ref, g_ref, block)

    return call(
        body, "first_norm", (count // rows,), scalars,
        [tiles(rows, width)] * 2 + [whole(vectors.shape)], [tiles(rows, width)] * 2,
        [shape((count, width), BF16)] * 2, [tokens, cotangent, vectors],
        scratch=[pltpu.VMEM((rows, width), F32)], after=after, hold=hold, nbytes=12 * count * width,
    )


def second_norm(scalars, tokens, parts, vectors, dps, after=(), hold=()):
    count, width = tokens.shape
    rows, block = row_tile(count), width // dps

    def body(sc, x_ref, vec_ref, *refs):
        h_ref, c_ref, scratch = refs[-3:]
        from_relative(sc, refs[:-3], scratch, block)
        h = x_ref[...] + scratch[...] + vec_ref[4:5]
        h_ref[...] = h
        hat, _ = normed(h)
        scratch[...] = hat * vec_ref[2:3] + vec_ref[3:4]
        to_relative(sc, scratch, c_ref, block)

    return call(
        body, "second_norm", (count // rows,), scalars,
        [tiles(rows, width), whole(vectors.shape)] + [tiles(rows, width)] * len(parts), [tiles(rows, width)] * 2,
        [shape((count, width), F32), shape((count, width), BF16)], [tokens, vectors] + list(parts),
        scratch=[pltpu.VMEM((rows, width), F32)], after=after, hold=hold, nbytes=14 * count * width,
    )


def layer_output(scalars, middle, parts, vectors, dps, after=(), hold=()):
    count, width = middle.shape
    rows, block = row_tile(count), width // dps

    def body(sc, h_ref, vec_ref, *refs):
        out_ref, scratch = refs[-2:]
        from_relative(sc, refs[:-2], scratch, block)
        out_ref[...] = h_ref[...] + scratch[...] + vec_ref[5:6]

    return call(
        body, "layer_output", (count // rows,), scalars,
        [tiles(rows, width), whole(vectors.shape)] + [tiles(rows, width)] * len(parts), tiles(rows, width),
        shape((count, width), F32), [middle, vectors] + list(parts),
        scratch=[pltpu.VMEM((rows, width), F32)], after=after, hold=hold, nbytes=12 * count * width,
    )


def add_rows(ref, values):
    step = pl.program_id(0)

    @pl.when(step == 0)
    def _():
        ref[...] = values

    @pl.when(step > 0)
    def _():
        ref[...] += values


def second_norm_back(scalars, middle, cotangent, parts, vectors, dps, after=(), hold=()):
    count, width = middle.shape
    rows, block = row_tile(count), width // dps

    def body(sc, h_ref, cot_ref, vec_ref, *refs):
        dh_ref, e_ref, sums_ref, scratch = refs[-4:]
        from_relative(sc, refs[:-4], scratch, block)
        dc = scratch[...]
        hat, inverse = normed(h_ref[...])
        cot = cot_ref[...]
        dh = cot + norm_back(hat, inverse, dc, vec_ref[2:3])
        dh_ref[...] = dh
        scratch[...] = dh
        to_relative(sc, scratch, e_ref, block)
        column = lambda values: jnp.sum(values, axis=0, keepdims=True)
        add_rows(sums_ref, jnp.concatenate([column(dc * hat), column(dc), column(dh), column(cot)], axis=0))

    return call(
        body, "second_norm_back", (count // rows,), scalars,
        [tiles(rows, width)] * 2 + [whole(vectors.shape)] + [tiles(rows, width)] * len(parts),
        [tiles(rows, width)] * 2 + [whole((4, width))],
        [shape((count, width), F32), shape((count, width), BF16), shape((4, width), F32)],
        [middle, cotangent, vectors] + list(parts),
        scratch=[pltpu.VMEM((rows, width), F32)], after=after, hold=hold, nbytes=18 * count * width,
    )


def first_norm_back(scalars, tokens, middle_grad, parts, vectors, dps, after=(), hold=()):
    count, width = tokens.shape
    rows, block = row_tile(count), width // dps

    def body(sc, x_ref, dh_ref, vec_ref, *refs):
        dx_ref, sums_ref, scratch = refs[-3:]
        from_relative(sc, refs[:-3], scratch, block)
        da = scratch[...]
        hat, inverse = normed(x_ref[...])
        dx_ref[...] = dh_ref[...] + norm_back(hat, inverse, da, vec_ref[0:1])
        column = lambda values: jnp.sum(values, axis=0, keepdims=True)
        add_rows(sums_ref, jnp.concatenate([column(da * hat), column(da)], axis=0))

    return call(
        body, "first_norm_back", (count // rows,), scalars,
        [tiles(rows, width)] * 2 + [whole(vectors.shape)] + [tiles(rows, width)] * len(parts),
        [tiles(rows, width), whole((2, width))],
        [shape((count, width), F32), shape((2, width), F32)], [tokens, middle_grad, vectors] + list(parts),
        scratch=[pltpu.VMEM((rows, width), F32)], after=after, hold=hold, nbytes=16 * count * width,
    )


def adam_step(weight, gradient, first, second, rate, decay):
    first = 0.9 * first + 0.1 * gradient
    second = 0.999 * second + 0.001 * gradient * gradient
    first_fix = 1.0 - 0.9**STEP
    second_fix = 1.0 - 0.999**STEP
    update = first / first_fix / (jnp.sqrt(second / second_fix) + 1e-08) + decay * weight
    return (gradient, first, second, weight - rate * update)


def by_part(columns, heads):
    return jnp.concatenate([columns[:, (h * 3 + c) * HD : (h * 3 + c + 1) * HD] for c in range(3) for h in range(heads)], axis=1)


def by_head(columns, heads):
    return jnp.concatenate([columns[:, (c * heads + h) * HD : (c * heads + h + 1) * HD] for h in range(heads) for c in range(3)], axis=1)


def plain(body, name, args, out_shape, after=(), hold=()):
    given, extra = len(args), len(after) + len(hold)
    made = len(out_shape)
    nbytes = sum(math.prod(a.shape) * a.dtype.itemsize for a in list(args) + list(out_shape))

    def run(*refs):
        body(*refs[:given], *refs[given + extra : given + extra + made])

    anywhere = pl.BlockSpec(memory_space=pltpu.HBM)
    here = pl.BlockSpec(memory_space=pltpu.VMEM)
    first = given + len(after)
    return pl.pallas_call(
        run, name=name,
        out_shape=list(out_shape) + [shape(h.shape, h.dtype) for h in hold],
        in_specs=[pl.BlockSpec(memory_space=pltpu.SMEM)] + [here] * (given - 1) + [anywhere] * extra,
        out_specs=[here] * made + [anywhere] * len(hold),
        input_output_aliases={first + i: made + i for i in range(len(hold))},
        compiler_params=pltpu.CompilerParams(vmem_limit_bytes=VMEM_LIMIT), cost_estimate=cost(name, nbytes),
    )(*args, *after, *hold)


def attn_piece(scalars, w_qkv, w_out):
    heads = w_qkv.shape[1] // (3 * HD)
    triple = w_qkv.shape[1]

    def body(sc, qkv_ref, out_ref, piece_ref):
        piece_ref[:, :triple] = by_part(qkv_ref[...], heads).astype(BF16)
        piece_ref[:, triple:] = out_ref[...].T.astype(BF16)

    return plain(body, "attn_piece", [scalars, w_qkv, w_out], [shape((w_qkv.shape[0], triple + w_out.shape[0]), BF16)])[0]


def hidden_pieces(scalars, w_up, hidden_bias, w_down, after=()):
    block, cols = w_up.shape[0], w_up.shape[1] // 2

    def body(sc, up_ref, bias_ref, down_ref, my_up_ref, my_down_ref, theirs_ref):
        mine, other = (pl.ds(pl.multiple_of(h * cols, cols), cols) for h in (sc[4], 1 - sc[4]))
        my_up_ref[:block, :] = up_ref[:, mine].astype(BF16)
        my_down_ref[...] = down_ref[mine, :].T.astype(BF16)
        theirs_ref[:block, :] = up_ref[:, other].astype(BF16)
        theirs_ref[block:, :] = down_ref[other, :].T.astype(BF16)
        rest = bias_ref[:, mine]
        row = lax.broadcasted_iota(jnp.int32, (BIAS_ROWS, cols), 0)
        terms = jnp.zeros((BIAS_ROWS, cols), F32)
        for i in range(3):
            term = rest.astype(BF16).astype(F32)
            terms = jnp.where(row == i, term, terms)
            rest = rest - term
        my_up_ref[block:, :] = terms.astype(BF16)

    return plain(
        body, "hidden_pieces", [scalars, w_up, hidden_bias[None, :], w_down],
        [shape((block + BIAS_ROWS, cols), BF16), shape((block, cols), BF16), shape((2 * block, cols), BF16)], after,
    )


def attn_adam(scalars, sums, w_qkv, qkv_m, qkv_v, w_out, out_m, out_v, after=()):
    heads, triple = w_qkv.shape[1] // (3 * HD), w_qkv.shape[1]
    count = len(sums)

    def body(sc, *refs):
        total = None
        for ref in refs[:count]:
            piece = (ref[0] if len(ref.shape) == 3 else ref[...]).astype(F32)
            total = piece if total is None else total + piece
        qw, qm, qv, ow, om, ov = (r[...] for r in refs[count : count + 6])
        outs = refs[count + 6 :]
        new = adam_step(qw, by_head(total[:, :triple], heads), qm, qv, 0.1, 0.05)
        new += adam_step(ow, total[:, triple:].T, om, ov, 0.2, 0.05)
        for ref, value in zip(outs, new):
            ref[...] = value

    out = plain(
        body, "attn_adam", [scalars] + list(sums) + [w_qkv, qkv_m, qkv_v, w_out, out_m, out_v],
        [shape(w_qkv.shape, F32)] * 4 + [shape(w_out.shape, F32)] * 4, after,
    )
    return tuple(out[:4]), tuple(out[4:])


def hidden_adam(scalars, up_total, down_total, far, up, down, after=(), hold=()):
    block, cols = far.shape[0] // 2, far.shape[1]

    def body(sc, up_total_ref, down_total_ref, far_ref, *refs):
        ins, outs = take(refs, 6)
        up_grad, down_grad = outs[0], outs[4]
        mine, other = (pl.ds(pl.multiple_of(h * cols, cols), cols) for h in (sc[4], 1 - sc[4]))
        up_grad[:, mine] = up_total_ref[:block, :].astype(F32)
        up_grad[:, other] = far_ref[:block, :].astype(F32)
        down_grad[mine, :] = down_total_ref[:block, :].astype(F32).T
        down_grad[other, :] = far_ref[block:, :].astype(F32).T
        for (w, m, v), made, rate in ((ins[:3], outs[:4], 0.1), (ins[3:], outs[4:], 0.05)):
            new = adam_step(w[...], made[0][...], m[...], v[...], rate, 0.05)
            for ref, value in zip(made[1:], new[1:]):
                ref[...] = value

    out = plain(
        body, "hidden_adam", [scalars, up_total, down_total, far] + list(up) + list(down),
        [shape(up[0].shape, F32)] * 4 + [shape(down[0].shape, F32)] * 4, after, hold,
    )
    return tuple(out[:4]), tuple(out[4:8]), out[8:]


def solution(mesh):
    dps, tensor = mesh.shape["dp"], mesh.shape["tensor"]
    nodes = tensor // NZ
    devices = dps * tensor
    z_groups = [
        [d * tensor + z * nodes + c for z in range(NZ)] for d in range(dps) for c in range(nodes)
    ]

    def swap(value, flip):
        return lax.ppermute(value, AXES, [(i, i ^ flip) for i in range(devices)])

    def gather_z(piece):
        return lax.all_gather(piece, AXES, axis=0, axis_index_groups=z_groups)

    def scatter_z(total):
        return lax.psum_scatter(total, AXES, scatter_dimension=0, axis_index_groups=z_groups, tiled=True)[0]

    def by_weight(k):
        return (bin(k).count("1"), k)

    def gather(own, count, unit, low_first):
        bufs = [own] + [None] * (count - 1)
        for k in sorted(range(1, count), key=by_weight):
            last = k & -k if low_first else 1 << (k.bit_length() - 1)
            bufs[k] = swap(bufs[k ^ last], last * unit)
        return bufs

    def plus(left, right):
        return (left.astype(F32) + right.astype(F32)).astype(BF16)

    def scatter(bufs, unit, low_first):
        bufs, sums = list(bufs), [bufs[0]]
        for k in sorted(range(1, len(bufs)), key=by_weight, reverse=True):
            last = k & -k if low_first else 1 << (k.bit_length() - 1)
            arrived = swap(bufs[k], last * unit)
            if k == last:
                sums.append(arrived)
            else:
                bufs[k ^ last] = plus(bufs[k ^ last], arrived)
        return sums

    def add_up(sums):
        total = sums[0].astype(F32)
        for piece in sums[1:]:
            total = total + piece.astype(F32)
        return total.astype(BF16)

    def along_z(piece):
        return [piece] + [swap(piece, j * nodes) for j in range(1, NZ)]

    def relative(own):
        return [own] + [swap(own, j) for j in range(1, nodes)]

    def ordered_rows(parts, member):
        if parts[0].shape[0] % 16 == 0:
            return Rows(parts, True)
        flip = 1
        while len(parts) > 1:
            odd = (member // flip) % 2 == 1
            parts = [
                jnp.where(odd, jnp.concatenate([b, a], axis=0), jnp.concatenate([a, b], axis=0))
                for a, b in zip(parts[0::2], parts[1::2])
            ]
            flip *= 2
        return Rows(parts, True)

    def relative_rows(parts, swapped=0):
        if parts[0].shape[0] % 16:
            parts = [jnp.concatenate(parts, axis=0)]
        return Rows(parts, False, swapped)

    def send_parts(parts):
        return [parts[0]] + [swap(parts[j], j) for j in range(1, nodes)]

    def per_device(
        tokens, cotangent, vectors, vectors_m, vectors_v,
        w_qkv, qkv_m, qkv_v, w_out, out_m, out_v, w_up, up_m, up_v,
        hidden_bias, bias_m, bias_v, w_down, down_m, down_v,
    ):
        dp_index = lax.axis_index("dp")
        tensor_index = lax.axis_index("tensor")
        z_index, member = tensor_index // nodes, tensor_index % nodes
        odd_x = dp_index % 2
        scalars = jnp.stack([dp_index, member, z_index % 2, z_index, odd_x]).astype(jnp.int32)
        block = w_qkv.shape[0]
        triple, width = w_qkv.shape[1], w_out.shape[0]
        hidden_here = w_up.shape[1] // 2

        attn_z = along_z(attn_piece(scalars, w_qkv, w_out))
        my_up, my_down, theirs = hidden_pieces(scalars, w_up, hidden_bias, w_down, after=[attn_z[0]])
        arrived = swap(theirs, tensor)
        (lower,) = pack(scalars, attn_z[:2], after=[my_up])
        lowers = gather(lower, dps, tensor, False)
        up_piece = jnp.concatenate([my_up, arrived[:block]], axis=0)
        down_piece = jnp.concatenate([my_down, arrived[block:]], axis=0)
        down_piece = jnp.concatenate(gather(down_piece, dps // 2, 2 * tensor, False), axis=0)
        upper, up_piece, down_piece = pack(scalars, attn_z[2:], after=[lower], hold=[up_piece, down_piece])
        uppers = gather(upper, dps, tensor, True)
        a_own, g_own = first_norm(scalars, tokens, cotangent, vectors, dps, after=[upper] + lowers[1:3])
        a_parts = relative(a_own)
        up_z = gather_z(up_piece)
        halves = [(0, [(2 * k + z // 2, z % 2) for z in range(NZ)]) for k in range(dps)]
        attn_w = [half for pair in zip(lowers, uppers) for half in pair]
        qkv_w = Weights(attn_w, halves, block, 0, triple)
        out_w = Weights(attn_w, halves, block, triple, width)

        a_rows = ordered_rows(a_parts, member)
        qkv, qkv_theirs, g_own, up_z = project(scalars, a_rows, qkv_w, "qkv", hold=[g_own, up_z])
        qkv_partner = swap(qkv_theirs, nodes)
        g_far = swap(g_own, tensor)
        mixed = attend_whole(scalars, qkv)

        up_rows = [(0, block + BIAS_ROWS)[k % 2] for k in range(dps)]
        up_w = Weights(
            gather(up_z, dps // 2, 2 * tensor, False), [(row, [(k // 2, None)] * NZ) for k, row in enumerate(up_rows)],
            block, 0, hidden_here,
        )
        mixed_mine, mixed_theirs, down_piece = attend_split(scalars, qkv, qkv_partner, after=[mixed], hold=[down_piece])
        mixed = SplitSlots(mixed, mixed_mine, swap(mixed_theirs, nodes))
        *attn_parts, g_far = project_back(
            scalars, mixed, out_w, nodes, "attn_out", after=up_w.args[1:], hold=[g_far]
        )
        middle, c_own = second_norm(scalars, tokens, send_parts(attn_parts), vectors, dps)
        down_w = Weights(
            [gather_z(down_piece)], [(k * block, [(0, None)] * NZ) for k in range(dps)], block, 0, hidden_here
        )

        c_far = swap(c_own, tensor)
        g_rows, g_far = relative_rows(relative(g_own)), relative_rows(relative(g_far), dps)
        c_rows = relative_rows(relative(c_own))
        hidden, slope = feed_forward(scalars, c_rows, up_w, block, "feed_forward")
        (c_far,) = gate(scalars, [hidden], [c_far])
        c_far = relative_rows(relative(c_far), dps)
        hidden_far, slope_far = feed_forward(scalars, c_far, up_w, block, "feed_forward_far", after=[hidden])
        du, bias_near, dc_near, _ = feed_back(
            scalars, g_rows, slope, down_w, up_w, nodes, 0, "feed_back", after=[hidden_far]
        )
        dc_near = send_parts(dc_near)
        du_far, bias_far, dc_far, _ = feed_back(
            scalars, g_far, slope_far, down_w, up_w, nodes, dps, "feed_back_far", after=[du]
        )
        (dc_sum,) = add(scalars, send_parts(dc_far), after=[du_far])
        dc_arrived = swap(dc_sum, tensor)

        def hidden_goal(sc, outs, part, k, z):
            if part == 0:
                return outs[0].at[sc[3] ^ z, pl.ds(k * block, block), :]
            return outs[1 + k // 2].at[sc[3] ^ z, pl.ds((k % 2) * block, block), :]

        down_part, *up_part = weight_grads(
            scalars,
            [([g_rows, g_far], [Slots(hidden), Slots(hidden_far)]), ([c_rows, c_far], [Slots(du), Slots(du_far)])],
            dps, [shape((NZ, rows * block, hidden_here), BF16) for rows in [dps] + [2] * (dps // 2)],
            hidden_goal, False, "hidden_grad", after=[dc_sum] + dc_near[1:],
        )
        down_part = scatter_z(down_part)
        out_far = feed_out(scalars, hidden_far, down_w, nodes, dps, "feed_out_far", after=[up_part[0]])
        middle_grad, e_own, sums_two = second_norm_back(
            scalars, middle, cotangent, dc_near + [dc_arrived], vectors, dps, after=[out_far[0]]
        )
        out_far = send_parts(out_far)

        e_rows = ordered_rows(relative(e_own), member)
        dmixed, dmixed_theirs, out_far[0] = project(
            scalars, e_rows, out_w, "mixed_grad", after=out_far[1:], hold=[out_far[0]]
        )
        dmixed_partner = swap(dmixed_theirs, nodes)
        out_arrived = swap(add_up(out_far), tensor)
        out_near = feed_out(scalars, hidden, down_w, nodes, 0, "feed_out", after=[dmixed])
        dqkv_mine, dqkv_theirs = attend_split_back(
            scalars, qkv, qkv_partner, dmixed, dmixed_partner, after=[out_near[0]]
        )
        dqkv, down_part = attend_whole_back(scalars, qkv, dmixed, after=[dqkv_mine], hold=[down_part])
        down_part = scatter([down_part[2 * j * block : 2 * (j + 1) * block] for j in range(dps // 2)], 2 * tensor, False)
        dqkv = SplitSlots(dqkv, dqkv_mine, swap(dqkv_theirs, nodes))

        def attn_goal(sc, outs, part, k, z):
            return outs[2 * k + z // 2].at[z % 2]

        da_parts = send_parts(project_back(scalars, dqkv, qkv_w, nodes, "first_back", after=[out_arrived]))
        *attn_part, up_part[0], down_part[0] = weight_grads(
            scalars, [([a_rows], [dqkv]), ([e_rows], [mixed])],
            dps, [shape((NZ // 2, block, triple + width), BF16)] * (2 * dps), attn_goal, True, "attn_grad",
            after=[da_parts[0]] + down_part[1:], hold=[up_part[0], down_part[0]],
        )
        down_part = add_up(down_part)
        lowers, uppers = attn_part[0::2], attn_part[1::2]
        up_part = scatter_z(add_up(scatter(up_part, 2 * tensor, False)))
        input_grad, sums_one = first_norm_back(
            scalars, tokens, middle_grad, da_parts, vectors, dps, after=[attn_part[0]]
        )

        here = (jnp.arange(nodes)[:, None] == member) & (jnp.arange(2)[None, :] == odd_x)
        own_slot_of = (jnp.arange(NZ)[:, None] ^ z_index) == jnp.arange(NZ)[None, :]
        bias_here = jnp.sum(jnp.where(own_slot_of[:, :, None], (bias_near + bias_far)[None], 0.0), axis=1)
        bias_part = jnp.where(here[None, :, :, None], bias_here[:, None, None, :], 0.0)
        rows_two = sums_one.shape[0] + sums_two.shape[0]
        value = jnp.concatenate([sums_one, sums_two, bias_part.reshape(-1, sums_two.shape[1])], axis=0)
        bits = [1 << i for i in range(devices.bit_length() - 1)]
        stages = [bits[:1]] + [bits[i : i + 2] for i in range(1, len(bits), 2)] if len(bits) % 2 else [
            bits[i : i + 2] for i in range(0, len(bits), 2)
        ]

        def exchange(value, stage):
            flips = stage + [sum(stage)] if len(stage) > 1 else stage
            return [swap(value, flip) for flip in flips]

        def combine(value, arrived):
            near = value + arrived[0]
            return near + (arrived[1] + arrived[2]) if len(arrived) > 1 else near

        arrived = exchange(value, stages[0])

        if dps == 4:
            far_upper, far_lower = swap(uppers[3], tensor), swap(lowers[3], 2 * tensor)
            upper_x, lower_y = swap(uppers[1], tensor), swap(lowers[2], 2 * tensor)
            upper, lower, value = add_groups(
                scalars, [[uppers[2], far_upper], [lowers[1], far_lower]], False, after=[input_grad], hold=[value]
            )
            uppers = [uppers[0], upper_x, swap(upper, 2 * tensor)]
            lowers = [lowers[0], swap(lower, tensor), lower_y]
        else:
            uppers, lowers = scatter(uppers, tensor, True), scatter(lowers, tensor, False)
        value = combine(value, arrived)
        arrived = exchange(value, stages[1])
        output = layer_output(
            scalars, middle, send_parts(out_near) + [out_arrived], vectors, dps, after=[input_grad, uppers[0], value]
        )
        value = combine(value, arrived)
        own, *pieces, value = add_groups(scalars, [lowers, uppers], True, after=[output], hold=[value])
        sums = [own] + [swap(piece, (j + 1) * nodes) for j, piece in enumerate(pieces)]
        for stage in stages[2:]:
            value = combine(value, exchange(value, stage))
        all_sums = value
        far = swap(jnp.concatenate([up_part[block:], down_part[block:]], axis=0), tensor)
        up_res, down_res, _ = hidden_adam(
            scalars, up_part, down_part, far, (w_up, up_m, up_v), (w_down, down_m, down_v), after=[own]
        )
        qkv_res, out_res = attn_adam(scalars, sums, w_qkv, qkv_m, qkv_v, w_out, out_m, out_v, after=[up_res[0]])
        vector_total = all_sums[:rows_two]
        bias_total = lax.dynamic_slice_in_dim(
            all_sums[rows_two:].reshape(-1), tensor_index * 2 * hidden_here, 2 * hidden_here, 0
        )

        vec_res = adam_step(vectors, vector_total, vectors_m, vectors_v, 0.3, 0.0)
        bias_res = adam_step(hidden_bias, bias_total, bias_m, bias_v, 0.3, 0.0)
        return (output, input_grad) + vec_res + qkv_res + out_res + up_res + bias_res + down_res

    rows, both = P(AXES, None), P("dp", "tensor")
    turned = P("tensor", "dp")
    in_specs = (
        (rows,) * 2 + (P(),) * 3 + (both,) * 3 + (turned,) * 3 + (both,) * 3 + (P("tensor"),) * 3 + (turned,) * 3
    )
    out_specs = (
        (rows,) * 2 + (P(),) * 4 + (both,) * 4 + (turned,) * 4 + (both,) * 4 + (P("tensor"),) * 4 + (turned,) * 4
    )
    return jax.shard_map(per_device, mesh=mesh, in_specs=in_specs, out_specs=out_specs, check_vma=False)
```

```python
import math

import jax
import jax.numpy as jnp
from jax import lax
from jax.experimental import pallas as pl
from jax.experimental.pallas import tpu as pltpu
from jax.sharding import PartitionSpec as P

HD = 64
SEQ = 576
STEP = 10
NZ = 4
BIAS_ROWS = 16
AXES = ("dp", "tensor")
F32 = jnp.float32
BF16 = jnp.bfloat16
VMEM_LIMIT = 63 * 1024 * 1024
TIMES = {
    "gate_lower": 1, "gate_gather": 1000, "attn_out": 1000, "second_norm_back": 1000, "feed_out": 1000, "first_back": 1000,
}


def nn(left, right):
    return jnp.dot(left, right, preferred_element_type=F32)


def nt(left, right):
    return lax.dot_general(left, right, (((1,), (1,)), ((), ())), preferred_element_type=F32)


def tn(left, right):
    return lax.dot_general(left, right, (((0,), (0,)), ((), ())), preferred_element_type=F32)


def cost(name, nbytes):
    return pl.CostEstimate(flops=int(5e8 * TIMES.get(name, 0)), bytes_accessed=int(nbytes), transcendentals=0)


def call(body, name, grid, scalars, in_specs, out_specs, out_shape, args, scratch=(), after=(), hold=(), nbytes=0):
    given, extra = len(args), len(after) + len(hold)
    single = not isinstance(out_shape, (list, tuple))
    out_specs, out_shape = ([out_specs], [out_shape]) if single else (list(out_specs), list(out_shape))
    made = len(out_shape)

    def run(sc, *refs):
        rest = refs[given + extra :]
        body(sc, *refs[:given], *rest[:made], *rest[made + len(hold) :])

    anywhere = pl.BlockSpec(memory_space=pltpu.HBM)
    first = 1 + given + len(after)
    out = pl.pallas_call(
        run,
        name=name,
        grid_spec=pltpu.PrefetchScalarGridSpec(
            num_scalar_prefetch=1,
            grid=grid,
            in_specs=list(in_specs) + [anywhere] * extra,
            out_specs=out_specs + [anywhere] * len(hold),
            scratch_shapes=list(scratch),
        ),
        out_shape=out_shape + [shape(h.shape, h.dtype) for h in hold],
        input_output_aliases={first + i: made + i for i in range(len(hold))},
        compiler_params=pltpu.CompilerParams(vmem_limit_bytes=VMEM_LIMIT),
        cost_estimate=cost(name, nbytes),
    )(scalars, *args, *after, *hold)
    return out[0] if single and not hold else tuple(out)


def shape(dims, dtype):
    return jax.ShapeDtypeStruct(dims, dtype)


def whole(dims):
    return pl.BlockSpec(dims, lambda *_: (0,) * len(dims))


def slot(dims):
    return pl.BlockSpec((1,) + dims, lambda s, *_: (s, 0, 0))


def lower_slots(dims):
    return pl.BlockSpec((1,) + dims, lambda s, *_: (jnp.minimum(s, NZ // 2 - 1), 0, 0))


def upper_slots(dims):
    return pl.BlockSpec((1,) + dims, lambda s, *_: (jnp.maximum(s - NZ // 2, 0), 0, 0))


class Copies:
    def __init__(self, sems):
        self.sems, self.used = sems, 0

    def start(self, source, target):
        copy = pltpu.make_async_copy(source, target, self.sems.at[self.used])
        self.used += 1
        copy.start()
        return copy


def wait(copies):
    for copy in copies:
        copy.wait()


def manual(body, name, scalars, args, out_shape, scratch, copies, after=(), hold=()):
    given, extra = len(args), len(after) + len(hold)
    nbytes = sum(math.prod(a.shape) * a.dtype.itemsize for a in list(args) + list(out_shape))

    def run(sc, *refs):
        rest = refs[given + extra :]
        body(sc, refs[:given], rest[: len(out_shape)], rest[len(out_shape) + len(hold) : -1], Copies(rest[-1]))

    anywhere = pl.BlockSpec(memory_space=pltpu.HBM)
    first = 1 + given + len(after)
    return pl.pallas_call(
        run,
        name=name,
        in_specs=[pl.BlockSpec(memory_space=pltpu.SMEM)] + [anywhere] * (given + extra),
        out_specs=[anywhere] * (len(out_shape) + len(hold)),
        out_shape=list(out_shape) + [shape(h.shape, h.dtype) for h in hold],
        input_output_aliases={first + i: len(out_shape) + i for i in range(len(hold))},
        scratch_shapes=list(scratch) + [pltpu.SemaphoreType.DMA((copies,))],
        compiler_params=pltpu.CompilerParams(vmem_limit_bytes=VMEM_LIMIT),
        cost_estimate=cost(name, nbytes),
    )(scalars, *args, *after, *hold)


def vmem(dims, dtype=BF16):
    return pltpu.VMEM(dims, dtype)


class Weights:
    def __init__(self, arrays, blocks, block, col, cols):
        full = arrays[0].shape[2]
        if (col % 128 or cols % 128) and cols != full:
            arrays, col, full = [a[:, :, col : col + cols] for a in arrays], 0, cols
        self.args, self.blocks, self.block = list(arrays), blocks, block
        self.col, self.cols, self.full = col, cols, full
        self.depth = block * len(blocks)
        self.flat = cols % 128 == 0
        self.scratch = vmem((self.depth, NZ * cols) if self.flat else (NZ, self.depth, cols))
        self.copies = len(blocks) * NZ

    def load(self, copies, refs, target, sc):
        by_slot = [[] for _ in range(NZ)]
        for z in range(NZ):
            for k, (row, places) in enumerate(self.blocks):
                number, place = places[z]
                source = refs[number].at[place(sc) if callable(place) else place, pl.ds(row, self.block), :]
                if self.cols != self.full:
                    source = source.at[:, pl.ds(self.col, self.cols)]
                rows = pl.ds(k * self.block, self.block)
                goal = target.at[rows, pl.ds(z * self.cols, self.cols)] if self.flat else target.at[z, rows, :]
                by_slot[z].append(copies.start(source, goal))
        return by_slot

    def slots(self, target, first, count):
        if self.flat:
            return target[:, first * self.cols : (first + count) * self.cols]
        assert count == 1
        return target[first]


def slots_at_once(cols):
    for step in (1, 2, 4):
        if cols * step % 512 == 0 and cols % 128 == 0:
            return step
    return 1


class Rows:
    def __init__(self, parts, ordered, swapped=0):
        self.ordered, self.swapped = ordered, swapped
        self.part = parts[0].shape[0]
        self.args = list(parts)
        self.count = self.part * len(parts)
        self.width = parts[0].shape[1]
        self.copies = len(parts) * max(1, swapped)

    def load(self, copies, refs, target, sc, first=0):
        started = []
        for j, ref in enumerate(refs):
            at = first + j * self.part
            if self.ordered and len(refs) > 1:
                at = pl.multiple_of((sc[1] ^ j) * self.part, 16)
            rows = pl.ds(at, self.part)
            if not self.swapped:
                started.append(copies.start(ref, target.at[rows, :]))
                continue
            block = self.width // self.swapped
            for k in range(self.swapped):
                source = ref.at[:, pl.ds((k ^ 1) * block, block)]
                started.append(copies.start(source, target.at[rows, pl.ds(k * block, block)]))
        return started


class Slots:
    def __init__(self, array):
        self.args, self.copies = [array], NZ
        _, self.count, self.cols = array.shape

    def load(self, copies, refs, target, sc, first=0):
        return [[copies.start(refs[0].at[z], target.at[z, pl.ds(first, self.count), :])] for z in range(NZ)]


class SplitSlots:
    def __init__(self, full, mine, theirs):
        self.args, self.copies = [full, mine, theirs], 2 * NZ
        self.count, self.cols = full.shape[1] + mine.shape[1], full.shape[2]

    def load(self, copies, refs, target, sc, first=0):
        full, mine, theirs = refs
        by_slot = [[copies.start(full.at[z], target.at[z, whole_image(sc), :])] for z in range(NZ)]
        for z in range(NZ):
            source = (theirs if z % 2 else mine).at[z // 2]
            by_slot[z].append(copies.start(source, target.at[z, split_rows(sc), :]))
        return by_slot


def gray_rank(index, count):
    rank, shift = index, 1
    while 1 << shift < count:
        rank, shift = rank ^ (index >> shift), shift + 1
    return rank


def ring_place(column, z):
    return column * NZ + jnp.where(column % 2 == 0, z, NZ - 1 - z)


def hidden_place(sc, k, slot):
    return ring_place((sc[0] ^ k) >> 1, sc[3] ^ slot)


def take(items, count):
    return items[:count], items[count:]


def store_parts(total, out_scratch, parts, copies, outs, sc, ordered, swapped):
    part = out_scratch.shape[1]
    started = []
    for j in range(parts):
        rows = pl.ds(pl.multiple_of((sc[1] ^ j) * part, 8) if ordered else j * part, part)
        if swapped:
            block = total.shape[1] // swapped
            for k in range(swapped):
                piece = total[rows, k * block : (k + 1) * block]
                out_scratch[j, :, (k ^ 1) * block : ((k ^ 1) + 1) * block] = piece.astype(BF16)
        else:
            out_scratch[j] = total[rows, :].astype(BF16)
        started.append(copies.start(out_scratch.at[j], outs[j]))
    return started


def gate(scalars, name, after, hold):
    def body(sc, ins, outs, scratch, copies):
        pass

    return manual(body, name, scalars, [], [], [], 1, after, hold)


def pack(scalars, pieces, after=(), hold=()):
    def body(sc, ins, outs, scratch, copies):
        arriving = [copies.start(ref, scratch[0].at[i]) for i, ref in enumerate(ins)]
        leaving = []
        for i, copy in enumerate(arriving):
            copy.wait()
            leaving.append(copies.start(scratch[0].at[i], outs[0].at[i]))
        wait(leaving)

    dims = (len(pieces),) + pieces[0].shape
    return manual(
        body, "pack", scalars, pieces, [shape(dims, BF16)], [vmem(dims)], 2 * len(pieces), after, hold
    )


def add(scalars, arrays, after=(), hold=()):
    out, *held = add_groups(scalars, [arrays], False, after, hold)
    return (out, *held)


def add_groups(scalars, groups, apart, after=(), hold=()):
    dims, terms = groups[0][0].shape, len(groups[0])
    three = len(dims) == 3
    count = dims[0] if three else 3 if dims[0] % 48 == 0 else 1
    rows = 0 if three else dims[0] // count
    place = (lambda ref, i: ref.at[i]) if three else (lambda ref, i: ref.at[pl.ds(i * rows, rows), :])
    at = (lambda i: i) if three else (lambda i: slice(i * rows, (i + 1) * rows))

    def body(sc, ins, outs, scratch, copies):
        arriving = []
        for g in range(len(groups)):
            for i in range(count):
                arriving.append([
                    copies.start(place(ins[g * terms + t], i), place(scratch[g * terms + t], i)) for t in range(terms)
                ])
        leaving = []
        for g in range(len(groups)):
            total_ref = scratch[len(groups) * terms + g]
            for i in range(count):
                wait(arriving[g * count + i])
                total = scratch[g * terms][at(i)].astype(F32)
                for t in range(1, terms):
                    total += scratch[g * terms + t][at(i)].astype(F32)
                total_ref[at(i)] = total.astype(BF16)
                goal = outs[g * count + i] if apart else place(outs[g], i)
                leaving.append(copies.start(place(total_ref, i), goal))
        wait(leaving)

    made = [shape(dims[1:], BF16)] * (count * len(groups)) if apart else [shape(dims, BF16)] * len(groups)
    return manual(
        body, "add", scalars, [a for g in groups for a in g], made, [vmem(dims)] * ((terms + 1) * len(groups)),
        (terms + 1) * count * len(groups), after, hold,
    )


def project(scalars, rows, weights, name, after=(), hold=()):
    count, cols = rows.count, weights.cols
    half = SEQ // 2

    def body(sc, ins, outs, scratch, copies):
        x, w, y = scratch
        row_refs, weight_refs = take(ins, len(rows.args))
        started = rows.load(copies, row_refs, x, sc)
        by_slot = weights.load(copies, weight_refs, w, sc)
        wait(started)
        step, leaving = slots_at_once(cols), []
        for z in range(0, NZ, step):
            for s in range(z, z + step):
                wait(by_slot[s])
            value = nn(x[...], weights.slots(w, z, step))
            for s in range(step):
                y[z + s] = value[:, s * cols : (s + 1) * cols].astype(BF16)
                leaving.append(copies.start(y.at[z + s], outs[0].at[z + s]))
                if (z + s) % 2:
                    leaving.append(copies.start(y.at[z + s, split_rows(sc), :], outs[1].at[(z + s) // 2]))
        wait(leaving)

    return manual(
        body, name, scalars, rows.args + weights.args,
        [shape((NZ, count, cols), BF16), shape((NZ // 2, half, cols), BF16)],
        [vmem((count, rows.width)), weights.scratch, vmem((NZ, count, cols))],
        rows.copies + weights.copies + NZ + NZ // 2, after, hold,
    )


def project_back(scalars, slots, weights, nodes, name, after=(), hold=()):
    count, cols, width = slots.count, weights.cols, weights.depth

    def body(sc, ins, outs, scratch, copies):
        y, w, total, parts = scratch
        slot_refs, weight_refs = take(ins, len(slots.args))
        for started in slots.load(copies, slot_refs, y, sc) + weights.load(copies, weight_refs, w, sc):
            wait(started)
        if weights.flat:
            total[...] = nt(jnp.concatenate([y[z] for z in range(NZ)], axis=1), w[...])
        else:
            value = nt(y[0], w[0])
            for z in range(1, NZ):
                value += nt(y[z], w[z])
            total[...] = value
        wait(store_parts(total, parts, nodes, copies, outs, sc, True, 0))

    return manual(
        body, name, scalars, slots.args + weights.args, [shape((count // nodes, width), BF16)] * nodes,
        [vmem((NZ, count, cols)), weights.scratch, vmem((count, width), F32), vmem((nodes, count // nodes, width))],
        slots.copies + weights.copies + nodes, after, hold,
    )


def weight_grads(scalars, products, dps, out_shape, goal, side, name, after=(), hold=()):
    counts = [sum(g.count for g in rows) for rows, _ in products]
    widths = [slots[0].cols for _, slots in products]
    width = products[0][0][0].width
    block = width // dps
    parts = 1 if side else len(products)
    cols = sum(widths) if side else widths[0]
    step = max(slots_at_once(c) for c in widths)
    args, scratch, copies_needed = [], [vmem((parts, NZ, width, cols))], parts * NZ * dps
    for (rows, slots), count, own in zip(products, counts, widths):
        args += [a for g in rows + slots for a in g.args]
        scratch += [vmem((count, width)), vmem((NZ, count, own)), vmem((width, count))]
        copies_needed += sum(g.copies for g in rows + slots)

    def body(sc, ins, outs, scratch, copies):
        result = scratch[0]
        loaded = []
        for i, (rows, slots) in enumerate(products):
            x, y, flipped = scratch[1 + 3 * i : 4 + 3 * i]
            started, at = [], 0
            for g in rows:
                refs, ins = take(ins, len(g.args))
                started += g.load(copies, refs, x, sc, at)
                at += g.count
            by_slot, at = [[] for _ in range(NZ)], 0
            for g in slots:
                refs, ins = take(ins, len(g.args))
                for z, some in enumerate(g.load(copies, refs, y, sc, at)):
                    by_slot[z] += some
                at += g.count
            loaded.append((started, by_slot))
        leaving = []

        def send(part, z):
            for k in range(dps):
                rows = pl.ds(k * block, block)
                leaving.append(copies.start(result.at[part, z, rows, :], goal(sc, outs, part, k, z)))

        def multiply(i, z, at, part):
            y, flipped, own = scratch[2 + 3 * i], scratch[3 + 3 * i], widths[i]
            for s in range(z, z + step):
                wait(loaded[i][1][s])
            whole_y = jnp.concatenate([y[z + s] for s in range(step)], axis=1) if step > 1 else y[z]
            value = nn(flipped[...], whole_y)
            for s in range(step):
                result[part, z + s, :, at : at + own] = value[:, s * own : (s + 1) * own].astype(BF16)

        def flip(i):
            wait(loaded[i][0])
            scratch[3 + 3 * i][...] = scratch[1 + 3 * i][...].T

        if side:
            for i in range(len(products)):
                flip(i)
            for z in range(0, NZ, step):
                for i in range(len(products)):
                    multiply(i, z, sum(widths[:i]), 0)
                for s in range(z, z + step):
                    send(0, s)
        else:
            for i in range(len(products)):
                flip(i)
                for z in range(0, NZ, step):
                    multiply(i, z, 0, i)
                    for s in range(z, z + step):
                        send(i, s)
        wait(leaving)

    return list(manual(body, name, scalars, args, out_shape, scratch, copies_needed, after, hold))


def feed_forward(scalars, rows, weights, bias_row, name, after=(), hold=()):
    count, cols = rows.count, weights.cols

    def body(sc, ins, outs, scratch, copies):
        x, w, b, hidden, slope = scratch
        row_refs, weight_refs = take(ins, len(rows.args))
        started = rows.load(copies, row_refs, x, sc)
        for z in range(NZ):
            started.append(copies.start(weight_refs[0].at[sc[3] ^ z, pl.ds(bias_row, BIAS_ROWS), :], b.at[z]))
        by_slot = weights.load(copies, weight_refs, w, sc)
        wait(started)
        leaving = []
        step = slots_at_once(cols)
        for z in range(0, NZ, step):
            for s in range(z, z + step):
                wait(by_slot[s])
            value = nn(x[...], weights.slots(w, z, step))
            for s in range(step):
                terms = b[z + s].astype(F32)
                u = value[:, s * cols : (s + 1) * cols] + (terms[0:1] + terms[1:2] + terms[2:3])
                cdf = 0.5 + 0.5 * lax.erf(u * math.sqrt(0.5))
                hidden[z + s] = (u * cdf).astype(BF16)
                slope[z + s] = (cdf + u * (jnp.exp(-0.5 * u * u) * (1.0 / math.sqrt(2.0 * math.pi)))).astype(BF16)
                leaving.append(copies.start(hidden.at[z + s], outs[0].at[z + s]))
                leaving.append(copies.start(slope.at[z + s], outs[1].at[z + s]))
        wait(leaving)

    return manual(
        body, name, scalars, rows.args + weights.args, [shape((NZ, count, cols), BF16)] * 2,
        [vmem((count, rows.width)), weights.scratch, vmem((NZ, BIAS_ROWS, cols)), vmem((NZ, count, cols)), vmem((NZ, count, cols))],
        rows.copies + NZ + weights.copies + 2 * NZ, after, hold,
    )


def feed_back(scalars, rows, slope, down, up, nodes, swapped, name, after=(), hold=()):
    count, cols, width = rows.count, down.cols, rows.width

    def body(sc, ins, outs, scratch, copies):
        x, wd, wu, steep, du, gb, total, parts = scratch
        row_refs, ins = take(ins, len(rows.args))
        slope_ref, ins = ins[0], ins[1:]
        down_refs, up_refs = take(ins, len(down.args))
        started = rows.load(copies, row_refs, x, sc)
        down_slots = down.load(copies, down_refs, wd, sc)
        steep_slots = [copies.start(slope_ref.at[z], steep.at[z]) for z in range(NZ)]
        up_slots = up.load(copies, up_refs, wu, sc)
        wait(started)
        leaving = []
        step = slots_at_once(cols)
        for z in range(0, NZ, step):
            for s in range(z, z + step):
                wait(down_slots[s])
                steep_slots[s].wait()
            value = nn(x[...], down.slots(wd, z, step))
            for s in range(step):
                grad = value[:, s * cols : (s + 1) * cols] * steep[z + s].astype(F32)
                gb[z + s : z + s + 1, :] = jnp.sum(grad, axis=0, keepdims=True)
                du[z + s] = grad.astype(BF16)
                leaving.append(copies.start(du.at[z + s], outs[0].at[z + s]))
        leaving.append(copies.start(gb, outs[1]))
        for z in range(NZ):
            wait(up_slots[z])
        total[...] = nt(jnp.concatenate([du[z] for z in range(NZ)], axis=1), wu[...])
        wait(leaving + store_parts(total, parts, nodes, copies, outs[2:], sc, False, swapped))

    out = manual(
        body, name, scalars, rows.args + [slope] + down.args + up.args,
        [shape((NZ, count, cols), BF16), shape((NZ, cols), F32)] + [shape((count // nodes, width), BF16)] * nodes,
        [vmem((count, width)), down.scratch, up.scratch, vmem((NZ, count, cols)), vmem((NZ, count, cols)),
         vmem((NZ, cols), F32), vmem((count, width), F32), vmem((nodes, count // nodes, width))],
        rows.copies + down.copies + up.copies + 2 * NZ + 1 + nodes, after, hold,
    )
    return out[0], out[1], list(out[2 : 2 + nodes]), out[2 + nodes :]


def feed_out(scalars, hidden, down, nodes, swapped, name, after=(), hold=()):
    _, count, cols = hidden.shape
    width = down.depth

    def body(sc, ins, outs, scratch, copies):
        y, w, total, parts = scratch
        started = [copies.start(ins[0].at[z], y.at[z]) for z in range(NZ)]
        by_slot = down.load(copies, ins[1:], w, sc)
        wait(started)
        for z in range(NZ):
            wait(by_slot[z])
        total[...] = nt(jnp.concatenate([y[z] for z in range(NZ)], axis=1), w[...])
        wait(store_parts(total, parts, nodes, copies, outs, sc, False, swapped))

    return manual(
        body, name, scalars, [hidden] + down.args, [shape((count // nodes, width), BF16)] * nodes,
        [vmem((NZ, count, cols)), down.scratch, vmem((count, width), F32), vmem((nodes, count // nodes, width))],
        NZ + down.copies + nodes, after, hold,
    )


def head_mask(cols, head):
    lane = lax.broadcasted_iota(jnp.int32, (1, cols), 1)
    return (lane >= head * HD) & (lane < (head + 1) * HD)


def attend(q, k, v):
    cols = q.shape[1]
    q = q * (1.0 / math.sqrt(HD))
    total = None
    for head in range(cols // HD):
        mask = head_mask(cols, head)
        scores = nt(jnp.where(mask, q, 0).astype(BF16), k)
        raised = jnp.exp(scores - jnp.max(scores, axis=1, keepdims=True))
        soft = raised * (1.0 / jnp.sum(raised, axis=1, keepdims=True))
        mixed = nn(soft.astype(BF16), jnp.where(mask, v, 0).astype(BF16))
        total = mixed if total is None else total + mixed
    return total.astype(BF16)


def attend_back(q, k, v, do):
    cols = q.shape[1]
    q = (q * (1.0 / math.sqrt(HD))).astype(BF16)
    dq = dk = dv = None
    for head in range(cols // HD):
        mask = head_mask(cols, head)
        qh = jnp.where(mask, q, 0).astype(BF16)
        doh = jnp.where(mask, do, 0).astype(BF16)
        kh = jnp.where(mask, k, 0).astype(BF16)
        scores = nt(k, qh)
        raised = jnp.exp(scores - jnp.max(scores, axis=0, keepdims=True))
        soft = raised * (1.0 / jnp.sum(raised, axis=0, keepdims=True))
        dsoft = nt(v, doh)
        dot = jnp.sum(dsoft * soft, axis=0, keepdims=True)
        dscores = (soft * (dsoft - dot)).astype(BF16)
        dvh = nn(soft.astype(BF16), doh)
        dkh = nn(dscores, qh)
        dqh = tn(dscores, kh)
        dq = dqh if dq is None else dq + dqh
        dk = dkh if dk is None else dk + dkh
        dv = dvh if dv is None else dv + dvh
    return (dq * (1.0 / math.sqrt(HD))).astype(BF16), dk.astype(BF16), dv.astype(BF16)


def whole_image(sc):
    return pl.ds(pl.multiple_of(sc[2] * (SEQ // 2), 32), SEQ)


def split_rows(sc):
    return pl.ds(pl.multiple_of((1 - sc[2]) * SEQ, 32), SEQ // 2)


def own_slot(dims):
    return pl.BlockSpec((1,) + dims, lambda s, *_: (2 * s, 0, 0))


def attend_whole(scalars, qkv, after=(), hold=()):
    slots, count, triple = qkv.shape
    cols = triple // 3

    def body(sc, qkv_ref, o_ref):
        rows = whole_image(sc)
        q, k, v = (qkv_ref[0, rows, j * cols : (j + 1) * cols] for j in range(3))
        o_ref[0] = attend(q, k, v)

    return call(
        body, "attend_whole", (slots,), scalars, [slot((count, triple))], slot((SEQ, cols)),
        shape((slots, SEQ, cols), BF16), [qkv],
        after=after, hold=hold, nbytes=2 * slots * count * 4 * cols,
    )


def attend_split(scalars, qkv, partner, after=(), hold=()):
    slots, half, triple = partner.shape
    count = qkv.shape[1]
    cols = triple // 3

    def body(sc, qkv_ref, partner_ref, mine_ref, theirs_ref, joined):
        joined[:half, :] = qkv_ref[0, split_rows(sc), :]
        joined[half:, :] = partner_ref[0]
        q, k, v = (joined[:, j * cols : (j + 1) * cols] for j in range(3))
        mixed = attend(q, k, v)
        mine_ref[0] = mixed[:half]
        theirs_ref[0] = mixed[half:]

    return call(
        body, "attend_split", (slots,), scalars, [own_slot((count, triple)), slot((half, triple))],
        [slot((half, cols))] * 2, [shape((slots, half, cols), BF16)] * 2, [qkv, partner],
        scratch=[pltpu.VMEM((2 * half, triple), BF16)],
        after=after, hold=hold, nbytes=2 * slots * count * 4 * cols,
    )


def attend_whole_back(scalars, qkv, do, after=(), hold=()):
    slots, count, triple = qkv.shape
    cols = triple // 3

    def body(sc, qkv_ref, do_ref, out_ref):
        rows = whole_image(sc)
        q, k, v = (qkv_ref[0, rows, j * cols : (j + 1) * cols] for j in range(3))
        grads = attend_back(q, k, v, do_ref[0, rows, :])
        for j in range(3):
            out_ref[0, :, j * cols : (j + 1) * cols] = grads[j]

    return call(
        body, "attend_whole_back", (slots,), scalars, [slot((count, triple)), slot((count, cols))],
        slot((SEQ, triple)), shape((slots, SEQ, triple), BF16), [qkv, do],
        after=after, hold=hold, nbytes=2 * slots * count * 7 * cols,
    )


def attend_split_back(scalars, qkv, partner, do, do_partner, after=(), hold=()):
    slots, half, triple = partner.shape
    count = qkv.shape[1]
    cols = triple // 3

    def body(sc, qkv_ref, partner_ref, do_ref, do_partner_ref, mine_ref, theirs_ref, joined, joined_do):
        joined[:half, :] = qkv_ref[0, split_rows(sc), :]
        joined[half:, :] = partner_ref[0]
        joined_do[:half, :] = do_ref[0, split_rows(sc), :]
        joined_do[half:, :] = do_partner_ref[0]
        q, k, v = (joined[:, j * cols : (j + 1) * cols] for j in range(3))
        grads = attend_back(q, k, v, joined_do[...])
        for j in range(3):
            mine_ref[0, :, j * cols : (j + 1) * cols] = grads[j][:half]
            theirs_ref[0, :, j * cols : (j + 1) * cols] = grads[j][half:]

    return call(
        body, "attend_split_back", (slots,), scalars,
        [own_slot((count, triple)), slot((half, triple)), own_slot((count, cols)), slot((half, cols))],
        [slot((half, triple))] * 2, [shape((slots, half, triple), BF16)] * 2, [qkv, partner, do, do_partner],
        scratch=[pltpu.VMEM((2 * half, triple), BF16), pltpu.VMEM((2 * half, cols), BF16)],
        after=after, hold=hold, nbytes=2 * slots * count * 7 * cols,
    )


def row_tile(count):
    return count // 3 if (count // 3) % 16 == 0 else count


def tiles(rows, width):
    return pl.BlockSpec((rows, width), lambda i, *_: (i, 0))


def to_relative(sc, scratch, out_ref, block):
    dps = scratch.shape[1] // block
    for k in range(dps):
        out_ref[:, k * block : (k + 1) * block] = scratch[
            :, pl.ds(pl.multiple_of((sc[0] ^ k) * block, block), block)
        ].astype(out_ref.dtype)


def from_relative(sc, refs, scratch, block):
    dps = scratch.shape[1] // block
    for k in range(dps):
        here = slice(k * block, (k + 1) * block)
        piece = refs[0][:, here].astype(F32)
        for ref in refs[1:]:
            piece += ref[:, here].astype(F32)
        scratch[:, pl.ds(pl.multiple_of((sc[0] ^ k) * block, block), block)] = piece


def normed(rows):
    centred = rows - jnp.mean(rows, axis=-1, keepdims=True)
    inverse = lax.rsqrt(jnp.mean(centred * centred, axis=-1, keepdims=True) + 1e-06)
    return centred * inverse, inverse


def norm_back(hat, inverse, grad, gain):
    scaled = grad * gain
    return inverse * (
        scaled - jnp.mean(scaled, axis=-1, keepdims=True) - hat * jnp.mean(scaled * hat, axis=-1, keepdims=True)
    )


def first_norm(scalars, tokens, cotangent, vectors, dps, after=(), hold=()):
    count, width = tokens.shape
    rows, block = row_tile(count), width // dps

    def body(sc, x_ref, cot_ref, vec_ref, a_ref, g_ref, scratch):
        hat, _ = normed(x_ref[...])
        scratch[...] = hat * vec_ref[0:1] + vec_ref[1:2]
        to_relative(sc, scratch, a_ref, block)
        to_relative(sc, cot_ref, g_ref, block)

    return call(
        body, "first_norm", (count // rows,), scalars,
        [tiles(rows, width)] * 2 + [whole(vectors.shape)], [tiles(rows, width)] * 2,
        [shape((count, width), BF16)] * 2, [tokens, cotangent, vectors],
        scratch=[pltpu.VMEM((rows, width), F32)], after=after, hold=hold, nbytes=12 * count * width,
    )


def second_norm(scalars, tokens, parts, vectors, dps, after=(), hold=()):
    count, width = tokens.shape
    rows, block = row_tile(count), width // dps

    def body(sc, x_ref, vec_ref, *refs):
        h_ref, c_ref, scratch = refs[-3:]
        from_relative(sc, refs[:-3], scratch, block)
        h = x_ref[...] + scratch[...] + vec_ref[4:5]
        h_ref[...] = h
        hat, _ = normed(h)
        scratch[...] = hat * vec_ref[2:3] + vec_ref[3:4]
        to_relative(sc, scratch, c_ref, block)

    return call(
        body, "second_norm", (count // rows,), scalars,
        [tiles(rows, width), whole(vectors.shape)] + [tiles(rows, width)] * len(parts), [tiles(rows, width)] * 2,
        [shape((count, width), F32), shape((count, width), BF16)], [tokens, vectors] + list(parts),
        scratch=[pltpu.VMEM((rows, width), F32)], after=after, hold=hold, nbytes=14 * count * width,
    )


def layer_output(scalars, middle, parts, vectors, dps, after=(), hold=()):
    count, width = middle.shape
    rows, block = row_tile(count), width // dps

    def body(sc, h_ref, vec_ref, *refs):
        out_ref, scratch = refs[-2:]
        from_relative(sc, refs[:-2], scratch, block)
        out_ref[...] = h_ref[...] + scratch[...] + vec_ref[5:6]

    return call(
        body, "layer_output", (count // rows,), scalars,
        [tiles(rows, width), whole(vectors.shape)] + [tiles(rows, width)] * len(parts), tiles(rows, width),
        shape((count, width), F32), [middle, vectors] + list(parts),
        scratch=[pltpu.VMEM((rows, width), F32)], after=after, hold=hold, nbytes=12 * count * width,
    )


def add_rows(ref, values):
    step = pl.program_id(0)

    @pl.when(step == 0)
    def _():
        ref[...] = values

    @pl.when(step > 0)
    def _():
        ref[...] += values


def second_norm_back(scalars, middle, cotangent, parts, vectors, dps, after=(), hold=()):
    count, width = middle.shape
    rows, block = row_tile(count), width // dps

    def body(sc, h_ref, cot_ref, vec_ref, *refs):
        dh_ref, e_ref, sums_ref, scratch = refs[-4:]
        from_relative(sc, refs[:-4], scratch, block)
        dc = scratch[...]
        hat, inverse = normed(h_ref[...])
        cot = cot_ref[...]
        dh = cot + norm_back(hat, inverse, dc, vec_ref[2:3])
        dh_ref[...] = dh
        scratch[...] = dh
        to_relative(sc, scratch, e_ref, block)
        column = lambda values: jnp.sum(values, axis=0, keepdims=True)
        add_rows(sums_ref, jnp.concatenate([column(dc * hat), column(dc), column(dh), column(cot)], axis=0))

    return call(
        body, "second_norm_back", (count // rows,), scalars,
        [tiles(rows, width)] * 2 + [whole(vectors.shape)] + [tiles(rows, width)] * len(parts),
        [tiles(rows, width)] * 2 + [whole((4, width))],
        [shape((count, width), F32), shape((count, width), BF16), shape((4, width), F32)],
        [middle, cotangent, vectors] + list(parts),
        scratch=[pltpu.VMEM((rows, width), F32)], after=after, hold=hold, nbytes=18 * count * width,
    )


def first_norm_back(scalars, tokens, middle_grad, parts, vectors, dps, after=(), hold=()):
    count, width = tokens.shape
    rows, block = row_tile(count), width // dps

    def body(sc, x_ref, dh_ref, vec_ref, *refs):
        dx_ref, sums_ref, scratch = refs[-3:]
        from_relative(sc, refs[:-3], scratch, block)
        da = scratch[...]
        hat, inverse = normed(x_ref[...])
        dx_ref[...] = dh_ref[...] + norm_back(hat, inverse, da, vec_ref[0:1])
        column = lambda values: jnp.sum(values, axis=0, keepdims=True)
        add_rows(sums_ref, jnp.concatenate([column(da * hat), column(da)], axis=0))

    return call(
        body, "first_norm_back", (count // rows,), scalars,
        [tiles(rows, width)] * 2 + [whole(vectors.shape)] + [tiles(rows, width)] * len(parts),
        [tiles(rows, width), whole((2, width))],
        [shape((count, width), F32), shape((2, width), F32)], [tokens, middle_grad, vectors] + list(parts),
        scratch=[pltpu.VMEM((rows, width), F32)], after=after, hold=hold, nbytes=16 * count * width,
    )


def adam_step(weight, gradient, first, second, rate, decay):
    first = 0.9 * first + 0.1 * gradient
    second = 0.999 * second + 0.001 * gradient * gradient
    first_fix = 1.0 - 0.9**STEP
    second_fix = 1.0 - 0.999**STEP
    update = first / first_fix / (jnp.sqrt(second / second_fix) + 1e-08) + decay * weight
    return (gradient, first, second, weight - rate * update)


def by_part(columns, heads):
    return jnp.concatenate([columns[:, (h * 3 + c) * HD : (h * 3 + c + 1) * HD] for c in range(3) for h in range(heads)], axis=1)


def by_head(columns, heads):
    return jnp.concatenate([columns[:, (c * heads + h) * HD : (c * heads + h + 1) * HD] for h in range(heads) for c in range(3)], axis=1)


def plain(body, name, args, out_shape, after=(), hold=()):
    given, extra = len(args), len(after) + len(hold)
    made = len(out_shape)
    nbytes = sum(math.prod(a.shape) * a.dtype.itemsize for a in list(args) + list(out_shape))

    def run(*refs):
        body(*refs[:given], *refs[given + extra : given + extra + made])

    anywhere = pl.BlockSpec(memory_space=pltpu.HBM)
    here = pl.BlockSpec(memory_space=pltpu.VMEM)
    first = given + len(after)
    return pl.pallas_call(
        run, name=name,
        out_shape=list(out_shape) + [shape(h.shape, h.dtype) for h in hold],
        in_specs=[pl.BlockSpec(memory_space=pltpu.SMEM)] + [here] * (given - 1) + [anywhere] * extra,
        out_specs=[here] * made + [anywhere] * len(hold),
        input_output_aliases={first + i: made + i for i in range(len(hold))},
        compiler_params=pltpu.CompilerParams(vmem_limit_bytes=VMEM_LIMIT), cost_estimate=cost(name, nbytes),
    )(*args, *after, *hold)


def attn_piece(scalars, w_qkv, w_out):
    heads = w_qkv.shape[1] // (3 * HD)
    triple = w_qkv.shape[1]

    def body(sc, qkv_ref, out_ref, piece_ref):
        piece_ref[:, :triple] = by_part(qkv_ref[...], heads).astype(BF16)
        piece_ref[:, triple:] = out_ref[...].T.astype(BF16)

    return plain(body, "attn_piece", [scalars, w_qkv, w_out], [shape((w_qkv.shape[0], triple + w_out.shape[0]), BF16)])[0]


def hidden_pieces(scalars, w_up, hidden_bias, w_down, after=()):
    block, cols = w_up.shape[0], w_up.shape[1] // 2

    def body(sc, up_ref, bias_ref, down_ref, my_up_ref, my_down_ref, theirs_ref):
        mine, other = (pl.ds(pl.multiple_of(h * cols, cols), cols) for h in (sc[4], 1 - sc[4]))
        my_up_ref[:block, :] = up_ref[:, mine].astype(BF16)
        my_down_ref[...] = down_ref[mine, :].T.astype(BF16)
        theirs_ref[:block, :] = up_ref[:, other].astype(BF16)
        theirs_ref[block:, :] = down_ref[other, :].T.astype(BF16)
        rest = bias_ref[:, mine]
        row = lax.broadcasted_iota(jnp.int32, (BIAS_ROWS, cols), 0)
        terms = jnp.zeros((BIAS_ROWS, cols), F32)
        for i in range(3):
            term = rest.astype(BF16).astype(F32)
            terms = jnp.where(row == i, term, terms)
            rest = rest - term
        my_up_ref[block:, :] = terms.astype(BF16)

    return plain(
        body, "hidden_pieces", [scalars, w_up, hidden_bias[None, :], w_down],
        [shape((block + BIAS_ROWS, cols), BF16), shape((block, cols), BF16), shape((2 * block, cols), BF16)], after,
    )


def attn_adam(scalars, sums, w_qkv, qkv_m, qkv_v, w_out, out_m, out_v, after=()):
    heads, triple = w_qkv.shape[1] // (3 * HD), w_qkv.shape[1]
    count = len(sums)

    def body(sc, *refs):
        total = None
        for ref in refs[:count]:
            piece = (ref[0] if len(ref.shape) == 3 else ref[...]).astype(F32)
            total = piece if total is None else total + piece
        qw, qm, qv, ow, om, ov = (r[...] for r in refs[count : count + 6])
        outs = refs[count + 6 :]
        new = adam_step(qw, by_head(total[:, :triple], heads), qm, qv, 0.1, 0.05)
        new += adam_step(ow, total[:, triple:].T, om, ov, 0.2, 0.05)
        for ref, value in zip(outs, new):
            ref[...] = value

    out = plain(
        body, "attn_adam", [scalars] + list(sums) + [w_qkv, qkv_m, qkv_v, w_out, out_m, out_v],
        [shape(w_qkv.shape, F32)] * 4 + [shape(w_out.shape, F32)] * 4, after,
    )
    return tuple(out[:4]), tuple(out[4:])


def hidden_adam(scalars, total, far, up, down, after=(), hold=()):
    block, cols = far.shape[0] // 2, far.shape[1]

    def body(sc, total_ref, far_ref, *refs):
        ins, outs = take(refs, 6)
        up_grad, down_grad = outs[0], outs[4]
        for ref, half in ((total_ref, sc[4]), (far_ref, 1 - sc[4])):
            at = pl.ds(pl.multiple_of(half * cols, cols), cols)
            down_grad[at, :] = ref[:block, :].astype(F32).T
            up_grad[:, at] = ref[block : 2 * block, :].astype(F32)
        for (w, m, v), made, rate in ((ins[:3], outs[:4], 0.1), (ins[3:], outs[4:], 0.05)):
            new = adam_step(w[...], made[0][...], m[...], v[...], rate, 0.05)
            for ref, value in zip(made[1:], new[1:]):
                ref[...] = value

    out = plain(
        body, "hidden_adam", [scalars, total, far] + list(up) + list(down),
        [shape(up[0].shape, F32)] * 4 + [shape(down[0].shape, F32)] * 4, after, hold,
    )
    return tuple(out[:4]), tuple(out[4:8]), out[8:]


def solution(mesh):
    dps, tensor = mesh.shape["dp"], mesh.shape["tensor"]
    nodes = tensor // NZ
    devices = dps * tensor

    def snake(columns):
        return [(d, z) for i, d in enumerate(columns) for z in (range(NZ) if i % 2 == 0 else range(NZ - 1, -1, -1))]

    rings = [[d * tensor + z * nodes + c for d, z in snake([i ^ (i >> 1) for i in range(dps)])] for c in range(nodes)]
    z_groups = [[d * tensor + z * nodes + c for z in range(NZ)] for d in range(dps) for c in range(nodes)]
    half_rings = [
        [d * tensor + z * nodes + c for d, z in snake(range(x, dps, 2))] for x in range(2) for c in range(nodes)
    ]

    def swap(value, flip):
        return lax.ppermute(value, AXES, [(i, i ^ flip) for i in range(devices)])

    def gather_ring(piece, groups):
        return lax.all_gather(piece, AXES, axis=0, axis_index_groups=groups)

    def scatter_ring(total, groups):
        return lax.psum_scatter(total, AXES, scatter_dimension=0, axis_index_groups=groups, tiled=True)[0]

    def by_weight(k):
        return (bin(k).count("1"), k)

    def gather(own, count, unit, low_first):
        bufs = [own] + [None] * (count - 1)
        for k in sorted(range(1, count), key=by_weight):
            last = k & -k if low_first else 1 << (k.bit_length() - 1)
            bufs[k] = swap(bufs[k ^ last], last * unit)
        return bufs

    def plus(left, right):
        return (left.astype(F32) + right.astype(F32)).astype(BF16)

    def add_up(sums):
        total = sums[0].astype(F32)
        for piece in sums[1:]:
            total = total + piece.astype(F32)
        return total.astype(BF16)

    def along_z(piece):
        return [piece] + [swap(piece, j * nodes) for j in range(1, NZ)]

    def relative(own):
        return [own] + [swap(own, j) for j in range(1, nodes)]

    def ordered_rows(parts, member):
        if parts[0].shape[0] % 16 == 0:
            return Rows(parts, True)
        flip = 1
        while len(parts) > 1:
            odd = (member // flip) % 2 == 1
            parts = [
                jnp.where(odd, jnp.concatenate([b, a], axis=0), jnp.concatenate([a, b], axis=0))
                for a, b in zip(parts[0::2], parts[1::2])
            ]
            flip *= 2
        return Rows(parts, True)

    def relative_rows(parts, swapped=0):
        if parts[0].shape[0] % 16:
            parts = [jnp.concatenate(parts, axis=0)]
        return Rows(parts, False, swapped)

    def send_parts(parts):
        return [parts[0]] + [swap(parts[j], j) for j in range(1, nodes)]

    def per_device(
        tokens, cotangent, vectors, vectors_m, vectors_v,
        w_qkv, qkv_m, qkv_v, w_out, out_m, out_v, w_up, up_m, up_v,
        hidden_bias, bias_m, bias_v, w_down, down_m, down_v,
    ):
        dp_index = lax.axis_index("dp")
        tensor_index = lax.axis_index("tensor")
        z_index, member = tensor_index // nodes, tensor_index % nodes
        odd_x = dp_index % 2
        scalars = jnp.stack([dp_index, member, z_index % 2, z_index, odd_x]).astype(jnp.int32)
        block = w_qkv.shape[0]
        triple, width = w_qkv.shape[1], w_out.shape[0]
        hidden_here = w_up.shape[1] // 2

        attn_z = along_z(attn_piece(scalars, w_qkv, w_out))
        my_up, my_down, theirs = hidden_pieces(scalars, w_up, hidden_bias, w_down, after=[attn_z[0]])
        arrived = swap(theirs, tensor)
        a_own, g_own = first_norm(scalars, tokens, cotangent, vectors, dps, after=[my_up])
        a_parts = relative(a_own)
        (lower,) = pack(scalars, attn_z[:2], after=[a_own])
        up_piece = jnp.concatenate([my_up, arrived[:block]], axis=0)
        down_piece = jnp.concatenate([my_down, arrived[block:]], axis=0)
        upper, up_piece, down_piece = pack(scalars, attn_z[2:], after=[lower], hold=[up_piece, down_piece])
        up_z = gather_ring(up_piece, z_groups)
        if dps == 4:
            lowers, uppers = [swap(lower, tensor), swap(lower, 2 * tensor)], [swap(upper, tensor), swap(upper, 2 * tensor)]
            lowers = list(gate(scalars, "gate_lower", [upper], lowers))
            lowers[0], uppers[1] = gate(scalars, "gate_gather", [lowers[1], uppers[0]], [lowers[0], uppers[1]])
            lowers = [lower] + lowers + [swap(lowers[0], 2 * tensor)]
            uppers = [upper] + uppers + [swap(uppers[1], tensor)]
        else:
            lowers, uppers = gather(lower, dps, tensor, False), gather(upper, dps, tensor, True)
        halves = [(0, [(2 * k + z // 2, z % 2) for z in range(NZ)]) for k in range(dps)]
        attn_w = [half for pair in zip(lowers, uppers) for half in pair]
        qkv_w = Weights(attn_w, halves, block, 0, triple)
        out_w = Weights(attn_w, halves, block, triple, width)

        a_rows = ordered_rows(a_parts, member)
        qkv, qkv_theirs, g_own = project(scalars, a_rows, qkv_w, "qkv", hold=[g_own])
        qkv_partner = swap(qkv_theirs, nodes)
        g_far = swap(g_own, tensor)
        (up_z,) = gate(scalars, "gate_up", [qkv], [up_z])
        up_w = Weights(
            gather(up_z, dps // 2, 2 * tensor, False),
            [(k % 2 * (block + BIAS_ROWS), [(k // 2, lambda sc, z=z: sc[3] ^ z) for z in range(NZ)]) for k in range(dps)],
            block, 0, hidden_here,
        )
        mixed = attend_whole(scalars, qkv, after=[up_z])
        mixed_mine, mixed_theirs, down_piece = attend_split(scalars, qkv, qkv_partner, after=[mixed], hold=[down_piece])
        down_w = Weights(
            [gather_ring(down_piece, half_rings)],
            [(k % 2 * block, [(0, lambda sc, k=k, z=z: hidden_place(sc, k, z)) for z in range(NZ)]) for k in range(dps)],
            block, 0, hidden_here,
        )
        mixed = SplitSlots(mixed, mixed_mine, swap(mixed_theirs, nodes))
        *attn_parts, g_far = project_back(
            scalars, mixed, out_w, nodes, "attn_out", after=up_w.args[1:], hold=[g_far]
        )
        middle, c_own = second_norm(scalars, tokens, send_parts(attn_parts), vectors, dps)

        c_far = swap(c_own, tensor)
        g_rows, g_far = relative_rows(relative(g_own)), relative_rows(relative(g_far), dps)
        c_rows = relative_rows(relative(c_own))
        hidden, slope = feed_forward(scalars, c_rows, up_w, block, "feed_forward")
        du, bias_near, dc_near, _ = feed_back(
            scalars, g_rows, slope, down_w, up_w, nodes, 0, "feed_back", after=[hidden]
        )
        dc_near = send_parts(dc_near)
        (c_far,) = gate(scalars, "gate_rows", [du], [c_far])
        c_far = relative_rows(relative(c_far), dps)
        hidden_far, slope_far = feed_forward(scalars, c_far, up_w, block, "feed_forward_far", after=[du])
        du_far, bias_far, dc_far, _ = feed_back(
            scalars, g_far, slope_far, down_w, up_w, nodes, dps, "feed_back_far", after=[hidden_far] + dc_near[1:]
        )
        (dc_sum,) = add(scalars, send_parts(dc_far), after=[du_far])
        dc_arrived = swap(dc_sum, tensor)

        out_far = feed_out(scalars, hidden_far, down_w, nodes, dps, "feed_out_far", after=[dc_sum])

        def hidden_goal(sc, outs, part, k, z):
            return outs[0].at[hidden_place(sc, k, z), pl.ds((2 * (k % 2) + part) * block, block), :]

        (hidden_part,) = weight_grads(
            scalars,
            [([g_rows, g_far], [Slots(hidden), Slots(hidden_far)]), ([c_rows, c_far], [Slots(du), Slots(du_far)])],
            dps, [shape((NZ * dps // 2, 4 * block, hidden_here), BF16)],
            hidden_goal, False, "hidden_grad", after=[out_far[0]],
        )
        hidden_total = scatter_ring(hidden_part, half_rings)
        middle_grad, e_own, sums_two = second_norm_back(
            scalars, middle, cotangent, dc_near + [dc_arrived], vectors, dps, after=[hidden_part]
        )
        out_far = send_parts(out_far)

        e_rows = ordered_rows(relative(e_own), member)
        dmixed, dmixed_theirs, out_far[0] = project(
            scalars, e_rows, out_w, "mixed_grad", after=out_far[1:], hold=[out_far[0]]
        )
        dmixed_partner = swap(dmixed_theirs, nodes)
        out_arrived = swap(add_up(out_far), tensor)
        out_near = feed_out(scalars, hidden, down_w, nodes, 0, "feed_out", after=[dmixed])
        dqkv_mine, dqkv_theirs = attend_split_back(
            scalars, qkv, qkv_partner, dmixed, dmixed_partner, after=[out_near[0]]
        )
        dqkv = attend_whole_back(scalars, qkv, dmixed, after=[dqkv_mine])
        dqkv = SplitSlots(dqkv, dqkv_mine, swap(dqkv_theirs, nodes))

        def attn_goal(sc, outs, part, k, z):
            return outs[0].at[ring_place(gray_rank(sc[0] ^ k, dps), sc[3] ^ z)]

        (attn_part,) = weight_grads(
            scalars, [([a_rows], [dqkv]), ([e_rows], [mixed])],
            dps, [shape((NZ * dps, block, triple + width), BF16)], attn_goal, True, "attn_grad", after=[out_arrived],
        )
        da_parts = send_parts(project_back(scalars, dqkv, qkv_w, nodes, "first_back", after=[attn_part]))
        input_grad, sums_one, hidden_total = first_norm_back(
            scalars, tokens, middle_grad, da_parts, vectors, dps, hold=[hidden_total]
        )
        attn_part = scatter_ring(attn_part, rings)

        here = (jnp.arange(nodes)[:, None] == member) & (jnp.arange(2)[None, :] == odd_x)
        own_slot_of = (jnp.arange(NZ)[:, None] ^ z_index) == jnp.arange(NZ)[None, :]
        bias_here = jnp.sum(jnp.where(own_slot_of[:, :, None], (bias_near + bias_far)[None], 0.0), axis=1)
        bias_part = jnp.where(here[None, :, :, None], bias_here[:, None, None, :], 0.0)
        rows_two = sums_one.shape[0] + sums_two.shape[0]
        value = jnp.concatenate([sums_one, sums_two, bias_part.reshape(-1, sums_two.shape[1])], axis=0)
        for flip in [1 << i for i in range(devices.bit_length() - 1)]:
            value = value + swap(value, flip)
        all_sums = value
        output = layer_output(scalars, middle, send_parts(out_near) + [out_arrived], vectors, dps, after=[input_grad])
        far = swap(hidden_total[2 * block :], tensor)
        up_res, down_res, _ = hidden_adam(
            scalars, hidden_total, far, (w_up, up_m, up_v), (w_down, down_m, down_v), after=[output]
        )
        qkv_res, out_res = attn_adam(scalars, [attn_part], w_qkv, qkv_m, qkv_v, w_out, out_m, out_v, after=[up_res[0]])
        vector_total = all_sums[:rows_two]
        bias_total = lax.dynamic_slice_in_dim(
            all_sums[rows_two:].reshape(-1), tensor_index * 2 * hidden_here, 2 * hidden_here, 0
        )

        vec_res = adam_step(vectors, vector_total, vectors_m, vectors_v, 0.3, 0.0)
        bias_res = adam_step(hidden_bias, bias_total, bias_m, bias_v, 0.3, 0.0)
        return (output, input_grad) + vec_res + qkv_res + out_res + up_res + bias_res + down_res

    rows, both = P(AXES, None), P("dp", "tensor")
    turned = P("tensor", "dp")
    in_specs = (
        (rows,) * 2 + (P(),) * 3 + (both,) * 3 + (turned,) * 3 + (both,) * 3 + (P("tensor"),) * 3 + (turned,) * 3
    )
    out_specs = (
        (rows,) * 2 + (P(),) * 4 + (both,) * 4 + (turned,) * 4 + (both,) * 4 + (P("tensor"),) * 4 + (turned,) * 4
    )
    return jax.shard_map(per_device, mesh=mesh, in_specs=in_specs, out_specs=out_specs, check_vma=False)
```

```python
import math

import jax
import jax.numpy as jnp
from jax import lax
from jax.experimental import pallas as pl
from jax.experimental.pallas import tpu as pltpu
from jax.sharding import PartitionSpec as P

HD = 64
SEQ = 576
STEP = 10
NZ = 4
BIAS_ROWS = 16
AXES = ("dp", "tensor")
F32 = jnp.float32
BF16 = jnp.bfloat16
VMEM_LIMIT = 63 * 1024 * 1024
TIMES = {"gate_lower": 1, "gate_gather": 1000, "attn_out": 1000, "second_norm_back": 1000, "feed_out": 5, "attend_whole_back": 20, "first_back": 1000}


def nn(left, right):
    return jnp.dot(left, right, preferred_element_type=F32)


def nt(left, right):
    return lax.dot_general(left, right, (((1,), (1,)), ((), ())), preferred_element_type=F32)


def tn(left, right):
    return lax.dot_general(left, right, (((0,), (0,)), ((), ())), preferred_element_type=F32)


def cost(name, nbytes):
    return pl.CostEstimate(flops=int(5e8 * TIMES.get(name, 0)), bytes_accessed=int(nbytes), transcendentals=0)


def call(body, name, grid, scalars, in_specs, out_specs, out_shape, args, scratch=(), after=(), hold=(), nbytes=0):
    given, extra = len(args), len(after) + len(hold)
    single = not isinstance(out_shape, (list, tuple))
    out_specs, out_shape = ([out_specs], [out_shape]) if single else (list(out_specs), list(out_shape))
    made = len(out_shape)

    def run(sc, *refs):
        rest = refs[given + extra :]
        body(sc, *refs[:given], *rest[:made], *rest[made + len(hold) :])

    anywhere = pl.BlockSpec(memory_space=pltpu.HBM)
    first = 1 + given + len(after)
    out = pl.pallas_call(
        run,
        name=name,
        grid_spec=pltpu.PrefetchScalarGridSpec(
            num_scalar_prefetch=1,
            grid=grid,
            in_specs=list(in_specs) + [anywhere] * extra,
            out_specs=out_specs + [anywhere] * len(hold),
            scratch_shapes=list(scratch),
        ),
        out_shape=out_shape + [shape(h.shape, h.dtype) for h in hold],
        input_output_aliases={first + i: made + i for i in range(len(hold))},
        compiler_params=pltpu.CompilerParams(vmem_limit_bytes=VMEM_LIMIT),
        cost_estimate=cost(name, nbytes),
    )(scalars, *args, *after, *hold)
    return out[0] if single and not hold else tuple(out)


def shape(dims, dtype):
    return jax.ShapeDtypeStruct(dims, dtype)


def whole(dims):
    return pl.BlockSpec(dims, lambda *_: (0,) * len(dims))


def slot(dims):
    return pl.BlockSpec((1,) + dims, lambda s, *_: (s, 0, 0))


def lower_slots(dims):
    return pl.BlockSpec((1,) + dims, lambda s, *_: (jnp.minimum(s, NZ // 2 - 1), 0, 0))


def upper_slots(dims):
    return pl.BlockSpec((1,) + dims, lambda s, *_: (jnp.maximum(s - NZ // 2, 0), 0, 0))


class Copies:
    def __init__(self, sems):
        self.sems, self.used = sems, 0

    def start(self, source, target):
        copy = pltpu.make_async_copy(source, target, self.sems.at[self.used])
        self.used += 1
        copy.start()
        return copy


def wait(copies):
    for copy in copies:
        copy.wait()


def manual(body, name, scalars, args, out_shape, scratch, copies, after=(), hold=()):
    given, extra = len(args), len(after) + len(hold)
    nbytes = sum(math.prod(a.shape) * a.dtype.itemsize for a in list(args) + list(out_shape))

    def run(sc, *refs):
        rest = refs[given + extra :]
        made = len(out_shape) + len(hold)
        body(sc, refs[:given], rest[:made], rest[made:-1], Copies(rest[-1]))

    anywhere = pl.BlockSpec(memory_space=pltpu.HBM)
    first = 1 + given + len(after)
    return pl.pallas_call(
        run,
        name=name,
        in_specs=[pl.BlockSpec(memory_space=pltpu.SMEM)] + [anywhere] * (given + extra),
        out_specs=[anywhere] * (len(out_shape) + len(hold)),
        out_shape=list(out_shape) + [shape(h.shape, h.dtype) for h in hold],
        input_output_aliases={first + i: len(out_shape) + i for i in range(len(hold))},
        scratch_shapes=list(scratch) + [pltpu.SemaphoreType.DMA((copies,))],
        compiler_params=pltpu.CompilerParams(vmem_limit_bytes=VMEM_LIMIT),
        cost_estimate=cost(name, nbytes),
    )(scalars, *args, *after, *hold)


def vmem(dims, dtype=BF16):
    return pltpu.VMEM(dims, dtype)


class Weights:
    def __init__(self, arrays, blocks, block, col, cols):
        full = arrays[0].shape[2]
        if (col % 128 or cols % 128) and cols != full:
            arrays, col, full = [a[:, :, col : col + cols] for a in arrays], 0, cols
        self.args, self.blocks, self.block = list(arrays), blocks, block
        self.col, self.cols, self.full = col, cols, full
        self.depth = block * len(blocks)
        self.flat = cols % 128 == 0
        self.scratch = vmem((self.depth, NZ * cols) if self.flat else (NZ, self.depth, cols))
        self.copies = len(blocks) * NZ

    def load(self, copies, refs, target, sc):
        by_slot = [[] for _ in range(NZ)]
        for z in range(NZ):
            for k, (row, places) in enumerate(self.blocks):
                number, place = places[z]
                source = refs[number].at[place(sc) if callable(place) else place, pl.ds(row, self.block), :]
                if self.cols != self.full:
                    source = source.at[:, pl.ds(self.col, self.cols)]
                rows = pl.ds(k * self.block, self.block)
                goal = target.at[rows, pl.ds(z * self.cols, self.cols)] if self.flat else target.at[z, rows, :]
                by_slot[z].append(copies.start(source, goal))
        return by_slot

    def slots(self, target, first, count):
        if self.flat:
            return target[:, first * self.cols : (first + count) * self.cols]
        assert count == 1
        return target[first]


def slots_at_once(cols):
    for step in (1, 2, 4):
        if cols * step % 512 == 0 and cols % 128 == 0:
            return step
    return 1


class Rows:
    def __init__(self, parts, ordered, swapped=0):
        self.ordered, self.swapped = ordered, swapped
        self.part = parts[0].shape[0]
        self.args = list(parts)
        self.count = self.part * len(parts)
        self.width = parts[0].shape[1]
        self.copies = len(parts) * max(1, swapped)

    def load(self, copies, refs, target, sc, first=0):
        started = []
        for j, ref in enumerate(refs):
            at = first + j * self.part
            if self.ordered and len(refs) > 1:
                at = pl.multiple_of((sc[1] ^ j) * self.part, 16)
            rows = pl.ds(at, self.part)
            if not self.swapped:
                started.append(copies.start(ref, target.at[rows, :]))
                continue
            block = self.width // self.swapped
            for k in range(self.swapped):
                source = ref.at[:, pl.ds((k ^ 1) * block, block)]
                started.append(copies.start(source, target.at[rows, pl.ds(k * block, block)]))
        return started


class Slots:
    def __init__(self, array):
        self.args, self.copies = [array], NZ
        _, self.count, self.cols = array.shape

    def load(self, copies, refs, target, sc, first=0):
        return [[copies.start(refs[0].at[z], target.at[z, pl.ds(first, self.count), :])] for z in range(NZ)]


class SplitSlots:
    def __init__(self, full, mine, theirs):
        self.args, self.copies = [full, mine, theirs], 2 * NZ
        self.count, self.cols = full.shape[1] + mine.shape[1], full.shape[2]

    def load(self, copies, refs, target, sc, first=0):
        full, mine, theirs = refs
        by_slot = [[copies.start(full.at[z], target.at[z, whole_image(sc), :])] for z in range(NZ)]
        for z in range(NZ):
            source = (theirs if z % 2 else mine).at[z // 2]
            by_slot[z].append(copies.start(source, target.at[z, split_rows(sc), :]))
        return by_slot


def ring_place(column, z):
    return column * NZ + jnp.where(column % 2 == 0, z, NZ - 1 - z)


def hidden_place(sc, k, slot):
    return ring_place((sc[0] ^ k) >> 1, sc[3] ^ slot)


def take(items, count):
    return items[:count], items[count:]


def multiply_parts(y, w, flat, parts, copies, outs, sc, ordered, swapped):
    members, part, width = parts.shape

    def product(rows):
        if flat:
            return nt(jnp.concatenate([y[z, rows, :] for z in range(NZ)], axis=1), w[...])
        value = nt(y[0, rows, :], w[0])
        for z in range(1, NZ):
            value += nt(y[z, rows, :], w[z])
        return value

    together = None if part % 16 == 0 else product(slice(None))
    started = []
    for j in range(members):
        if together is not None:
            value = together[j * part : (j + 1) * part]
        else:
            value = product(pl.ds(pl.multiple_of((sc[1] ^ j) * part, 16) if ordered else j * part, part))
        block = width // swapped if swapped else width
        for k in range(width // block):
            to = k ^ 1 if swapped else k
            parts[j, :, to * block : (to + 1) * block] = value[:, k * block : (k + 1) * block].astype(BF16)
        goal = outs[j]
        started.append((j, goal))
        if together is None or not ordered:
            started[-1] = copies.start(parts.at[j], goal)
    if together is not None and ordered:
        started = [copies.start(parts.at[sc[1] ^ j], goal) for j, goal in started]
    return started


def gate(scalars, name, after, hold):
    def body(sc, ins, outs, scratch, copies):
        pass

    return manual(body, name, scalars, [], [], [], 1, after, hold)


def add(scalars, arrays, after=(), hold=()):
    out, *held = add_groups(scalars, [arrays], False, after, hold)
    return (out, *held)


def add_groups(scalars, groups, apart, after=(), hold=()):
    dims, terms = groups[0][0].shape, len(groups[0])
    three = len(dims) == 3
    count = dims[0] if three else 3 if dims[0] % 48 == 0 else 1
    rows = 0 if three else dims[0] // count
    place = (lambda ref, i: ref.at[i]) if three else (lambda ref, i: ref.at[pl.ds(i * rows, rows), :])
    at = (lambda i: i) if three else (lambda i: slice(i * rows, (i + 1) * rows))

    def body(sc, ins, outs, scratch, copies):
        arriving = []
        for g in range(len(groups)):
            for i in range(count):
                arriving.append([
                    copies.start(place(ins[g * terms + t], i), place(scratch[g * terms + t], i)) for t in range(terms)
                ])
        leaving = []
        for g in range(len(groups)):
            total_ref = scratch[len(groups) * terms + g]
            for i in range(count):
                wait(arriving[g * count + i])
                total = scratch[g * terms][at(i)].astype(F32)
                for t in range(1, terms):
                    total += scratch[g * terms + t][at(i)].astype(F32)
                total_ref[at(i)] = total.astype(BF16)
                goal = outs[g * count + i] if apart else place(outs[g], i)
                leaving.append(copies.start(place(total_ref, i), goal))
        wait(leaving)

    made = [shape(dims[1:], BF16)] * (count * len(groups)) if apart else [shape(dims, BF16)] * len(groups)
    return manual(
        body, "add", scalars, [a for g in groups for a in g], made, [vmem(dims)] * ((terms + 1) * len(groups)),
        (terms + 1) * count * len(groups), after, hold,
    )


def project(scalars, rows, weights, name, after=(), hold=()):
    count, cols = rows.count, weights.cols
    half = SEQ // 2
    chunks = 2 if count % 32 == 0 else 1

    def body(sc, ins, outs, scratch, copies):
        x, w, y = scratch
        row_refs, weight_refs = take(ins, len(rows.args))
        started = rows.load(copies, row_refs, x, sc)
        by_slot = weights.load(copies, weight_refs, w, sc)
        wait(started)
        step, leaving = slots_at_once(cols), []
        for c in range(chunks):
            here = pl.ds(c * (count // chunks), count // chunks)
            for z in range(0, NZ, step):
                if c == 0:
                    for s in range(z, z + step):
                        wait(by_slot[s])
                value = nn(x[here, :], weights.slots(w, z, step))
                for s in range(step):
                    y[z + s, here, :] = value[:, s * cols : (s + 1) * cols].astype(BF16)
                    leaving.append(copies.start(y.at[z + s, here, :], outs[0].at[z + s, here, :]))
        for z in range(1, NZ, 2):
            leaving.append(copies.start(y.at[z, split_rows(sc), :], outs[1].at[z // 2]))
        wait(leaving)

    return manual(
        body, name, scalars, rows.args + weights.args,
        [shape((NZ, count, cols), BF16), shape((NZ // 2, half, cols), BF16)],
        [vmem((count, rows.width)), weights.scratch, vmem((NZ, count, cols))],
        rows.copies + weights.copies + NZ * chunks + NZ // 2, after, hold,
    )


def project_back(scalars, slots, weights, nodes, name, after=(), hold=()):
    count, cols, width = slots.count, weights.cols, weights.depth

    def body(sc, ins, outs, scratch, copies):
        y, w, parts = scratch
        slot_refs, weight_refs = take(ins, len(slots.args))
        for started in slots.load(copies, slot_refs, y, sc) + weights.load(copies, weight_refs, w, sc):
            wait(started)
        wait(multiply_parts(y, w, weights.flat, parts, copies, outs, sc, True, 0))

    return manual(
        body, name, scalars, slots.args + weights.args, [shape((count // nodes, width), BF16)] * nodes,
        [vmem((NZ, count, cols)), weights.scratch, vmem((nodes, count // nodes, width))],
        slots.copies + weights.copies + nodes, after, hold,
    )


def weight_grads(scalars, products, dps, out_shape, goal, side, name, after=(), hold=()):
    counts = [sum(g.count for g in rows) for rows, _ in products]
    widths = [slots[0].cols for _, slots in products]
    width = products[0][0][0].width
    block = width // dps
    parts = 1 if side else len(products)
    cols = sum(widths) if side else widths[0]
    step = max(slots_at_once(c) for c in widths)
    args, scratch, copies_needed = [], [vmem((parts, NZ, width, cols))], parts * NZ * dps
    for (rows, slots), count, own in zip(products, counts, widths):
        args += [a for g in rows + slots for a in g.args]
        scratch += [vmem((count, width)), vmem((NZ, count, own)), vmem((width, count))]
        copies_needed += sum(g.copies for g in rows + slots)

    def body(sc, ins, outs, scratch, copies):
        result = scratch[0]
        loaded = []
        for i, (rows, slots) in enumerate(products):
            x, y, flipped = scratch[1 + 3 * i : 4 + 3 * i]
            started, at = [], 0
            for g in rows:
                refs, ins = take(ins, len(g.args))
                started += g.load(copies, refs, x, sc, at)
                at += g.count
            by_slot, at = [[] for _ in range(NZ)], 0
            for g in slots:
                refs, ins = take(ins, len(g.args))
                for z, some in enumerate(g.load(copies, refs, y, sc, at)):
                    by_slot[z] += some
                at += g.count
            loaded.append((started, by_slot))
        leaving = []

        def send(part, z, ks=range(dps)):
            for k in ks:
                rows = pl.ds(k * block, block)
                leaving.append(copies.start(result.at[part, z, rows, :], goal(sc, outs, part, k, z)))

        def multiply(i, z, at, part, ks=range(dps)):
            y, flipped, own = scratch[2 + 3 * i], scratch[3 + 3 * i], widths[i]
            here = slice(ks[0] * block, (ks[-1] + 1) * block)
            if ks[0] == 0:
                for s in range(z, z + step):
                    wait(loaded[i][1][s])
            whole_y = jnp.concatenate([y[z + s] for s in range(step)], axis=1) if step > 1 else y[z]
            value = nn(flipped[here, :], whole_y)
            for s in range(step):
                result[part, z + s, here, at : at + own] = value[:, s * own : (s + 1) * own].astype(BF16)

        def flip(i):
            wait(loaded[i][0])
            scratch[3 + 3 * i][...] = scratch[1 + 3 * i][...].T

        if side:
            for i in range(len(products)):
                flip(i)
            for ks in (range(dps // 2), range(dps // 2, dps)):
                for z in range(0, NZ, step):
                    for i in range(len(products)):
                        multiply(i, z, sum(widths[:i]), 0, ks)
                    for s in range(z, z + step):
                        send(0, s, ks)
        else:
            for i in range(len(products)):
                flip(i)
                for z in range(0, NZ, step):
                    multiply(i, z, 0, i)
                    for s in range(z, z + step):
                        send(i, s)
        wait(leaving)

    return list(manual(body, name, scalars, args, out_shape, scratch, copies_needed, after, hold))


def feed_forward(scalars, rows, weights, bias_row, name, after=(), hold=()):
    count, cols = rows.count, weights.cols

    def body(sc, ins, outs, scratch, copies):
        x, w, b, hidden, slope = scratch
        row_refs, weight_refs = take(ins, len(rows.args))
        started = rows.load(copies, row_refs, x, sc)
        for z in range(NZ):
            started.append(copies.start(weight_refs[0].at[sc[3] ^ z, pl.ds(bias_row, BIAS_ROWS), :], b.at[z]))
        by_slot = weights.load(copies, weight_refs, w, sc)
        wait(started)
        leaving = []
        step = slots_at_once(cols)
        for z in range(0, NZ, step):
            for s in range(z, z + step):
                wait(by_slot[s])
            value = nn(x[...], weights.slots(w, z, step))
            for s in range(step):
                terms = b[z + s].astype(F32)
                u = value[:, s * cols : (s + 1) * cols] + (terms[0:1] + terms[1:2] + terms[2:3])
                cdf = 0.5 + 0.5 * lax.erf(u * math.sqrt(0.5))
                hidden[z + s] = (u * cdf).astype(BF16)
                slope[z + s] = (cdf + u * (jnp.exp(-0.5 * u * u) * (1.0 / math.sqrt(2.0 * math.pi)))).astype(BF16)
                leaving.append(copies.start(hidden.at[z + s], outs[0].at[z + s]))
                leaving.append(copies.start(slope.at[z + s], outs[1].at[z + s]))
        wait(leaving)

    return manual(
        body, name, scalars, rows.args + weights.args, [shape((NZ, count, cols), BF16)] * 2,
        [vmem((count, rows.width)), weights.scratch, vmem((NZ, BIAS_ROWS, cols)), vmem((NZ, count, cols)), vmem((NZ, count, cols))],
        rows.copies + NZ + weights.copies + 2 * NZ, after, hold,
    )


def feed_back(scalars, rows, slope, down, up, nodes, swapped, name, after=(), hold=()):
    count, cols, width = rows.count, down.cols, rows.width

    def body(sc, ins, outs, scratch, copies):
        x, wd, wu, steep, du, gb, parts = scratch
        row_refs, ins = take(ins, len(rows.args))
        slope_ref, ins = ins[0], ins[1:]
        down_refs, up_refs = take(ins, len(down.args))
        started = rows.load(copies, row_refs, x, sc)
        down_slots = down.load(copies, down_refs, wd, sc)
        steep_slots = [copies.start(slope_ref.at[z], steep.at[z]) for z in range(NZ)]
        up_slots = up.load(copies, up_refs, wu, sc)
        wait(started)
        leaving = []
        step = slots_at_once(cols)
        for z in range(0, NZ, step):
            for s in range(z, z + step):
                wait(down_slots[s])
                steep_slots[s].wait()
            value = nn(x[...], down.slots(wd, z, step))
            for s in range(step):
                grad = value[:, s * cols : (s + 1) * cols] * steep[z + s].astype(F32)
                gb[z + s : z + s + 1, :] = jnp.sum(grad, axis=0, keepdims=True)
                du[z + s] = grad.astype(BF16)
                leaving.append(copies.start(du.at[z + s], outs[0].at[z + s]))
        leaving.append(copies.start(gb, outs[1]))
        for z in range(NZ):
            wait(up_slots[z])
        wait(leaving + multiply_parts(du, wu, True, parts, copies, outs[2:], sc, False, swapped))

    out = manual(
        body, name, scalars, rows.args + [slope] + down.args + up.args,
        [shape((NZ, count, cols), BF16), shape((NZ, cols), F32)] + [shape((count // nodes, width), BF16)] * nodes,
        [vmem((count, width)), down.scratch, up.scratch, vmem((NZ, count, cols)), vmem((NZ, count, cols)),
         vmem((NZ, cols), F32), vmem((nodes, count // nodes, width))],
        rows.copies + down.copies + up.copies + 2 * NZ + 1 + nodes, after, hold,
    )
    return out[0], out[1], list(out[2 : 2 + nodes]), out[2 + nodes :]


def feed_out(scalars, hidden, down, nodes, swapped, name, after=(), hold=()):
    _, count, cols = hidden.shape
    width = down.depth

    def body(sc, ins, outs, scratch, copies):
        y, w, parts = scratch
        started = [copies.start(ins[0].at[z], y.at[z]) for z in range(NZ)]
        by_slot = down.load(copies, ins[1:], w, sc)
        wait(started)
        for z in range(NZ):
            wait(by_slot[z])
        wait(multiply_parts(y, w, True, parts, copies, outs, sc, False, swapped))

    return manual(
        body, name, scalars, [hidden] + down.args, [shape((count // nodes, width), BF16)] * nodes,
        [vmem((NZ, count, cols)), down.scratch, vmem((nodes, count // nodes, width))],
        NZ + down.copies + nodes, after, hold,
    )


def head_mask(cols, head):
    lane = lax.broadcasted_iota(jnp.int32, (1, cols), 1)
    return (lane >= head * HD) & (lane < (head + 1) * HD)


def by_head_rows(values):
    cols = values.shape[1]
    return jnp.concatenate(
        [jnp.where(head_mask(cols, h), values, 0).astype(BF16) for h in range(cols // HD)], axis=0
    )


def own_columns(stacked, cols):
    count = stacked.shape[0] // (cols // HD)
    total = None
    for h in range(cols // HD):
        piece = jnp.where(head_mask(cols, h), stacked[h * count : (h + 1) * count], 0.0)
        total = piece if total is None else total + piece
    return total


def attend(q, k, v):
    queries = by_head_rows((q * (1.0 / math.sqrt(HD))).astype(BF16))
    scores = nt(k, queries)
    raised = jnp.exp(scores - jnp.max(scores, axis=0, keepdims=True))
    soft = (raised * (1.0 / jnp.sum(raised, axis=0, keepdims=True))).astype(BF16)
    return own_columns(tn(soft, v), q.shape[1]).astype(BF16)


def attend_back(q, k, v, do):
    cols = q.shape[1]
    queries, grads = by_head_rows((q * (1.0 / math.sqrt(HD))).astype(BF16)), by_head_rows(do)
    scores = nt(k, queries)
    raised = jnp.exp(scores - jnp.max(scores, axis=0, keepdims=True))
    soft = raised * (1.0 / jnp.sum(raised, axis=0, keepdims=True))
    dsoft = nt(v, grads)
    dot = jnp.sum(dsoft * soft, axis=0, keepdims=True)
    dscores = (soft * (dsoft - dot)).astype(BF16)
    dv = nn(soft.astype(BF16), grads)
    dk = nn(dscores, queries)
    dq = own_columns(tn(dscores, k), cols) * (1.0 / math.sqrt(HD))
    return dq.astype(BF16), dk.astype(BF16), dv.astype(BF16)


def slots_together(cols):
    return 2 if 2 * cols == 256 else 1


def part_of(pieces, j, cols):
    return jnp.concatenate([p[:, j * cols : (j + 1) * cols] for p in pieces], axis=1) if len(pieces) > 1 else pieces[0][
        :, j * cols : (j + 1) * cols
    ]


def whole_image(sc):
    return pl.ds(pl.multiple_of(sc[2] * (SEQ // 2), 32), SEQ)


def split_rows(sc):
    return pl.ds(pl.multiple_of((1 - sc[2]) * SEQ, 32), SEQ // 2)


def pair_slots(dims, together):
    return pl.BlockSpec((together,) + dims, lambda s, *_: (s, 0, 0))


def own_slots(dims, together):
    return [pl.BlockSpec((1,) + dims, lambda s, *_, i=i: (2 * (s * together + i), 0, 0)) for i in range(together)]


def attend_whole(scalars, qkv, after=(), hold=()):
    slots, count, triple = qkv.shape
    cols = triple // 3
    together = slots_together(cols)

    def body(sc, qkv_ref, o_ref):
        rows = whole_image(sc)
        pieces = [qkv_ref[i, rows, :] for i in range(together)]
        mixed = attend(*(part_of(pieces, j, cols) for j in range(3)))
        for i in range(together):
            o_ref[i] = mixed[:, i * cols : (i + 1) * cols]

    return call(
        body, "attend_whole", (slots // together,), scalars, [pair_slots((count, triple), together)],
        pair_slots((SEQ, cols), together), shape((slots, SEQ, cols), BF16), [qkv],
        after=after, hold=hold, nbytes=2 * slots * count * 4 * cols,
    )


def attend_split(scalars, qkv, partner, after=(), hold=()):
    slots, half, triple = partner.shape
    count = qkv.shape[1]
    cols = triple // 3
    together = slots_together(cols)

    def body(sc, *refs):
        qkv_refs, (partner_ref, mine_ref, theirs_ref, joined) = refs[:together], refs[together:]
        for i, ref in enumerate(qkv_refs):
            joined[i, :half, :] = ref[0, split_rows(sc), :]
            joined[i, half:, :] = partner_ref[i]
        pieces = [joined[i] for i in range(together)]
        mixed = attend(*(part_of(pieces, j, cols) for j in range(3)))
        for i in range(together):
            mine_ref[i] = mixed[:half, i * cols : (i + 1) * cols]
            theirs_ref[i] = mixed[half:, i * cols : (i + 1) * cols]

    return call(
        body, "attend_split", (slots // together,), scalars,
        own_slots((count, triple), together) + [pair_slots((half, triple), together)],
        [pair_slots((half, cols), together)] * 2, [shape((slots, half, cols), BF16)] * 2, [qkv] * together + [partner],
        scratch=[vmem((together, 2 * half, triple))], after=after, hold=hold, nbytes=2 * slots * count * 4 * cols,
    )


def attend_whole_back(scalars, qkv, do, after=(), hold=()):
    slots, count, triple = qkv.shape
    cols = triple // 3
    together = slots_together(cols)

    def body(sc, qkv_ref, do_ref, out_ref):
        rows = whole_image(sc)
        pieces = [qkv_ref[i, rows, :] for i in range(together)]
        do = part_of([do_ref[i, rows, :] for i in range(together)], 0, cols)
        grads = attend_back(*(part_of(pieces, j, cols) for j in range(3)), do)
        for i in range(together):
            for j in range(3):
                out_ref[i, :, j * cols : (j + 1) * cols] = grads[j][:, i * cols : (i + 1) * cols]

    return call(
        body, "attend_whole_back", (slots // together,), scalars,
        [pair_slots((count, triple), together), pair_slots((count, cols), together)],
        pair_slots((SEQ, triple), together), shape((slots, SEQ, triple), BF16), [qkv, do],
        after=after, hold=hold, nbytes=2 * slots * count * 7 * cols,
    )


def attend_split_back(scalars, qkv, partner, do, do_partner, after=(), hold=()):
    slots, half, triple = partner.shape
    count = qkv.shape[1]
    cols = triple // 3
    together = slots_together(cols)

    def body(sc, *refs):
        qkv_refs, do_refs = refs[:together], refs[together : 2 * together]
        partner_ref, do_partner_ref, mine_ref, theirs_ref, joined, joined_do = refs[2 * together :]
        for i in range(together):
            joined[i, :half, :] = qkv_refs[i][0, split_rows(sc), :]
            joined[i, half:, :] = partner_ref[i]
            joined_do[i, :half, :] = do_refs[i][0, split_rows(sc), :]
            joined_do[i, half:, :] = do_partner_ref[i]
        pieces = [joined[i] for i in range(together)]
        do = part_of([joined_do[i] for i in range(together)], 0, cols)
        grads = attend_back(*(part_of(pieces, j, cols) for j in range(3)), do)
        for i in range(together):
            for j in range(3):
                mine_ref[i, :, j * cols : (j + 1) * cols] = grads[j][:half, i * cols : (i + 1) * cols]
                theirs_ref[i, :, j * cols : (j + 1) * cols] = grads[j][half:, i * cols : (i + 1) * cols]

    return call(
        body, "attend_split_back", (slots // together,), scalars,
        own_slots((count, triple), together) + own_slots((count, cols), together)
        + [pair_slots((half, triple), together), pair_slots((half, cols), together)],
        [pair_slots((half, triple), together)] * 2, [shape((slots, half, triple), BF16)] * 2,
        [qkv] * together + [do] * together + [partner, do_partner],
        scratch=[vmem((together, 2 * half, triple)), vmem((together, 2 * half, cols))],
        after=after, hold=hold, nbytes=2 * slots * count * 7 * cols,
    )


def by_rows(body, name, scalars, kinds, out_kinds, out_shape, args, after=(), hold=()):
    count = next(a for a, kind in zip(args, kinds) if kind == "r").shape[0]
    width = args[0].shape[1]
    steps = 3 if count % 48 == 0 else 1
    rows = count // steps
    made = len(out_shape)
    total = sum(steps if kind == "r" else 1 for kind in kinds + out_kinds)

    def part(ref, i):
        return ref.at[pl.ds(i * rows, rows), :]

    def run(sc, ins, outs, scratch, copies):
        here, results, work = scratch[: len(ins)], scratch[len(ins) : len(ins) + made], scratch[-1]
        first = [copies.start(r, h) for r, h, kind in zip(ins, here, kinds) if kind == "w"]
        arriving = [
            [copies.start(part(r, i), part(h, i)) for r, h, kind in zip(ins, here, kinds) if kind == "r"]
            for i in range(steps)
        ]
        wait(first)
        leaving = []
        for i in range(steps):
            wait(arriving[i])
            body(
                i, sc, [part(h, i) if kind == "r" else h for h, kind in zip(here, kinds)],
                [part(h, i) if kind == "r" else h for h, kind in zip(results, out_kinds)], work,
            )
            leaving += [copies.start(part(h, i), part(o, i)) for h, o, kind in zip(results, outs, out_kinds) if kind == "r"]
        leaving += [copies.start(h, o) for h, o, kind in zip(results, outs, out_kinds) if kind == "w"]
        wait(leaving)

    scratch = [vmem(a.shape, a.dtype) for a in list(args) + list(out_shape)] + [vmem((rows, width), F32)]
    return manual(run, name, scalars, args, out_shape, scratch, total, after, hold)


def to_relative(sc, scratch, out_ref, block):
    dps = scratch.shape[1] // block
    for k in range(dps):
        out_ref[:, k * block : (k + 1) * block] = scratch[
            :, pl.ds(pl.multiple_of((sc[0] ^ k) * block, block), block)
        ].astype(out_ref.dtype)


def from_relative(sc, refs, scratch, block):
    dps = scratch.shape[1] // block
    for k in range(dps):
        here = slice(k * block, (k + 1) * block)
        piece = refs[0][:, here].astype(F32)
        for ref in refs[1:]:
            piece += ref[:, here].astype(F32)
        scratch[:, pl.ds(pl.multiple_of((sc[0] ^ k) * block, block), block)] = piece


def normed(rows):
    centred = rows - jnp.mean(rows, axis=-1, keepdims=True)
    inverse = lax.rsqrt(jnp.mean(centred * centred, axis=-1, keepdims=True) + 1e-06)
    return centred * inverse, inverse


def norm_back(hat, inverse, grad, gain):
    scaled = grad * gain
    return inverse * (
        scaled - jnp.mean(scaled, axis=-1, keepdims=True) - hat * jnp.mean(scaled * hat, axis=-1, keepdims=True)
    )


def column(values):
    return jnp.sum(values, axis=0, keepdims=True)


def add_rows(step, ref, values):
    ref[...] = values if step == 0 else ref[...] + values


def first_norm(scalars, tokens, cotangent, vectors, dps, after=(), hold=()):
    count, width = tokens.shape
    block = width // dps

    def body(step, sc, ins, outs, work):
        x_ref, cot_ref, vec_ref = ins
        hat, _ = normed(x_ref[...])
        work[...] = hat * vec_ref[0:1] + vec_ref[1:2]
        to_relative(sc, work, outs[0], block)
        work[...] = cot_ref[...]
        to_relative(sc, work, outs[1], block)

    return by_rows(
        body, "first_norm", scalars, "rrw", "rr", [shape((count, width), BF16)] * 2, [tokens, cotangent, vectors], after, hold
    )


def second_norm(scalars, tokens, parts, vectors, dps, after=(), hold=()):
    count, width = tokens.shape
    block = width // dps

    def body(step, sc, ins, outs, work):
        x_ref, vec_ref, *part_refs = ins
        from_relative(sc, part_refs, work, block)
        h = x_ref[...] + work[...] + vec_ref[4:5]
        outs[0][...] = h
        hat, _ = normed(h)
        work[...] = hat * vec_ref[2:3] + vec_ref[3:4]
        to_relative(sc, work, outs[1], block)

    return by_rows(
        body, "second_norm", scalars, "rw" + "r" * len(parts), "rr",
        [shape((count, width), F32), shape((count, width), BF16)], [tokens, vectors] + list(parts), after, hold,
    )


def layer_output(scalars, middle, parts, vectors, dps, after=(), hold=()):
    count, width = middle.shape
    block = width // dps

    def body(step, sc, ins, outs, work):
        h_ref, vec_ref, *part_refs = ins
        from_relative(sc, part_refs, work, block)
        outs[0][...] = h_ref[...] + work[...] + vec_ref[5:6]

    return by_rows(
        body, "layer_output", scalars, "rw" + "r" * len(parts), "r", [shape((count, width), F32)],
        [middle, vectors] + list(parts), after, hold,
    )


def second_norm_back(scalars, middle, cotangent, parts, vectors, dps, after=(), hold=()):
    count, width = middle.shape
    block = width // dps

    def body(step, sc, ins, outs, work):
        h_ref, cot_ref, vec_ref, *part_refs = ins
        from_relative(sc, part_refs, work, block)
        dc = work[...]
        hat, inverse = normed(h_ref[...])
        cot = cot_ref[...]
        dh = cot + norm_back(hat, inverse, dc, vec_ref[2:3])
        outs[0][...] = dh
        work[...] = dh
        to_relative(sc, work, outs[1], block)
        add_rows(step, outs[2], jnp.concatenate([column(dc * hat), column(dc), column(dh), column(cot)], axis=0))

    return by_rows(
        body, "second_norm_back", scalars, "rrw" + "r" * len(parts), "rrw",
        [shape((count, width), F32), shape((count, width), BF16), shape((4, width), F32)],
        [middle, cotangent, vectors] + list(parts), after, hold,
    )


def first_norm_back(scalars, tokens, middle_grad, parts, vectors, dps, after=(), hold=()):
    count, width = tokens.shape
    block = width // dps

    def body(step, sc, ins, outs, work):
        x_ref, dh_ref, vec_ref, *part_refs = ins
        from_relative(sc, part_refs, work, block)
        da = work[...]
        hat, inverse = normed(x_ref[...])
        outs[0][...] = dh_ref[...] + norm_back(hat, inverse, da, vec_ref[0:1])
        add_rows(step, outs[1], jnp.concatenate([column(da * hat), column(da)], axis=0))

    return by_rows(
        body, "first_norm_back", scalars, "rrw" + "r" * len(parts), "rw",
        [shape((count, width), F32), shape((2, width), F32)], [tokens, middle_grad, vectors] + list(parts), after, hold,
    )


def adam_step(weight, gradient, first, second, rate, decay):
    first = 0.9 * first + 0.1 * gradient
    second = 0.999 * second + 0.001 * gradient * gradient
    first_fix = 1.0 - 0.9**STEP
    second_fix = 1.0 - 0.999**STEP
    update = first / first_fix / (jnp.sqrt(second / second_fix) + 1e-08) + decay * weight
    return (gradient, first, second, weight - rate * update)


def by_part(columns, heads):
    return jnp.concatenate([columns[:, (h * 3 + c) * HD : (h * 3 + c + 1) * HD] for c in range(3) for h in range(heads)], axis=1)


def by_head(columns, heads):
    return jnp.concatenate([columns[:, (c * heads + h) * HD : (c * heads + h + 1) * HD] for h in range(heads) for c in range(3)], axis=1)


def plain(body, name, args, out_shape, after=(), hold=()):
    given, extra = len(args), len(after) + len(hold)
    made = len(out_shape)
    nbytes = sum(math.prod(a.shape) * a.dtype.itemsize for a in list(args) + list(out_shape))

    def run(*refs):
        body(*refs[:given], *refs[given + extra : given + extra + made])

    anywhere = pl.BlockSpec(memory_space=pltpu.HBM)
    here = pl.BlockSpec(memory_space=pltpu.VMEM)
    first = given + len(after)
    return pl.pallas_call(
        run, name=name,
        out_shape=list(out_shape) + [shape(h.shape, h.dtype) for h in hold],
        in_specs=[pl.BlockSpec(memory_space=pltpu.SMEM)] + [here] * (given - 1) + [anywhere] * extra,
        out_specs=[here] * made + [anywhere] * len(hold),
        input_output_aliases={first + i: made + i for i in range(len(hold))},
        compiler_params=pltpu.CompilerParams(vmem_limit_bytes=VMEM_LIMIT), cost_estimate=cost(name, nbytes),
    )(*args, *after, *hold)


def weight_pieces(scalars, w_qkv, w_out, w_up, hidden_bias, w_down):
    block, cols = w_up.shape[0], w_up.shape[1] // 2
    heads, triple = w_qkv.shape[1] // (3 * HD), w_qkv.shape[1]

    def body(sc, qkv_ref, out_ref, up_ref, bias_ref, down_ref, attn_ref, my_up_ref, my_down_ref, theirs_ref):
        attn_ref[:, :triple] = by_part(qkv_ref[...], heads).astype(BF16)
        attn_ref[:, triple:] = out_ref[...].T.astype(BF16)
        mine, other = (pl.ds(pl.multiple_of(h * cols, cols), cols) for h in (sc[4], 1 - sc[4]))
        my_up_ref[:block, :] = up_ref[:, mine].astype(BF16)
        my_down_ref[...] = down_ref[mine, :].T.astype(BF16)
        theirs_ref[:block, :] = up_ref[:, other].astype(BF16)
        theirs_ref[block:, :] = down_ref[other, :].T.astype(BF16)
        rest = bias_ref[:, mine]
        row = lax.broadcasted_iota(jnp.int32, (BIAS_ROWS, cols), 0)
        terms = jnp.zeros((BIAS_ROWS, cols), F32)
        for i in range(3):
            term = rest.astype(BF16).astype(F32)
            terms = jnp.where(row == i, term, terms)
            rest = rest - term
        my_up_ref[block:, :] = terms.astype(BF16)

    return plain(
        body, "weight_pieces", [scalars, w_qkv, w_out, w_up, hidden_bias[None, :], w_down],
        [shape((block, triple + w_out.shape[0]), BF16), shape((block + BIAS_ROWS, cols), BF16),
         shape((block, cols), BF16), shape((2 * block, cols), BF16)],
    )


def attn_adam(scalars, near, far, w_qkv, qkv_m, qkv_v, w_out, out_m, out_v, after=()):
    heads, triple = w_qkv.shape[1] // (3 * HD), w_qkv.shape[1]
    block = far.shape[0]

    def body(sc, near_ref, far_ref, *refs):
        total = near_ref[:block, :].astype(F32) + far_ref[...].astype(F32)
        qw, qm, qv, ow, om, ov = (r[...] for r in refs[:6])
        new = adam_step(qw, by_head(total[:, :triple], heads), qm, qv, 0.1, 0.05)
        new += adam_step(ow, total[:, triple:].T, om, ov, 0.2, 0.05)
        for ref, value in zip(refs[6:], new):
            ref[...] = value

    out = plain(
        body, "attn_adam", [scalars, near, far, w_qkv, qkv_m, qkv_v, w_out, out_m, out_v],
        [shape(w_qkv.shape, F32)] * 4 + [shape(w_out.shape, F32)] * 4, after,
    )
    return tuple(out[:4]), tuple(out[4:])


def hidden_adam(scalars, total, far, up, down, after=(), hold=()):
    block, cols = far.shape[0] // 2, far.shape[1]

    def body(sc, total_ref, far_ref, *refs):
        ins, outs = take(refs, 6)
        up_grad, down_grad = outs[0], outs[4]
        for ref, half in ((total_ref, sc[4]), (far_ref, 1 - sc[4])):
            at = pl.ds(pl.multiple_of(half * cols, cols), cols)
            down_grad[at, :] = ref[:block, :].astype(F32).T
            up_grad[:, at] = ref[block : 2 * block, :].astype(F32)
        for (w, m, v), made, rate in ((ins[:3], outs[:4], 0.1), (ins[3:], outs[4:], 0.05)):
            new = adam_step(w[...], made[0][...], m[...], v[...], rate, 0.05)
            for ref, value in zip(made[1:], new[1:]):
                ref[...] = value

    out = plain(
        body, "hidden_adam", [scalars, total, far] + list(up) + list(down),
        [shape(up[0].shape, F32)] * 4 + [shape(down[0].shape, F32)] * 4, after, hold,
    )
    return tuple(out[:4]), tuple(out[4:8]), out[8:]


def solution(mesh):
    dps, tensor = mesh.shape["dp"], mesh.shape["tensor"]
    nodes = tensor // NZ
    devices = dps * tensor

    def snake(columns):
        return [(d, z) for i, d in enumerate(columns) for z in (range(NZ) if i % 2 == 0 else range(NZ - 1, -1, -1))]

    z_groups = [[d * tensor + z * nodes + c for z in range(NZ)] for d in range(dps) for c in range(nodes)]
    half_rings = [
        [d * tensor + z * nodes + c for d, z in snake(range(x, dps, 2))] for x in range(2) for c in range(nodes)
    ]

    def swap(value, flip):
        return lax.ppermute(value, AXES, [(i, i ^ flip) for i in range(devices)])

    def gather_ring(piece, groups):
        return lax.all_gather(piece, AXES, axis=0, axis_index_groups=groups)

    def scatter_ring(total, groups):
        return lax.psum_scatter(total, AXES, scatter_dimension=0, axis_index_groups=groups, tiled=True)[0]

    def by_weight(k):
        return (bin(k).count("1"), k)

    def gather(own, count, unit, low_first):
        bufs = [own] + [None] * (count - 1)
        for k in sorted(range(1, count), key=by_weight):
            last = k & -k if low_first else 1 << (k.bit_length() - 1)
            bufs[k] = swap(bufs[k ^ last], last * unit)
        return bufs

    def plus(left, right):
        return (left.astype(F32) + right.astype(F32)).astype(BF16)

    def add_up(sums):
        total = sums[0].astype(F32)
        for piece in sums[1:]:
            total = total + piece.astype(F32)
        return total.astype(BF16)

    def along_z(piece):
        return [piece] + [swap(piece, j * nodes) for j in range(1, NZ)]

    def relative(own):
        return [own] + [swap(own, j) for j in range(1, nodes)]

    def ordered_rows(parts, member):
        if parts[0].shape[0] % 16 == 0:
            return Rows(parts, True)
        flip = 1
        while len(parts) > 1:
            odd = (member // flip) % 2 == 1
            parts = [
                jnp.where(odd, jnp.concatenate([b, a], axis=0), jnp.concatenate([a, b], axis=0))
                for a, b in zip(parts[0::2], parts[1::2])
            ]
            flip *= 2
        return Rows(parts, True)

    def relative_rows(parts, swapped=0):
        if parts[0].shape[0] % 16:
            parts = [jnp.concatenate(parts, axis=0)]
        return Rows(parts, False, swapped)

    def send_parts(parts):
        return [parts[0]] + [swap(parts[j], j) for j in range(1, nodes)]

    def per_device(
        tokens, cotangent, vectors, vectors_m, vectors_v,
        w_qkv, qkv_m, qkv_v, w_out, out_m, out_v, w_up, up_m, up_v,
        hidden_bias, bias_m, bias_v, w_down, down_m, down_v,
    ):
        dp_index = lax.axis_index("dp")
        tensor_index = lax.axis_index("tensor")
        z_index, member = tensor_index // nodes, tensor_index % nodes
        odd_x = dp_index % 2
        scalars = jnp.stack([dp_index, member, z_index % 2, z_index, odd_x]).astype(jnp.int32)
        block = w_qkv.shape[0]
        triple, width = w_qkv.shape[1], w_out.shape[0]
        hidden_here = w_up.shape[1] // 2

        attn_own, my_up, my_down, theirs = weight_pieces(scalars, w_qkv, w_out, w_up, hidden_bias, w_down)
        attn_z = along_z(attn_own)
        arrived = swap(theirs, tensor)
        lower, upper = jnp.stack(attn_z[:2]), jnp.stack(attn_z[2:])
        up_piece = jnp.concatenate([my_up, arrived[:block]], axis=0)
        down_piece = jnp.concatenate([my_down, arrived[block:]], axis=0)
        early = attn_own
        if dps == 4:
            lowers, uppers = [swap(lower, tensor), swap(lower, 2 * tensor)], [swap(upper, tensor), swap(upper, 2 * tensor)]
            *lowers, up_piece, down_piece = gate(
                scalars, "gate_lower", [upper], lowers + [up_piece, down_piece]
            )
            early = up_piece
        a_own, g_own = first_norm(scalars, tokens, cotangent, vectors, dps, after=[early])
        a_parts = relative(a_own)
        if dps == 4:
            lowers[0], uppers[1], g_own = gate(
                scalars, "gate_gather", [lowers[1], uppers[0], a_own], [lowers[0], uppers[1], g_own]
            )
            lowers = [lower] + lowers + [swap(lowers[0], 2 * tensor)]
            uppers = [upper] + uppers + [swap(uppers[1], tensor)]
        else:
            lowers, uppers = gather(lower, dps, tensor, False), gather(upper, dps, tensor, True)
        up_z = gather_ring(up_piece, z_groups)
        halves = [(0, [(2 * k + z // 2, z % 2) for z in range(NZ)]) for k in range(dps)]
        attn_w = [half for pair in zip(lowers, uppers) for half in pair]
        qkv_w = Weights(attn_w, halves, block, 0, triple)
        out_w = Weights(attn_w, halves, block, triple, width)

        a_rows = ordered_rows(a_parts, member)
        qkv, qkv_theirs = project(scalars, a_rows, qkv_w, "qkv")
        qkv_partner = swap(qkv_theirs, nodes)
        g_far = swap(g_own, tensor)
        (up_z,) = gate(scalars, "gate_up", [qkv], [up_z])
        up_w = Weights(
            gather(up_z, dps // 2, 2 * tensor, False),
            [(k % 2 * (block + BIAS_ROWS), [(k // 2, lambda sc, z=z: sc[3] ^ z) for z in range(NZ)]) for k in range(dps)],
            block, 0, hidden_here,
        )
        mixed = attend_whole(scalars, qkv, after=[up_z])
        mixed_mine, mixed_theirs, down_piece = attend_split(scalars, qkv, qkv_partner, after=[mixed], hold=[down_piece])
        down_w = Weights(
            [gather_ring(down_piece, half_rings)],
            [(k % 2 * block, [(0, lambda sc, k=k, z=z: hidden_place(sc, k, z)) for z in range(NZ)]) for k in range(dps)],
            block, 0, hidden_here,
        )
        mixed = SplitSlots(mixed, mixed_mine, swap(mixed_theirs, nodes))
        *attn_parts, g_far = project_back(
            scalars, mixed, out_w, nodes, "attn_out", after=up_w.args[1:], hold=[g_far]
        )
        middle, c_own = second_norm(scalars, tokens, send_parts(attn_parts), vectors, dps)

        c_far = swap(c_own, tensor)
        g_rows, g_far = relative_rows(relative(g_own)), relative_rows(relative(g_far), dps)
        c_rows = relative_rows(relative(c_own))
        hidden, slope = feed_forward(scalars, c_rows, up_w, block, "feed_forward")
        du, bias_near, dc_near, _ = feed_back(
            scalars, g_rows, slope, down_w, up_w, nodes, 0, "feed_back", after=[hidden]
        )
        dc_near = send_parts(dc_near)
        (c_far,) = gate(scalars, "gate_rows", [du], [c_far])
        c_far = relative_rows(relative(c_far), dps)
        hidden_far, slope_far = feed_forward(scalars, c_far, up_w, block, "feed_forward_far", after=[du])
        du_far, bias_far, dc_far, _ = feed_back(
            scalars, g_far, slope_far, down_w, up_w, nodes, dps, "feed_back_far", after=[hidden_far] + dc_near[1:]
        )
        (dc_sum,) = add(scalars, send_parts(dc_far), after=[du_far])
        dc_arrived = swap(dc_sum, tensor)

        out_far = feed_out(scalars, hidden_far, down_w, nodes, dps, "feed_out_far", after=[dc_sum])

        def hidden_goal(sc, outs, part, k, z):
            return outs[0].at[hidden_place(sc, k, z), pl.ds((2 * (k % 2) + part) * block, block), :]

        (hidden_part,) = weight_grads(
            scalars,
            [([g_rows, g_far], [Slots(hidden), Slots(hidden_far)]), ([c_rows, c_far], [Slots(du), Slots(du_far)])],
            dps, [shape((NZ * dps // 2, 4 * block, hidden_here), BF16)],
            hidden_goal, False, "hidden_grad", after=[out_far[0]],
        )
        hidden_total = scatter_ring(hidden_part, half_rings)
        middle_grad, e_own, sums_two = second_norm_back(
            scalars, middle, cotangent, dc_near + [dc_arrived], vectors, dps, after=[hidden_part]
        )
        out_far = send_parts(out_far)

        e_rows = ordered_rows(relative(e_own), member)
        dmixed, dmixed_theirs = project(scalars, e_rows, out_w, "mixed_grad", after=out_far[1:])
        dmixed_partner = swap(dmixed_theirs, nodes)
        *out_near, out_far[0] = feed_out(
            scalars, hidden, down_w, nodes, 0, "feed_out", after=[dmixed], hold=[out_far[0]]
        )
        out_arrived = swap(add_up(out_far), tensor)
        dqkv_mine, dqkv_theirs = attend_split_back(
            scalars, qkv, qkv_partner, dmixed, dmixed_partner, after=[out_near[0]]
        )
        dqkv_whole = attend_whole_back(scalars, qkv, dmixed, after=[dqkv_mine])
        dqkv = SplitSlots(dqkv_whole, dqkv_mine, swap(dqkv_theirs, nodes))

        def attn_goal(first, cols):
            def goal(sc, outs, part, k, z):
                place = outs[0].at[hidden_place(sc, k, z), pl.ds((k % 2) * block, block), :]
                return place if cols == triple + width else place.at[:, pl.ds(first, cols)]

            return goal

        attn_shape = [shape((NZ * dps // 2, 2 * block, triple + width), BF16)]
        if triple % 128 == 0 and width % 128 == 0:
            out_part = weight_grads(
                scalars, [([e_rows], [mixed])], dps, attn_shape, attn_goal(triple, width), True, "out_grad",
                after=[dqkv_whole],
            )
            (attn_part,) = weight_grads(
                scalars, [([a_rows], [dqkv])], dps, [], attn_goal(0, triple), True, "attn_grad",
                after=[out_arrived], hold=out_part,
            )
        else:
            (attn_part,) = weight_grads(
                scalars, [([a_rows], [dqkv]), ([e_rows], [mixed])], dps, attn_shape, attn_goal(0, triple + width), True,
                "attn_grad", after=[out_arrived],
            )
        da_parts = send_parts(project_back(scalars, dqkv, qkv_w, nodes, "first_back", after=[attn_part]))
        input_grad, sums_one, hidden_total = first_norm_back(
            scalars, tokens, middle_grad, da_parts, vectors, dps, hold=[hidden_total]
        )
        attn_part = scatter_ring(attn_part, half_rings)

        here = (jnp.arange(nodes)[:, None] == member) & (jnp.arange(2)[None, :] == odd_x)
        own_slot_of = (jnp.arange(NZ)[:, None] ^ z_index) == jnp.arange(NZ)[None, :]
        bias_here = jnp.sum(jnp.where(own_slot_of[:, :, None], (bias_near + bias_far)[None], 0.0), axis=1)
        bias_part = jnp.where(here[None, :, :, None], bias_here[:, None, None, :], 0.0)
        rows_two = sums_one.shape[0] + sums_two.shape[0]
        value = jnp.concatenate([sums_one, sums_two, bias_part.reshape(-1, sums_two.shape[1])], axis=0)
        for flip in [1 << i for i in range(devices.bit_length() - 1)]:
            value = value + swap(value, flip)
        all_sums = value
        (output,) = layer_output(scalars, middle, send_parts(out_near) + [out_arrived], vectors, dps, after=[input_grad])
        far = swap(hidden_total[2 * block :], tensor)
        up_res, down_res, _ = hidden_adam(
            scalars, hidden_total, far, (w_up, up_m, up_v), (w_down, down_m, down_v), after=[output]
        )
        attn_far = swap(attn_part[block:], tensor)
        qkv_res, out_res = attn_adam(scalars, attn_part, attn_far, w_qkv, qkv_m, qkv_v, w_out, out_m, out_v, after=[up_res[0]])
        vector_total = all_sums[:rows_two]
        bias_total = lax.dynamic_slice_in_dim(
            all_sums[rows_two:].reshape(-1), tensor_index * 2 * hidden_here, 2 * hidden_here, 0
        )

        vec_res = adam_step(vectors, vector_total, vectors_m, vectors_v, 0.3, 0.0)
        bias_res = adam_step(hidden_bias, bias_total, bias_m, bias_v, 0.3, 0.0)
        return (output, input_grad) + vec_res + qkv_res + out_res + up_res + bias_res + down_res

    rows, both = P(AXES, None), P("dp", "tensor")
    turned = P("tensor", "dp")
    in_specs = (
        (rows,) * 2 + (P(),) * 3 + (both,) * 3 + (turned,) * 3 + (both,) * 3 + (P("tensor"),) * 3 + (turned,) * 3
    )
    out_specs = (
        (rows,) * 2 + (P(),) * 4 + (both,) * 4 + (turned,) * 4 + (both,) * 4 + (P("tensor"),) * 4 + (turned,) * 4
    )
    return jax.shard_map(per_device, mesh=mesh, in_specs=in_specs, out_specs=out_specs, check_vma=False)
```

```python
import math

import jax
import jax.numpy as jnp
from jax import lax
from jax.experimental import pallas as pl
from jax.experimental.pallas import tpu as pltpu
from jax.sharding import PartitionSpec as P

HD = 64
SEQ = 576
STEP = 10
NZ = 4
BIAS_ROWS = 16
AXES = ("dp", "tensor")
F32 = jnp.float32
BF16 = jnp.bfloat16
VMEM_LIMIT = 63 * 1024 * 1024
TIMES = {"gate_lower": 1, "gate_gather": 1000, "attn_out": 1000, "feed_out_far": 1000, "feed_out": 5, "attend_whole_back": 20, "first_back": 1000}


def nn(left, right):
    return jnp.dot(left, right, preferred_element_type=F32)


def nt(left, right):
    return lax.dot_general(left, right, (((1,), (1,)), ((), ())), preferred_element_type=F32)


def tn(left, right):
    return lax.dot_general(left, right, (((0,), (0,)), ((), ())), preferred_element_type=F32)


def cost(name, nbytes):
    return pl.CostEstimate(flops=int(5e8 * TIMES.get(name, 0)), bytes_accessed=int(nbytes), transcendentals=0)


def call(body, name, grid, scalars, in_specs, out_specs, out_shape, args, scratch=(), after=(), hold=(), nbytes=0):
    given, extra = len(args), len(after) + len(hold)
    single = not isinstance(out_shape, (list, tuple))
    out_specs, out_shape = ([out_specs], [out_shape]) if single else (list(out_specs), list(out_shape))
    made = len(out_shape)

    def run(sc, *refs):
        rest = refs[given + extra :]
        body(sc, *refs[:given], *rest[:made], *rest[made + len(hold) :])

    anywhere = pl.BlockSpec(memory_space=pltpu.HBM)
    first = 1 + given + len(after)
    out = pl.pallas_call(
        run,
        name=name,
        grid_spec=pltpu.PrefetchScalarGridSpec(
            num_scalar_prefetch=1,
            grid=grid,
            in_specs=list(in_specs) + [anywhere] * extra,
            out_specs=out_specs + [anywhere] * len(hold),
            scratch_shapes=list(scratch),
        ),
        out_shape=out_shape + [shape(h.shape, h.dtype) for h in hold],
        input_output_aliases={first + i: made + i for i in range(len(hold))},
        compiler_params=pltpu.CompilerParams(vmem_limit_bytes=VMEM_LIMIT),
        cost_estimate=cost(name, nbytes),
    )(scalars, *args, *after, *hold)
    return out[0] if single and not hold else tuple(out)


def shape(dims, dtype):
    return jax.ShapeDtypeStruct(dims, dtype)


def whole(dims):
    return pl.BlockSpec(dims, lambda *_: (0,) * len(dims))


def slot(dims):
    return pl.BlockSpec((1,) + dims, lambda s, *_: (s, 0, 0))


def lower_slots(dims):
    return pl.BlockSpec((1,) + dims, lambda s, *_: (jnp.minimum(s, NZ // 2 - 1), 0, 0))


def upper_slots(dims):
    return pl.BlockSpec((1,) + dims, lambda s, *_: (jnp.maximum(s - NZ // 2, 0), 0, 0))


class Copies:
    def __init__(self, sems):
        self.sems, self.used = sems, 0

    def start(self, source, target):
        copy = pltpu.make_async_copy(source, target, self.sems.at[self.used])
        self.used += 1
        copy.start()
        return copy


def wait(copies):
    for copy in copies:
        copy.wait()


def manual(body, name, scalars, args, out_shape, scratch, copies, after=(), hold=()):
    given, extra = len(args), len(after) + len(hold)
    nbytes = sum(math.prod(a.shape) * a.dtype.itemsize for a in list(args) + list(out_shape))

    def run(sc, *refs):
        rest = refs[given + extra :]
        made = len(out_shape) + len(hold)
        body(sc, refs[:given], rest[:made], rest[made:-1], Copies(rest[-1]))

    anywhere = pl.BlockSpec(memory_space=pltpu.HBM)
    first = 1 + given + len(after)
    return pl.pallas_call(
        run,
        name=name,
        in_specs=[pl.BlockSpec(memory_space=pltpu.SMEM)] + [anywhere] * (given + extra),
        out_specs=[anywhere] * (len(out_shape) + len(hold)),
        out_shape=list(out_shape) + [shape(h.shape, h.dtype) for h in hold],
        input_output_aliases={first + i: len(out_shape) + i for i in range(len(hold))},
        scratch_shapes=list(scratch) + [pltpu.SemaphoreType.DMA((copies,))],
        compiler_params=pltpu.CompilerParams(vmem_limit_bytes=VMEM_LIMIT),
        cost_estimate=cost(name, nbytes),
    )(scalars, *args, *after, *hold)


def vmem(dims, dtype=BF16):
    return pltpu.VMEM(dims, dtype)


class Weights:
    def __init__(self, arrays, blocks, block, col, cols):
        full = arrays[0].shape[2]
        if (col % 128 or cols % 128) and cols != full:
            arrays, col, full = [a[:, :, col : col + cols] for a in arrays], 0, cols
        self.args, self.blocks, self.block = list(arrays), blocks, block
        self.col, self.cols, self.full = col, cols, full
        self.depth = block * len(blocks)
        self.flat = cols % 128 == 0
        self.scratch = vmem((self.depth, NZ * cols) if self.flat else (NZ, self.depth, cols))
        self.copies = len(blocks) * NZ

    def load(self, copies, refs, target, sc):
        by_slot = [[] for _ in range(NZ)]
        for z in range(NZ):
            for k, (row, places) in enumerate(self.blocks):
                number, place = places[z]
                source = refs[number].at[place(sc) if callable(place) else place, pl.ds(row, self.block), :]
                if self.cols != self.full:
                    source = source.at[:, pl.ds(self.col, self.cols)]
                rows = pl.ds(k * self.block, self.block)
                goal = target.at[rows, pl.ds(z * self.cols, self.cols)] if self.flat else target.at[z, rows, :]
                by_slot[z].append(copies.start(source, goal))
        return by_slot

    def slots(self, target, first, count):
        if self.flat:
            return target[:, first * self.cols : (first + count) * self.cols]
        assert count == 1
        return target[first]


def slots_at_once(cols):
    for step in (1, 2, 4):
        if cols * step % 512 == 0 and cols % 128 == 0:
            return step
    return 1


class Rows:
    def __init__(self, parts, ordered, swapped=0):
        self.ordered, self.swapped = ordered, swapped
        self.part = parts[0].shape[0]
        self.args = list(parts)
        self.count = self.part * len(parts)
        self.width = parts[0].shape[1]
        self.copies = len(parts) * max(1, swapped)

    def load(self, copies, refs, target, sc, first=0):
        started = []
        for j, ref in enumerate(refs):
            at = first + j * self.part
            if self.ordered and len(refs) > 1:
                at = pl.multiple_of((sc[1] ^ j) * self.part, 16)
            rows = pl.ds(at, self.part)
            if not self.swapped:
                started.append(copies.start(ref, target.at[rows, :]))
                continue
            block = self.width // self.swapped
            for k in range(self.swapped):
                source = ref.at[:, pl.ds((k ^ 1) * block, block)]
                started.append(copies.start(source, target.at[rows, pl.ds(k * block, block)]))
        return started


class Slots:
    def __init__(self, array):
        self.args, self.copies = [array], NZ
        _, self.count, self.cols = array.shape

    def load(self, copies, refs, target, sc, first=0):
        return [[copies.start(refs[0].at[z], target.at[z, pl.ds(first, self.count), :])] for z in range(NZ)]


class SplitSlots:
    def __init__(self, full, mine, theirs):
        self.args, self.copies = [full, mine, theirs], 2 * NZ
        self.count, self.cols = full.shape[1] + mine.shape[1], full.shape[2]

    def load(self, copies, refs, target, sc, first=0):
        full, mine, theirs = refs
        by_slot = [[copies.start(full.at[z], target.at[z, whole_image(sc), :])] for z in range(NZ)]
        for z in range(NZ):
            source = (theirs if z % 2 else mine).at[z // 2]
            by_slot[z].append(copies.start(source, target.at[z, split_rows(sc), :]))
        return by_slot


def ring_place(column, z):
    return column * NZ + jnp.where(column % 2 == 0, z, NZ - 1 - z)


def hidden_place(sc, k, slot):
    return ring_place((sc[0] ^ k) >> 1, sc[3] ^ slot)


def take(items, count):
    return items[:count], items[count:]


def multiply_parts(y, w, flat, parts, copies, outs, sc, ordered, swapped):
    members, part, width = parts.shape

    def product(rows):
        if flat:
            return nt(jnp.concatenate([y[z, rows, :] for z in range(NZ)], axis=1), w[...])
        value = nt(y[0, rows, :], w[0])
        for z in range(1, NZ):
            value += nt(y[z, rows, :], w[z])
        return value

    together = None if part % 16 == 0 else product(slice(None))
    started = []
    for j in range(members):
        if together is not None:
            value = together[j * part : (j + 1) * part]
        else:
            value = product(pl.ds(pl.multiple_of((sc[1] ^ j) * part, 16) if ordered else j * part, part))
        block = width // swapped if swapped else width
        for k in range(width // block):
            to = k ^ 1 if swapped else k
            parts[j, :, to * block : (to + 1) * block] = value[:, k * block : (k + 1) * block].astype(BF16)
        goal = outs[j]
        started.append((j, goal))
        if together is None or not ordered:
            started[-1] = copies.start(parts.at[j], goal)
    if together is not None and ordered:
        started = [copies.start(parts.at[sc[1] ^ j], goal) for j, goal in started]
    return started


def gate(scalars, name, after, hold):
    def body(sc, ins, outs, scratch, copies):
        pass

    return manual(body, name, scalars, [], [], [], 1, after, hold)


def add(scalars, arrays, after=(), hold=()):
    out, *held = add_groups(scalars, [arrays], False, after, hold)
    return (out, *held)


def add_groups(scalars, groups, apart, after=(), hold=()):
    dims, terms = groups[0][0].shape, len(groups[0])
    three = len(dims) == 3
    count = dims[0] if three else 3 if dims[0] % 48 == 0 else 1
    rows = 0 if three else dims[0] // count
    place = (lambda ref, i: ref.at[i]) if three else (lambda ref, i: ref.at[pl.ds(i * rows, rows), :])
    at = (lambda i: i) if three else (lambda i: slice(i * rows, (i + 1) * rows))

    def body(sc, ins, outs, scratch, copies):
        arriving = []
        for g in range(len(groups)):
            for i in range(count):
                arriving.append([
                    copies.start(place(ins[g * terms + t], i), place(scratch[g * terms + t], i)) for t in range(terms)
                ])
        leaving = []
        for g in range(len(groups)):
            total_ref = scratch[len(groups) * terms + g]
            for i in range(count):
                wait(arriving[g * count + i])
                total = scratch[g * terms][at(i)].astype(F32)
                for t in range(1, terms):
                    total += scratch[g * terms + t][at(i)].astype(F32)
                total_ref[at(i)] = total.astype(BF16)
                goal = outs[g * count + i] if apart else place(outs[g], i)
                leaving.append(copies.start(place(total_ref, i), goal))
        wait(leaving)

    made = [shape(dims[1:], BF16)] * (count * len(groups)) if apart else [shape(dims, BF16)] * len(groups)
    return manual(
        body, "add", scalars, [a for g in groups for a in g], made, [vmem(dims)] * ((terms + 1) * len(groups)),
        (terms + 1) * count * len(groups), after, hold,
    )


def project(scalars, rows, weights, name, after=(), hold=()):
    count, cols = rows.count, weights.cols
    half = SEQ // 2
    chunks = 2 if count % 32 == 0 else 1

    def body(sc, ins, outs, scratch, copies):
        x, w, y = scratch
        row_refs, weight_refs = take(ins, len(rows.args))
        started = rows.load(copies, row_refs, x, sc)
        by_slot = weights.load(copies, weight_refs, w, sc)
        wait(started)
        step, leaving = slots_at_once(cols), []
        for c in range(chunks):
            here = pl.ds(c * (count // chunks), count // chunks)
            for z in range(0, NZ, step):
                if c == 0:
                    for s in range(z, z + step):
                        wait(by_slot[s])
                value = nn(x[here, :], weights.slots(w, z, step))
                for s in range(step):
                    y[z + s, here, :] = value[:, s * cols : (s + 1) * cols].astype(BF16)
                    leaving.append(copies.start(y.at[z + s, here, :], outs[0].at[z + s, here, :]))
        for z in range(1, NZ, 2):
            leaving.append(copies.start(y.at[z, split_rows(sc), :], outs[1].at[z // 2]))
        wait(leaving)

    return manual(
        body, name, scalars, rows.args + weights.args,
        [shape((NZ, count, cols), BF16), shape((NZ // 2, half, cols), BF16)],
        [vmem((count, rows.width)), weights.scratch, vmem((NZ, count, cols))],
        rows.copies + weights.copies + NZ * chunks + NZ // 2, after, hold,
    )


def project_back(scalars, slots, weights, nodes, name, after=(), hold=()):
    count, cols, width = slots.count, weights.cols, weights.depth

    def body(sc, ins, outs, scratch, copies):
        y, w, parts = scratch
        slot_refs, weight_refs = take(ins, len(slots.args))
        for started in slots.load(copies, slot_refs, y, sc) + weights.load(copies, weight_refs, w, sc):
            wait(started)
        wait(multiply_parts(y, w, weights.flat, parts, copies, outs, sc, True, 0))

    return manual(
        body, name, scalars, slots.args + weights.args, [shape((count // nodes, width), BF16)] * nodes,
        [vmem((NZ, count, cols)), weights.scratch, vmem((nodes, count // nodes, width))],
        slots.copies + weights.copies + nodes, after, hold,
    )


def weight_grads(scalars, products, dps, out_shape, goal, side, name, after=(), hold=()):
    counts = [sum(g.count for g in rows) for rows, _ in products]
    widths = [slots[0].cols for _, slots in products]
    width = products[0][0][0].width
    block = width // dps
    parts = 1 if side else len(products)
    cols = sum(widths) if side else widths[0]
    step = max(slots_at_once(c) for c in widths)
    args, scratch, copies_needed = [], [vmem((parts, NZ, width, cols))], parts * NZ * dps
    for (rows, slots), count, own in zip(products, counts, widths):
        args += [a for g in rows + slots for a in g.args]
        scratch += [vmem((count, width)), vmem((NZ, count, own)), vmem((width, count))]
        copies_needed += sum(g.copies for g in rows + slots)

    def body(sc, ins, outs, scratch, copies):
        result = scratch[0]
        loaded = []
        for i, (rows, slots) in enumerate(products):
            x, y, flipped = scratch[1 + 3 * i : 4 + 3 * i]
            started, at = [], 0
            for g in rows:
                refs, ins = take(ins, len(g.args))
                started += g.load(copies, refs, x, sc, at)
                at += g.count
            by_slot, at = [[] for _ in range(NZ)], 0
            for g in slots:
                refs, ins = take(ins, len(g.args))
                for z, some in enumerate(g.load(copies, refs, y, sc, at)):
                    by_slot[z] += some
                at += g.count
            loaded.append((started, by_slot))
        leaving = []

        def send(part, z, ks=range(dps)):
            for k in ks:
                rows = pl.ds(k * block, block)
                leaving.append(copies.start(result.at[part, z, rows, :], goal(sc, outs, part, k, z)))

        def multiply(i, z, at, part, ks=range(dps)):
            y, flipped, own = scratch[2 + 3 * i], scratch[3 + 3 * i], widths[i]
            here = slice(ks[0] * block, (ks[-1] + 1) * block)
            if ks[0] == 0:
                for s in range(z, z + step):
                    wait(loaded[i][1][s])
            whole_y = jnp.concatenate([y[z + s] for s in range(step)], axis=1) if step > 1 else y[z]
            value = nn(flipped[here, :], whole_y)
            for s in range(step):
                result[part, z + s, here, at : at + own] = value[:, s * own : (s + 1) * own].astype(BF16)

        def flip(i):
            wait(loaded[i][0])
            scratch[3 + 3 * i][...] = scratch[1 + 3 * i][...].T

        if side:
            for i in range(len(products)):
                flip(i)
            for ks in (range(dps // 2), range(dps // 2, dps)):
                for z in range(0, NZ, step):
                    for i in range(len(products)):
                        multiply(i, z, sum(widths[:i]), 0, ks)
                    for s in range(z, z + step):
                        send(0, s, ks)
        else:
            for i in range(len(products)):
                flip(i)
                for z in range(0, NZ, step):
                    multiply(i, z, 0, i)
                    for s in range(z, z + step):
                        send(i, s)
        wait(leaving)

    return list(manual(body, name, scalars, args, out_shape, scratch, copies_needed, after, hold))


def gelu_and_slope(u):
    cdf = 0.5 + 0.5 * lax.erf(u * math.sqrt(0.5))
    return u * cdf, cdf + u * (jnp.exp(-0.5 * u * u) * (1.0 / math.sqrt(2.0 * math.pi)))


def feed_forward(scalars, rows, weights, bias_row, name, after=(), hold=()):
    count, cols = rows.count, weights.cols

    def body(sc, ins, outs, scratch, copies):
        x, w, b, hidden, slope = scratch
        row_refs, weight_refs = take(ins, len(rows.args))
        started = rows.load(copies, row_refs, x, sc)
        for z in range(NZ):
            started.append(copies.start(weight_refs[0].at[sc[3] ^ z, pl.ds(bias_row, BIAS_ROWS), :], b.at[z]))
        by_slot = weights.load(copies, weight_refs, w, sc)
        wait(started)
        leaving = []
        step = slots_at_once(cols)
        for z in range(0, NZ, step):
            for s in range(z, z + step):
                wait(by_slot[s])
            value = nn(x[...], weights.slots(w, z, step))
            for s in range(step):
                terms = b[z + s].astype(F32)
                act, steep = gelu_and_slope(value[:, s * cols : (s + 1) * cols] + (terms[0:1] + terms[1:2] + terms[2:3]))
                hidden[z + s] = act.astype(BF16)
                slope[z + s] = steep.astype(BF16)
                leaving.append(copies.start(hidden.at[z + s], outs[0].at[z + s]))
                leaving.append(copies.start(slope.at[z + s], outs[1].at[z + s]))
        wait(leaving)

    return manual(
        body, name, scalars, rows.args + weights.args, [shape((NZ, count, cols), BF16)] * 2,
        [vmem((count, rows.width)), weights.scratch, vmem((NZ, BIAS_ROWS, cols)), vmem((NZ, count, cols)), vmem((NZ, count, cols))],
        rows.copies + NZ + weights.copies + 2 * NZ, after, hold,
    )


def feed_back(scalars, rows, slope, down, up, nodes, swapped, name, after=(), hold=()):
    count, cols, width = rows.count, down.cols, rows.width

    def body(sc, ins, outs, scratch, copies):
        x, wd, wu, steep, du, gb, parts = scratch
        row_refs, ins = take(ins, len(rows.args))
        slope_ref, ins = ins[0], ins[1:]
        down_refs, up_refs = take(ins, len(down.args))
        started = rows.load(copies, row_refs, x, sc)
        down_slots = down.load(copies, down_refs, wd, sc)
        steep_slots = [copies.start(slope_ref.at[z], steep.at[z]) for z in range(NZ)]
        up_slots = up.load(copies, up_refs, wu, sc)
        wait(started)
        leaving = []
        step = slots_at_once(cols)
        for z in range(0, NZ, step):
            for s in range(z, z + step):
                wait(down_slots[s])
                steep_slots[s].wait()
            value = nn(x[...], down.slots(wd, z, step))
            for s in range(step):
                grad = value[:, s * cols : (s + 1) * cols] * steep[z + s].astype(F32)
                gb[z + s : z + s + 1, :] = jnp.sum(grad, axis=0, keepdims=True)
                du[z + s] = grad.astype(BF16)
                leaving.append(copies.start(du.at[z + s], outs[0].at[z + s]))
        leaving.append(copies.start(gb, outs[1]))
        for z in range(NZ):
            wait(up_slots[z])
        wait(leaving + multiply_parts(du, wu, True, parts, copies, outs[2:], sc, False, swapped))

    out = manual(
        body, name, scalars, rows.args + [slope] + down.args + up.args,
        [shape((NZ, count, cols), BF16), shape((NZ, cols), F32)] + [shape((count // nodes, width), BF16)] * nodes,
        [vmem((count, width)), down.scratch, up.scratch, vmem((NZ, count, cols)), vmem((NZ, count, cols)),
         vmem((NZ, cols), F32), vmem((nodes, count // nodes, width))],
        rows.copies + down.copies + up.copies + 2 * NZ + 1 + nodes, after, hold,
    )
    return out[0], out[1], list(out[2 : 2 + nodes]), out[2 + nodes :]


def feed_both(scalars, rows, grads, up, down, bias_row, nodes, swapped, name, after=(), hold=()):
    count, cols, width = rows.count, up.cols, rows.width

    def body(sc, ins, outs, scratch, copies):
        x, g, wu, wd, b, hidden, steep, du, gb, parts = scratch
        row_refs, ins = take(ins, len(rows.args))
        grad_refs, ins = take(ins, len(grads.args))
        up_refs, down_refs = take(ins, len(up.args))
        started = rows.load(copies, row_refs, x, sc)
        for z in range(NZ):
            started.append(copies.start(up_refs[0].at[sc[3] ^ z, pl.ds(bias_row, BIAS_ROWS), :], b.at[z]))
        up_slots = up.load(copies, up_refs, wu, sc)
        grads_started = grads.load(copies, grad_refs, g, sc)
        down_slots = down.load(copies, down_refs, wd, sc)
        wait(started)
        leaving = []
        step = slots_at_once(cols)
        for z in range(0, NZ, step):
            for s in range(z, z + step):
                wait(up_slots[s])
            value = nn(x[...], up.slots(wu, z, step))
            for s in range(step):
                terms = b[z + s].astype(F32)
                act, slope = gelu_and_slope(value[:, s * cols : (s + 1) * cols] + (terms[0:1] + terms[1:2] + terms[2:3]))
                hidden[z + s] = act.astype(BF16)
                steep[z + s] = slope.astype(BF16)
                leaving.append(copies.start(hidden.at[z + s], outs[0].at[z + s]))
        wait(grads_started)
        for z in range(0, NZ, step):
            for s in range(z, z + step):
                wait(down_slots[s])
            value = nn(g[...], down.slots(wd, z, step))
            for s in range(step):
                grad = value[:, s * cols : (s + 1) * cols] * steep[z + s].astype(F32)
                gb[z + s : z + s + 1, :] = jnp.sum(grad, axis=0, keepdims=True)
                du[z + s] = grad.astype(BF16)
                leaving.append(copies.start(du.at[z + s], outs[1].at[z + s]))
        leaving.append(copies.start(gb, outs[2]))
        wait(leaving + multiply_parts(du, wu, True, parts, copies, outs[3:], sc, False, swapped))

    out = manual(
        body, name, scalars, rows.args + grads.args + up.args + down.args,
        [shape((NZ, count, cols), BF16)] * 2 + [shape((NZ, cols), F32)] + [shape((count // nodes, width), BF16)] * nodes,
        [vmem((count, width)), vmem((count, width)), up.scratch, down.scratch, vmem((NZ, BIAS_ROWS, cols)),
         vmem((NZ, count, cols)), vmem((NZ, count, cols)), vmem((NZ, count, cols)), vmem((NZ, cols), F32),
         vmem((nodes, count // nodes, width))],
        rows.copies + grads.copies + up.copies + down.copies + 3 * NZ + 1 + nodes, after, hold,
    )
    return out[0], out[1], out[2], list(out[3 : 3 + nodes]), out[3 + nodes :]


def feed_out(scalars, hidden, down, nodes, swapped, name, after=(), hold=()):
    _, count, cols = hidden.shape
    width = down.depth

    def body(sc, ins, outs, scratch, copies):
        y, w, parts = scratch
        started = [copies.start(ins[0].at[z], y.at[z]) for z in range(NZ)]
        by_slot = down.load(copies, ins[1:], w, sc)
        wait(started)
        for z in range(NZ):
            wait(by_slot[z])
        wait(multiply_parts(y, w, True, parts, copies, outs, sc, False, swapped))

    return manual(
        body, name, scalars, [hidden] + down.args, [shape((count // nodes, width), BF16)] * nodes,
        [vmem((NZ, count, cols)), down.scratch, vmem((nodes, count // nodes, width))],
        NZ + down.copies + nodes, after, hold,
    )


def head_mask(cols, head):
    lane = lax.broadcasted_iota(jnp.int32, (1, cols), 1)
    return (lane >= head * HD) & (lane < (head + 1) * HD)


def by_head_rows(values):
    cols = values.shape[1]
    return jnp.concatenate(
        [jnp.where(head_mask(cols, h), values, 0).astype(BF16) for h in range(cols // HD)], axis=0
    )


def own_columns(stacked, cols):
    count = stacked.shape[0] // (cols // HD)
    total = None
    for h in range(cols // HD):
        piece = jnp.where(head_mask(cols, h), stacked[h * count : (h + 1) * count], 0.0)
        total = piece if total is None else total + piece
    return total


def attend(q, k, v):
    queries = by_head_rows((q * (1.0 / math.sqrt(HD))).astype(BF16))
    scores = nt(k, queries)
    raised = jnp.exp(scores - jnp.max(scores, axis=0, keepdims=True))
    soft = (raised * (1.0 / jnp.sum(raised, axis=0, keepdims=True))).astype(BF16)
    return own_columns(tn(soft, v), q.shape[1]).astype(BF16)


def attend_back(q, k, v, do):
    cols = q.shape[1]
    queries, grads = by_head_rows((q * (1.0 / math.sqrt(HD))).astype(BF16)), by_head_rows(do)
    scores = nt(k, queries)
    raised = jnp.exp(scores - jnp.max(scores, axis=0, keepdims=True))
    soft = raised * (1.0 / jnp.sum(raised, axis=0, keepdims=True))
    dsoft = nt(v, grads)
    dot = jnp.sum(dsoft * soft, axis=0, keepdims=True)
    dscores = (soft * (dsoft - dot)).astype(BF16)
    dv = nn(soft.astype(BF16), grads)
    dk = nn(dscores, queries)
    dq = own_columns(tn(dscores, k), cols) * (1.0 / math.sqrt(HD))
    return dq.astype(BF16), dk.astype(BF16), dv.astype(BF16)


def slots_together(cols):
    return 2 if 2 * cols == 256 else 1


def part_of(pieces, j, cols):
    return jnp.concatenate([p[:, j * cols : (j + 1) * cols] for p in pieces], axis=1) if len(pieces) > 1 else pieces[0][
        :, j * cols : (j + 1) * cols
    ]


def whole_image(sc):
    return pl.ds(pl.multiple_of(sc[2] * (SEQ // 2), 32), SEQ)


def split_rows(sc):
    return pl.ds(pl.multiple_of((1 - sc[2]) * SEQ, 32), SEQ // 2)


def pair_slots(dims, together):
    return pl.BlockSpec((together,) + dims, lambda s, *_: (s, 0, 0))


def own_slots(dims, together):
    return [pl.BlockSpec((1,) + dims, lambda s, *_, i=i: (2 * (s * together + i), 0, 0)) for i in range(together)]


def attend_whole(scalars, qkv, after=(), hold=()):
    slots, count, triple = qkv.shape
    cols = triple // 3
    together = slots_together(cols)

    def body(sc, qkv_ref, o_ref):
        rows = whole_image(sc)
        pieces = [qkv_ref[i, rows, :] for i in range(together)]
        mixed = attend(*(part_of(pieces, j, cols) for j in range(3)))
        for i in range(together):
            o_ref[i] = mixed[:, i * cols : (i + 1) * cols]

    return call(
        body, "attend_whole", (slots // together,), scalars, [pair_slots((count, triple), together)],
        pair_slots((SEQ, cols), together), shape((slots, SEQ, cols), BF16), [qkv],
        after=after, hold=hold, nbytes=2 * slots * count * 4 * cols,
    )


def attend_split(scalars, qkv, partner, after=(), hold=()):
    slots, half, triple = partner.shape
    count = qkv.shape[1]
    cols = triple // 3
    together = slots_together(cols)

    def body(sc, *refs):
        qkv_refs, (partner_ref, mine_ref, theirs_ref, joined) = refs[:together], refs[together:]
        for i, ref in enumerate(qkv_refs):
            joined[i, :half, :] = ref[0, split_rows(sc), :]
            joined[i, half:, :] = partner_ref[i]
        pieces = [joined[i] for i in range(together)]
        mixed = attend(*(part_of(pieces, j, cols) for j in range(3)))
        for i in range(together):
            mine_ref[i] = mixed[:half, i * cols : (i + 1) * cols]
            theirs_ref[i] = mixed[half:, i * cols : (i + 1) * cols]

    return call(
        body, "attend_split", (slots // together,), scalars,
        own_slots((count, triple), together) + [pair_slots((half, triple), together)],
        [pair_slots((half, cols), together)] * 2, [shape((slots, half, cols), BF16)] * 2, [qkv] * together + [partner],
        scratch=[vmem((together, 2 * half, triple))], after=after, hold=hold, nbytes=2 * slots * count * 4 * cols,
    )


def attend_whole_back(scalars, qkv, do, after=(), hold=()):
    slots, count, triple = qkv.shape
    cols = triple // 3
    together = slots_together(cols)

    def body(sc, qkv_ref, do_ref, out_ref):
        rows = whole_image(sc)
        pieces = [qkv_ref[i, rows, :] for i in range(together)]
        do = part_of([do_ref[i, rows, :] for i in range(together)], 0, cols)
        grads = attend_back(*(part_of(pieces, j, cols) for j in range(3)), do)
        for i in range(together):
            for j in range(3):
                out_ref[i, :, j * cols : (j + 1) * cols] = grads[j][:, i * cols : (i + 1) * cols]

    return call(
        body, "attend_whole_back", (slots // together,), scalars,
        [pair_slots((count, triple), together), pair_slots((count, cols), together)],
        pair_slots((SEQ, triple), together), shape((slots, SEQ, triple), BF16), [qkv, do],
        after=after, hold=hold, nbytes=2 * slots * count * 7 * cols,
    )


def attend_split_back(scalars, qkv, partner, do, do_partner, after=(), hold=()):
    slots, half, triple = partner.shape
    count = qkv.shape[1]
    cols = triple // 3
    together = slots_together(cols)

    def body(sc, *refs):
        qkv_refs, do_refs = refs[:together], refs[together : 2 * together]
        partner_ref, do_partner_ref, mine_ref, theirs_ref, joined, joined_do = refs[2 * together :]
        for i in range(together):
            joined[i, :half, :] = qkv_refs[i][0, split_rows(sc), :]
            joined[i, half:, :] = partner_ref[i]
            joined_do[i, :half, :] = do_refs[i][0, split_rows(sc), :]
            joined_do[i, half:, :] = do_partner_ref[i]
        pieces = [joined[i] for i in range(together)]
        do = part_of([joined_do[i] for i in range(together)], 0, cols)
        grads = attend_back(*(part_of(pieces, j, cols) for j in range(3)), do)
        for i in range(together):
            for j in range(3):
                mine_ref[i, :, j * cols : (j + 1) * cols] = grads[j][:half, i * cols : (i + 1) * cols]
                theirs_ref[i, :, j * cols : (j + 1) * cols] = grads[j][half:, i * cols : (i + 1) * cols]

    return call(
        body, "attend_split_back", (slots // together,), scalars,
        own_slots((count, triple), together) + own_slots((count, cols), together)
        + [pair_slots((half, triple), together), pair_slots((half, cols), together)],
        [pair_slots((half, triple), together)] * 2, [shape((slots, half, triple), BF16)] * 2,
        [qkv] * together + [do] * together + [partner, do_partner],
        scratch=[vmem((together, 2 * half, triple)), vmem((together, 2 * half, cols))],
        after=after, hold=hold, nbytes=2 * slots * count * 7 * cols,
    )


def by_rows(body, name, scalars, kinds, out_kinds, out_shape, args, after=(), hold=()):
    count = next(a for a, kind in zip(args, kinds) if kind == "r").shape[0]
    width = args[0].shape[1]
    steps = 3 if count % 48 == 0 else 1
    rows = count // steps
    made = len(out_shape)
    total = sum(steps if kind == "r" else 1 for kind in kinds + out_kinds)

    def part(ref, i):
        return ref.at[pl.ds(i * rows, rows), :]

    def run(sc, ins, outs, scratch, copies):
        here, results, work = scratch[: len(ins)], scratch[len(ins) : len(ins) + made], scratch[-1]
        first = [copies.start(r, h) for r, h, kind in zip(ins, here, kinds) if kind == "w"]
        arriving = [
            [copies.start(part(r, i), part(h, i)) for r, h, kind in zip(ins, here, kinds) if kind == "r"]
            for i in range(steps)
        ]
        wait(first)
        leaving = []
        for i in range(steps):
            wait(arriving[i])
            body(
                i, sc, [part(h, i) if kind == "r" else h for h, kind in zip(here, kinds)],
                [part(h, i) if kind == "r" else h for h, kind in zip(results, out_kinds)], work,
            )
            leaving += [copies.start(part(h, i), part(o, i)) for h, o, kind in zip(results, outs, out_kinds) if kind == "r"]
        leaving += [copies.start(h, o) for h, o, kind in zip(results, outs, out_kinds) if kind == "w"]
        wait(leaving)

    scratch = [vmem(a.shape, a.dtype) for a in list(args) + list(out_shape)] + [vmem((rows, width), F32)]
    return manual(run, name, scalars, args, out_shape, scratch, total, after, hold)


def to_relative(sc, scratch, out_ref, block):
    dps = scratch.shape[1] // block
    for k in range(dps):
        out_ref[:, k * block : (k + 1) * block] = scratch[
            :, pl.ds(pl.multiple_of((sc[0] ^ k) * block, block), block)
        ].astype(out_ref.dtype)


def from_relative(sc, refs, scratch, block):
    dps = scratch.shape[1] // block
    for k in range(dps):
        here = slice(k * block, (k + 1) * block)
        piece = refs[0][:, here].astype(F32)
        for ref in refs[1:]:
            piece += ref[:, here].astype(F32)
        scratch[:, pl.ds(pl.multiple_of((sc[0] ^ k) * block, block), block)] = piece


def normed(rows):
    centred = rows - jnp.mean(rows, axis=-1, keepdims=True)
    inverse = lax.rsqrt(jnp.mean(centred * centred, axis=-1, keepdims=True) + 1e-06)
    return centred * inverse, inverse


def norm_back(hat, inverse, grad, gain):
    scaled = grad * gain
    return inverse * (
        scaled - jnp.mean(scaled, axis=-1, keepdims=True) - hat * jnp.mean(scaled * hat, axis=-1, keepdims=True)
    )


def column(values):
    return jnp.sum(values, axis=0, keepdims=True)


def add_rows(step, ref, values):
    ref[...] = values if step == 0 else ref[...] + values


def first_norm(scalars, tokens, cotangent, vectors, dps, after=(), hold=()):
    count, width = tokens.shape
    block = width // dps

    def body(step, sc, ins, outs, work):
        x_ref, cot_ref, vec_ref = ins
        hat, _ = normed(x_ref[...])
        work[...] = hat * vec_ref[0:1] + vec_ref[1:2]
        to_relative(sc, work, outs[0], block)
        work[...] = cot_ref[...]
        to_relative(sc, work, outs[1], block)

    return by_rows(
        body, "first_norm", scalars, "rrw", "rr", [shape((count, width), BF16)] * 2, [tokens, cotangent, vectors], after, hold
    )


def second_norm(scalars, tokens, parts, vectors, dps, after=(), hold=()):
    count, width = tokens.shape
    block = width // dps

    def body(step, sc, ins, outs, work):
        x_ref, vec_ref, *part_refs = ins
        from_relative(sc, part_refs, work, block)
        h = x_ref[...] + work[...] + vec_ref[4:5]
        outs[0][...] = h
        hat, _ = normed(h)
        work[...] = hat * vec_ref[2:3] + vec_ref[3:4]
        to_relative(sc, work, outs[1], block)

    return by_rows(
        body, "second_norm", scalars, "rw" + "r" * len(parts), "rr",
        [shape((count, width), F32), shape((count, width), BF16)], [tokens, vectors] + list(parts), after, hold,
    )


def layer_output(scalars, middle, parts, vectors, dps, after=(), hold=()):
    count, width = middle.shape
    block = width // dps

    def body(step, sc, ins, outs, work):
        h_ref, vec_ref, *part_refs = ins
        from_relative(sc, part_refs, work, block)
        outs[0][...] = h_ref[...] + work[...] + vec_ref[5:6]

    return by_rows(
        body, "layer_output", scalars, "rw" + "r" * len(parts), "r", [shape((count, width), F32)],
        [middle, vectors] + list(parts), after, hold,
    )


def second_norm_back(scalars, middle, cotangent, parts, vectors, dps, after=(), hold=()):
    count, width = middle.shape
    block = width // dps

    def body(step, sc, ins, outs, work):
        h_ref, cot_ref, vec_ref, *part_refs = ins
        from_relative(sc, part_refs, work, block)
        dc = work[...]
        hat, inverse = normed(h_ref[...])
        cot = cot_ref[...]
        dh = cot + norm_back(hat, inverse, dc, vec_ref[2:3])
        outs[0][...] = dh
        work[...] = dh
        to_relative(sc, work, outs[1], block)
        add_rows(step, outs[2], jnp.concatenate([column(dc * hat), column(dc), column(dh), column(cot)], axis=0))

    return by_rows(
        body, "second_norm_back", scalars, "rrw" + "r" * len(parts), "rrw",
        [shape((count, width), F32), shape((count, width), BF16), shape((4, width), F32)],
        [middle, cotangent, vectors] + list(parts), after, hold,
    )


def first_norm_back(scalars, tokens, middle_grad, parts, vectors, dps, after=(), hold=()):
    count, width = tokens.shape
    block = width // dps

    def body(step, sc, ins, outs, work):
        x_ref, dh_ref, vec_ref, *part_refs = ins
        from_relative(sc, part_refs, work, block)
        da = work[...]
        hat, inverse = normed(x_ref[...])
        outs[0][...] = dh_ref[...] + norm_back(hat, inverse, da, vec_ref[0:1])
        add_rows(step, outs[1], jnp.concatenate([column(da * hat), column(da)], axis=0))

    return by_rows(
        body, "first_norm_back", scalars, "rrw" + "r" * len(parts), "rw",
        [shape((count, width), F32), shape((2, width), F32)], [tokens, middle_grad, vectors] + list(parts), after, hold,
    )


def adam_step(weight, gradient, first, second, rate, decay):
    first = 0.9 * first + 0.1 * gradient
    second = 0.999 * second + 0.001 * gradient * gradient
    first_fix = 1.0 - 0.9**STEP
    second_fix = 1.0 - 0.999**STEP
    update = first / first_fix / (jnp.sqrt(second / second_fix) + 1e-08) + decay * weight
    return (gradient, first, second, weight - rate * update)


def by_part(columns, heads):
    return jnp.concatenate([columns[:, (h * 3 + c) * HD : (h * 3 + c + 1) * HD] for c in range(3) for h in range(heads)], axis=1)


def by_head(columns, heads):
    return jnp.concatenate([columns[:, (c * heads + h) * HD : (c * heads + h + 1) * HD] for h in range(heads) for c in range(3)], axis=1)


def plain(body, name, args, out_shape, after=(), hold=()):
    given, extra = len(args), len(after) + len(hold)
    made = len(out_shape)
    nbytes = sum(math.prod(a.shape) * a.dtype.itemsize for a in list(args) + list(out_shape))

    def run(*refs):
        body(*refs[:given], *refs[given + extra : given + extra + made])

    anywhere = pl.BlockSpec(memory_space=pltpu.HBM)
    here = pl.BlockSpec(memory_space=pltpu.VMEM)
    first = given + len(after)
    return pl.pallas_call(
        run, name=name,
        out_shape=list(out_shape) + [shape(h.shape, h.dtype) for h in hold],
        in_specs=[pl.BlockSpec(memory_space=pltpu.SMEM)] + [here] * (given - 1) + [anywhere] * extra,
        out_specs=[here] * made + [anywhere] * len(hold),
        input_output_aliases={first + i: made + i for i in range(len(hold))},
        compiler_params=pltpu.CompilerParams(vmem_limit_bytes=VMEM_LIMIT), cost_estimate=cost(name, nbytes),
    )(*args, *after, *hold)


def weight_pieces(scalars, w_qkv, w_out, w_up, hidden_bias, w_down):
    block, cols = w_up.shape[0], w_up.shape[1] // 2
    heads, triple = w_qkv.shape[1] // (3 * HD), w_qkv.shape[1]

    def body(sc, qkv_ref, out_ref, up_ref, bias_ref, down_ref, attn_ref, my_up_ref, my_down_ref, theirs_ref):
        attn_ref[:, :triple] = by_part(qkv_ref[...], heads).astype(BF16)
        attn_ref[:, triple:] = out_ref[...].T.astype(BF16)
        mine, other = (pl.ds(pl.multiple_of(h * cols, cols), cols) for h in (sc[4], 1 - sc[4]))
        my_up_ref[:block, :] = up_ref[:, mine].astype(BF16)
        my_down_ref[...] = down_ref[mine, :].T.astype(BF16)
        theirs_ref[:block, :] = up_ref[:, other].astype(BF16)
        theirs_ref[block:, :] = down_ref[other, :].T.astype(BF16)
        rest = bias_ref[:, mine]
        row = lax.broadcasted_iota(jnp.int32, (BIAS_ROWS, cols), 0)
        terms = jnp.zeros((BIAS_ROWS, cols), F32)
        for i in range(3):
            term = rest.astype(BF16).astype(F32)
            terms = jnp.where(row == i, term, terms)
            rest = rest - term
        my_up_ref[block:, :] = terms.astype(BF16)

    return plain(
        body, "weight_pieces", [scalars, w_qkv, w_out, w_up, hidden_bias[None, :], w_down],
        [shape((block, triple + w_out.shape[0]), BF16), shape((block + BIAS_ROWS, cols), BF16),
         shape((block, cols), BF16), shape((2 * block, cols), BF16)],
    )


def attn_adam(scalars, near, far, w_qkv, qkv_m, qkv_v, w_out, out_m, out_v, after=()):
    heads, triple = w_qkv.shape[1] // (3 * HD), w_qkv.shape[1]
    block = far.shape[0]

    def body(sc, near_ref, far_ref, *refs):
        total = near_ref[:block, :].astype(F32) + far_ref[...].astype(F32)
        qw, qm, qv, ow, om, ov = (r[...] for r in refs[:6])
        new = adam_step(qw, by_head(total[:, :triple], heads), qm, qv, 0.1, 0.05)
        new += adam_step(ow, total[:, triple:].T, om, ov, 0.2, 0.05)
        for ref, value in zip(refs[6:], new):
            ref[...] = value

    out = plain(
        body, "attn_adam", [scalars, near, far, w_qkv, qkv_m, qkv_v, w_out, out_m, out_v],
        [shape(w_qkv.shape, F32)] * 4 + [shape(w_out.shape, F32)] * 4, after,
    )
    return tuple(out[:4]), tuple(out[4:])


def hidden_adam(scalars, total, far, up, down, after=(), hold=()):
    block, cols = far.shape[0] // 2, far.shape[1]

    def body(sc, total_ref, far_ref, *refs):
        ins, outs = take(refs, 6)
        up_grad, down_grad = outs[0], outs[4]
        for ref, half in ((total_ref, sc[4]), (far_ref, 1 - sc[4])):
            at = pl.ds(pl.multiple_of(half * cols, cols), cols)
            down_grad[at, :] = ref[:block, :].astype(F32).T
            up_grad[:, at] = ref[block : 2 * block, :].astype(F32)
        for (w, m, v), made, rate in ((ins[:3], outs[:4], 0.1), (ins[3:], outs[4:], 0.05)):
            new = adam_step(w[...], made[0][...], m[...], v[...], rate, 0.05)
            for ref, value in zip(made[1:], new[1:]):
                ref[...] = value

    out = plain(
        body, "hidden_adam", [scalars, total, far] + list(up) + list(down),
        [shape(up[0].shape, F32)] * 4 + [shape(down[0].shape, F32)] * 4, after, hold,
    )
    return tuple(out[:4]), tuple(out[4:8]), out[8:]


def solution(mesh):
    dps, tensor = mesh.shape["dp"], mesh.shape["tensor"]
    nodes = tensor // NZ
    devices = dps * tensor

    def snake(columns):
        return [(d, z) for i, d in enumerate(columns) for z in (range(NZ) if i % 2 == 0 else range(NZ - 1, -1, -1))]

    z_groups = [[d * tensor + z * nodes + c for z in range(NZ)] for d in range(dps) for c in range(nodes)]
    half_rings = [
        [d * tensor + z * nodes + c for d, z in snake(range(x, dps, 2))] for x in range(2) for c in range(nodes)
    ]

    def swap(value, flip):
        return lax.ppermute(value, AXES, [(i, i ^ flip) for i in range(devices)])

    def gather_ring(piece, groups):
        return lax.all_gather(piece, AXES, axis=0, axis_index_groups=groups)

    def scatter_ring(total, groups):
        return lax.psum_scatter(total, AXES, scatter_dimension=0, axis_index_groups=groups, tiled=True)[0]

    def by_weight(k):
        return (bin(k).count("1"), k)

    def gather(own, count, unit, low_first):
        bufs = [own] + [None] * (count - 1)
        for k in sorted(range(1, count), key=by_weight):
            last = k & -k if low_first else 1 << (k.bit_length() - 1)
            bufs[k] = swap(bufs[k ^ last], last * unit)
        return bufs

    def plus(left, right):
        return (left.astype(F32) + right.astype(F32)).astype(BF16)

    def add_up(sums):
        total = sums[0].astype(F32)
        for piece in sums[1:]:
            total = total + piece.astype(F32)
        return total.astype(BF16)

    def along_z(piece):
        return [piece] + [swap(piece, j * nodes) for j in range(1, NZ)]

    def relative(own):
        return [own] + [swap(own, j) for j in range(1, nodes)]

    def ordered_rows(parts, member):
        if parts[0].shape[0] % 16 == 0:
            return Rows(parts, True)
        flip = 1
        while len(parts) > 1:
            odd = (member // flip) % 2 == 1
            parts = [
                jnp.where(odd, jnp.concatenate([b, a], axis=0), jnp.concatenate([a, b], axis=0))
                for a, b in zip(parts[0::2], parts[1::2])
            ]
            flip *= 2
        return Rows(parts, True)

    def relative_rows(parts, swapped=0):
        if parts[0].shape[0] % 16:
            parts = [jnp.concatenate(parts, axis=0)]
        return Rows(parts, False, swapped)

    def send_parts(parts):
        return [parts[0]] + [swap(parts[j], j) for j in range(1, nodes)]

    def per_device(
        tokens, cotangent, vectors, vectors_m, vectors_v,
        w_qkv, qkv_m, qkv_v, w_out, out_m, out_v, w_up, up_m, up_v,
        hidden_bias, bias_m, bias_v, w_down, down_m, down_v,
    ):
        dp_index = lax.axis_index("dp")
        tensor_index = lax.axis_index("tensor")
        z_index, member = tensor_index // nodes, tensor_index % nodes
        odd_x = dp_index % 2
        scalars = jnp.stack([dp_index, member, z_index % 2, z_index, odd_x]).astype(jnp.int32)
        block = w_qkv.shape[0]
        triple, width = w_qkv.shape[1], w_out.shape[0]
        hidden_here = w_up.shape[1] // 2

        attn_own, my_up, my_down, theirs = weight_pieces(scalars, w_qkv, w_out, w_up, hidden_bias, w_down)
        attn_z = along_z(attn_own)
        arrived = swap(theirs, tensor)
        lower, upper = jnp.stack(attn_z[:2]), jnp.stack(attn_z[2:])
        up_piece = jnp.concatenate([my_up, arrived[:block]], axis=0)
        down_piece = jnp.concatenate([my_down, arrived[block:]], axis=0)
        early = attn_own
        if dps == 4:
            lowers, uppers = [swap(lower, tensor), swap(lower, 2 * tensor)], [swap(upper, tensor), swap(upper, 2 * tensor)]
            *lowers, up_piece, down_piece = gate(
                scalars, "gate_lower", [upper], lowers + [up_piece, down_piece]
            )
            early = up_piece
        a_own, g_own = first_norm(scalars, tokens, cotangent, vectors, dps, after=[early])
        a_parts = relative(a_own)
        if dps == 4:
            lowers[0], uppers[1], g_own = gate(
                scalars, "gate_gather", [lowers[1], uppers[0], a_own], [lowers[0], uppers[1], g_own]
            )
            lowers = [lower] + lowers + [swap(lowers[0], 2 * tensor)]
            uppers = [upper] + uppers + [swap(uppers[1], tensor)]
        else:
            lowers, uppers = gather(lower, dps, tensor, False), gather(upper, dps, tensor, True)
        up_z = gather_ring(up_piece, z_groups)
        halves = [(0, [(2 * k + z // 2, z % 2) for z in range(NZ)]) for k in range(dps)]
        attn_w = [half for pair in zip(lowers, uppers) for half in pair]
        qkv_w = Weights(attn_w, halves, block, 0, triple)
        out_w = Weights(attn_w, halves, block, triple, width)

        a_rows = ordered_rows(a_parts, member)
        qkv, qkv_theirs = project(scalars, a_rows, qkv_w, "qkv")
        qkv_partner = swap(qkv_theirs, nodes)
        g_far = swap(g_own, tensor)
        (up_z,) = gate(scalars, "gate_up", [qkv], [up_z])
        up_w = Weights(
            gather(up_z, dps // 2, 2 * tensor, False),
            [(k % 2 * (block + BIAS_ROWS), [(k // 2, lambda sc, z=z: sc[3] ^ z) for z in range(NZ)]) for k in range(dps)],
            block, 0, hidden_here,
        )
        mixed = attend_whole(scalars, qkv, after=[up_z])
        mixed_mine, mixed_theirs, down_piece = attend_split(scalars, qkv, qkv_partner, after=[mixed], hold=[down_piece])
        down_w = Weights(
            [gather_ring(down_piece, half_rings)],
            [(k % 2 * block, [(0, lambda sc, k=k, z=z: hidden_place(sc, k, z)) for z in range(NZ)]) for k in range(dps)],
            block, 0, hidden_here,
        )
        mixed = SplitSlots(mixed, mixed_mine, swap(mixed_theirs, nodes))
        *attn_parts, g_far = project_back(
            scalars, mixed, out_w, nodes, "attn_out", after=up_w.args[1:], hold=[g_far]
        )
        middle, c_own = second_norm(scalars, tokens, send_parts(attn_parts), vectors, dps)

        c_far = swap(c_own, tensor)
        g_rows, g_far = relative_rows(relative(g_own)), relative_rows(relative(g_far), dps)
        c_rows = relative_rows(relative(c_own))
        hidden, slope = feed_forward(scalars, c_rows, up_w, block, "feed_forward")
        du, bias_near, dc_near, _ = feed_back(
            scalars, g_rows, slope, down_w, up_w, nodes, 0, "feed_back", after=[hidden]
        )
        dc_near = send_parts(dc_near)
        (c_far,) = gate(scalars, "gate_rows", [du], [c_far])
        c_far = relative_rows(relative(c_far), dps)
        hidden_far, du_far, bias_far, dc_far, _ = feed_both(
            scalars, c_far, g_far, up_w, down_w, block, nodes, dps, "feed_both", after=[du] + dc_near[1:]
        )
        (dc_sum,) = add(scalars, send_parts(dc_far), after=[du_far])
        dc_arrived = swap(dc_sum, tensor)


        def hidden_goal(sc, outs, part, k, z):
            return outs[0].at[hidden_place(sc, k, z), pl.ds((2 * (k % 2) + part) * block, block), :]

        (hidden_part,) = weight_grads(
            scalars,
            [([g_rows, g_far], [Slots(hidden), Slots(hidden_far)]), ([c_rows, c_far], [Slots(du), Slots(du_far)])],
            dps, [shape((NZ * dps // 2, 4 * block, hidden_here), BF16)],
            hidden_goal, False, "hidden_grad", after=[dc_sum],
        )
        out_far = feed_out(scalars, hidden_far, down_w, nodes, dps, "feed_out_far", after=[hidden_part])
        hidden_total = scatter_ring(hidden_part, half_rings)
        middle_grad, e_own, sums_two = second_norm_back(
            scalars, middle, cotangent, dc_near + [dc_arrived], vectors, dps, after=[out_far[0]]
        )
        out_far = send_parts(out_far)

        e_rows = ordered_rows(relative(e_own), member)
        dmixed, dmixed_theirs = project(scalars, e_rows, out_w, "mixed_grad", after=out_far[1:])
        dmixed_partner = swap(dmixed_theirs, nodes)
        out_near = feed_out(scalars, hidden, down_w, nodes, 0, "feed_out", after=[dmixed])
        dqkv_mine, dqkv_theirs = attend_split_back(
            scalars, qkv, qkv_partner, dmixed, dmixed_partner, after=[out_near[0]]
        )
        dqkv_whole = attend_whole_back(scalars, qkv, dmixed, after=[dqkv_mine])
        dqkv = SplitSlots(dqkv_whole, dqkv_mine, swap(dqkv_theirs, nodes))

        def attn_goal(first, cols):
            def goal(sc, outs, part, k, z):
                place = outs[0].at[hidden_place(sc, k, z), pl.ds((k % 2) * block, block), :]
                return place if cols == triple + width else place.at[:, pl.ds(first, cols)]

            return goal

        attn_shape = [shape((NZ * dps // 2, 2 * block, triple + width), BF16)]
        if triple % 128 == 0 and width % 128 == 0:
            out_part = weight_grads(
                scalars, [([e_rows], [mixed])], dps, attn_shape, attn_goal(triple, width), True, "out_grad",
                after=[dqkv_whole],
            )
            attn_part, out_far[0] = weight_grads(
                scalars, [([a_rows], [dqkv])], dps, [], attn_goal(0, triple), True, "attn_grad",
                hold=out_part + [out_far[0]],
            )
        else:
            attn_part, out_far[0] = weight_grads(
                scalars, [([a_rows], [dqkv]), ([e_rows], [mixed])], dps, attn_shape, attn_goal(0, triple + width), True,
                "attn_grad", hold=[out_far[0]],
            )
        out_arrived = swap(add_up(out_far), tensor)
        da_parts = send_parts(project_back(scalars, dqkv, qkv_w, nodes, "first_back", after=[attn_part]))
        input_grad, sums_one, hidden_total = first_norm_back(
            scalars, tokens, middle_grad, da_parts, vectors, dps, hold=[hidden_total]
        )
        attn_part = scatter_ring(attn_part, half_rings)

        here = (jnp.arange(nodes)[:, None] == member) & (jnp.arange(2)[None, :] == odd_x)
        own_slot_of = (jnp.arange(NZ)[:, None] ^ z_index) == jnp.arange(NZ)[None, :]
        bias_here = jnp.sum(jnp.where(own_slot_of[:, :, None], (bias_near + bias_far)[None], 0.0), axis=1)
        bias_part = jnp.where(here[None, :, :, None], bias_here[:, None, None, :], 0.0)
        rows_two = sums_one.shape[0] + sums_two.shape[0]
        value = jnp.concatenate([sums_one, sums_two, bias_part.reshape(-1, sums_two.shape[1])], axis=0)
        for flip in [1 << i for i in range(devices.bit_length() - 1)]:
            value = value + swap(value, flip)
        all_sums = value
        (output,) = layer_output(scalars, middle, send_parts(out_near) + [out_arrived], vectors, dps, after=[input_grad])
        far = swap(hidden_total[2 * block :], tensor)
        up_res, down_res, _ = hidden_adam(
            scalars, hidden_total, far, (w_up, up_m, up_v), (w_down, down_m, down_v), after=[output]
        )
        attn_far = swap(attn_part[block:], tensor)
        qkv_res, out_res = attn_adam(scalars, attn_part, attn_far, w_qkv, qkv_m, qkv_v, w_out, out_m, out_v, after=[up_res[0]])
        vector_total = all_sums[:rows_two]
        bias_total = lax.dynamic_slice_in_dim(
            all_sums[rows_two:].reshape(-1), tensor_index * 2 * hidden_here, 2 * hidden_here, 0
        )

        vec_res = adam_step(vectors, vector_total, vectors_m, vectors_v, 0.3, 0.0)
        bias_res = adam_step(hidden_bias, bias_total, bias_m, bias_v, 0.3, 0.0)
        return (output, input_grad) + vec_res + qkv_res + out_res + up_res + bias_res + down_res

    rows, both = P(AXES, None), P("dp", "tensor")
    turned = P("tensor", "dp")
    in_specs = (
        (rows,) * 2 + (P(),) * 3 + (both,) * 3 + (turned,) * 3 + (both,) * 3 + (P("tensor"),) * 3 + (turned,) * 3
    )
    out_specs = (
        (rows,) * 2 + (P(),) * 4 + (both,) * 4 + (turned,) * 4 + (both,) * 4 + (P("tensor"),) * 4 + (turned,) * 4
    )
    return jax.shard_map(per_device, mesh=mesh, in_specs=in_specs, out_specs=out_specs, check_vma=False)
```

```python
import math

import jax
import jax.numpy as jnp
from jax import lax
from jax.experimental import pallas as pl
from jax.experimental.pallas import tpu as pltpu
from jax.sharding import PartitionSpec as P

HD = 64
SEQ = 576
STEP = 10
NZ = 4
BIAS_ROWS = 16
AXES = ("dp", "tensor")
F32 = jnp.float32
BF16 = jnp.bfloat16
VMEM_LIMIT = 63 * 1024 * 1024
TIMES = {"gate_lower": 1, "gate_gather": 1000, "attn_out": 1000, "feed_out_far": 1000, "feed_out": 5, "attend_whole_back": 20, "first_back": 1000}


def nn(left, right):
    return jnp.dot(left, right, preferred_element_type=F32)


def nt(left, right):
    return lax.dot_general(left, right, (((1,), (1,)), ((), ())), preferred_element_type=F32)


def tn(left, right):
    return lax.dot_general(left, right, (((0,), (0,)), ((), ())), preferred_element_type=F32)


def cost(name, nbytes):
    return pl.CostEstimate(flops=int(5e8 * TIMES.get(name, 0)), bytes_accessed=int(nbytes), transcendentals=0)


def call(body, name, grid, scalars, in_specs, out_specs, out_shape, args, scratch=(), after=(), hold=(), nbytes=0):
    given, extra = len(args), len(after) + len(hold)
    single = not isinstance(out_shape, (list, tuple))
    out_specs, out_shape = ([out_specs], [out_shape]) if single else (list(out_specs), list(out_shape))
    made = len(out_shape)

    def run(sc, *refs):
        rest = refs[given + extra :]
        body(sc, *refs[:given], *rest[:made], *rest[made + len(hold) :])

    anywhere = pl.BlockSpec(memory_space=pltpu.HBM)
    first = 1 + given + len(after)
    out = pl.pallas_call(
        run,
        name=name,
        grid_spec=pltpu.PrefetchScalarGridSpec(
            num_scalar_prefetch=1,
            grid=grid,
            in_specs=list(in_specs) + [anywhere] * extra,
            out_specs=out_specs + [anywhere] * len(hold),
            scratch_shapes=list(scratch),
        ),
        out_shape=out_shape + [shape(h.shape, h.dtype) for h in hold],
        input_output_aliases={first + i: made + i for i in range(len(hold))},
        compiler_params=pltpu.CompilerParams(vmem_limit_bytes=VMEM_LIMIT),
        cost_estimate=cost(name, nbytes),
    )(scalars, *args, *after, *hold)
    return out[0] if single and not hold else tuple(out)


def shape(dims, dtype):
    return jax.ShapeDtypeStruct(dims, dtype)


def whole(dims):
    return pl.BlockSpec(dims, lambda *_: (0,) * len(dims))


def slot(dims):
    return pl.BlockSpec((1,) + dims, lambda s, *_: (s, 0, 0))


def lower_slots(dims):
    return pl.BlockSpec((1,) + dims, lambda s, *_: (jnp.minimum(s, NZ // 2 - 1), 0, 0))


def upper_slots(dims):
    return pl.BlockSpec((1,) + dims, lambda s, *_: (jnp.maximum(s - NZ // 2, 0), 0, 0))


class Copies:
    def __init__(self, sems):
        self.sems, self.used = sems, 0

    def start(self, source, target):
        copy = pltpu.make_async_copy(source, target, self.sems.at[self.used])
        self.used += 1
        copy.start()
        return copy


def wait(copies):
    for copy in copies:
        copy.wait()


def manual(body, name, scalars, args, out_shape, scratch, copies, after=(), hold=()):
    given, extra = len(args), len(after) + len(hold)
    nbytes = sum(math.prod(a.shape) * a.dtype.itemsize for a in list(args) + list(out_shape))

    def run(sc, *refs):
        rest = refs[given + extra :]
        made = len(out_shape) + len(hold)
        body(sc, refs[:given], rest[:made], rest[made:-1], Copies(rest[-1]))

    anywhere = pl.BlockSpec(memory_space=pltpu.HBM)
    first = 1 + given + len(after)
    return pl.pallas_call(
        run,
        name=name,
        in_specs=[pl.BlockSpec(memory_space=pltpu.SMEM)] + [anywhere] * (given + extra),
        out_specs=[anywhere] * (len(out_shape) + len(hold)),
        out_shape=list(out_shape) + [shape(h.shape, h.dtype) for h in hold],
        input_output_aliases={first + i: len(out_shape) + i for i in range(len(hold))},
        scratch_shapes=list(scratch) + [pltpu.SemaphoreType.DMA((copies,))],
        compiler_params=pltpu.CompilerParams(vmem_limit_bytes=VMEM_LIMIT),
        cost_estimate=cost(name, nbytes),
    )(scalars, *args, *after, *hold)


def vmem(dims, dtype=BF16):
    return pltpu.VMEM(dims, dtype)


class Weights:
    def __init__(self, arrays, blocks, block, col, cols):
        full = arrays[0].shape[2]
        if (col % 128 or cols % 128) and cols != full:
            arrays, col, full = [a[:, :, col : col + cols] for a in arrays], 0, cols
        self.args, self.blocks, self.block = list(arrays), blocks, block
        self.col, self.cols, self.full = col, cols, full
        self.depth = block * len(blocks)
        self.flat = cols % 128 == 0
        self.scratch = vmem((self.depth, NZ * cols) if self.flat else (NZ, self.depth, cols))
        self.copies = len(blocks) * NZ

    def load(self, copies, refs, target, sc):
        by_slot = [[] for _ in range(NZ)]
        for z in range(NZ):
            for k, (row, places) in enumerate(self.blocks):
                number, place = places[z]
                source = refs[number].at[place(sc) if callable(place) else place, pl.ds(row, self.block), :]
                if self.cols != self.full:
                    source = source.at[:, pl.ds(self.col, self.cols)]
                rows = pl.ds(k * self.block, self.block)
                goal = target.at[rows, pl.ds(z * self.cols, self.cols)] if self.flat else target.at[z, rows, :]
                by_slot[z].append(copies.start(source, goal))
        return by_slot

    def slots(self, target, first, count):
        if self.flat:
            return target[:, first * self.cols : (first + count) * self.cols]
        assert count == 1
        return target[first]


def slots_at_once(cols):
    for step in (1, 2, 4):
        if cols * step % 512 == 0 and cols % 128 == 0:
            return step
    return 1


class Rows:
    def __init__(self, parts, ordered, swapped=0):
        self.ordered, self.swapped = ordered, swapped
        self.part = parts[0].shape[0]
        self.args = list(parts)
        self.count = self.part * len(parts)
        self.width = parts[0].shape[1]
        self.copies = len(parts) * max(1, swapped)

    def load(self, copies, refs, target, sc, first=0):
        started = []
        for j, ref in enumerate(refs):
            at = first + j * self.part
            if self.ordered and len(refs) > 1:
                at = pl.multiple_of((sc[1] ^ j) * self.part, 16)
            rows = pl.ds(at, self.part)
            if not self.swapped:
                started.append(copies.start(ref, target.at[rows, :]))
                continue
            block = self.width // self.swapped
            for k in range(self.swapped):
                source = ref.at[:, pl.ds((k ^ 1) * block, block)]
                started.append(copies.start(source, target.at[rows, pl.ds(k * block, block)]))
        return started


class Slots:
    def __init__(self, array):
        self.args, self.copies = [array], NZ
        _, self.count, self.cols = array.shape

    def load(self, copies, refs, target, sc, first=0):
        return [[copies.start(refs[0].at[z], target.at[z, pl.ds(first, self.count), :])] for z in range(NZ)]


class SplitSlots:
    def __init__(self, full, mine, theirs):
        self.args, self.copies = [full, mine, theirs], 2 * NZ
        self.count, self.cols = full.shape[1] + mine.shape[1], full.shape[2]

    def load(self, copies, refs, target, sc, first=0):
        full, mine, theirs = refs
        by_slot = [[copies.start(full.at[z], target.at[z, whole_image(sc), :])] for z in range(NZ)]
        for z in range(NZ):
            source = (theirs if z % 2 else mine).at[z // 2]
            by_slot[z].append(copies.start(source, target.at[z, split_rows(sc), :]))
        return by_slot


def ring_place(column, z):
    return column * NZ + jnp.where(column % 2 == 0, z, NZ - 1 - z)


def hidden_place(sc, k, slot):
    return ring_place((sc[0] ^ k) >> 1, sc[3] ^ slot)


def take(items, count):
    return items[:count], items[count:]


def multiply_parts(y, w, flat, parts, copies, outs, sc, ordered, swapped):
    members, part, width = parts.shape

    def product(rows):
        if flat:
            return nt(jnp.concatenate([y[z, rows, :] for z in range(NZ)], axis=1), w[...])
        value = nt(y[0, rows, :], w[0])
        for z in range(1, NZ):
            value += nt(y[z, rows, :], w[z])
        return value

    together = None if part % 16 == 0 else product(slice(None))
    started = []
    for j in range(members):
        if together is not None:
            value = together[j * part : (j + 1) * part]
        else:
            value = product(pl.ds(pl.multiple_of((sc[1] ^ j) * part, 16) if ordered else j * part, part))
        block = width // swapped if swapped else width
        for k in range(width // block):
            to = k ^ 1 if swapped else k
            parts[j, :, to * block : (to + 1) * block] = value[:, k * block : (k + 1) * block].astype(BF16)
        goal = outs[j]
        started.append((j, goal))
        if together is None or not ordered:
            started[-1] = copies.start(parts.at[j], goal)
    if together is not None and ordered:
        started = [copies.start(parts.at[sc[1] ^ j], goal) for j, goal in started]
    return started


def gate(scalars, name, after, hold):
    def body(sc, ins, outs, scratch, copies):
        pass

    return manual(body, name, scalars, [], [], [], 1, after, hold)


def project(scalars, rows, weights, name, after=(), hold=()):
    count, cols = rows.count, weights.cols
    half = SEQ // 2
    chunks = 2 if count % 32 == 0 else 1

    def body(sc, ins, outs, scratch, copies):
        x, w, y = scratch
        row_refs, weight_refs = take(ins, len(rows.args))
        started = rows.load(copies, row_refs, x, sc)
        by_slot = weights.load(copies, weight_refs, w, sc)
        wait(started)
        step, leaving = slots_at_once(cols), []
        for c in range(chunks):
            here = pl.ds(c * (count // chunks), count // chunks)
            for z in range(0, NZ, step):
                if c == 0:
                    for s in range(z, z + step):
                        wait(by_slot[s])
                value = nn(x[here, :], weights.slots(w, z, step))
                for s in range(step):
                    y[z + s, here, :] = value[:, s * cols : (s + 1) * cols].astype(BF16)
                    leaving.append(copies.start(y.at[z + s, here, :], outs[0].at[z + s, here, :]))
        for z in range(1, NZ, 2):
            leaving.append(copies.start(y.at[z, split_rows(sc), :], outs[1].at[z // 2]))
        wait(leaving)

    return manual(
        body, name, scalars, rows.args + weights.args,
        [shape((NZ, count, cols), BF16), shape((NZ // 2, half, cols), BF16)],
        [vmem((count, rows.width)), weights.scratch, vmem((NZ, count, cols))],
        rows.copies + weights.copies + NZ * chunks + NZ // 2, after, hold,
    )


def project_back(scalars, slots, weights, nodes, name, after=(), hold=()):
    count, cols, width = slots.count, weights.cols, weights.depth

    def body(sc, ins, outs, scratch, copies):
        y, w, parts = scratch
        slot_refs, weight_refs = take(ins, len(slots.args))
        for started in slots.load(copies, slot_refs, y, sc) + weights.load(copies, weight_refs, w, sc):
            wait(started)
        wait(multiply_parts(y, w, weights.flat, parts, copies, outs, sc, True, 0))

    return manual(
        body, name, scalars, slots.args + weights.args, [shape((count // nodes, width), BF16)] * nodes,
        [vmem((NZ, count, cols)), weights.scratch, vmem((nodes, count // nodes, width))],
        slots.copies + weights.copies + nodes, after, hold,
    )


def weight_grads(scalars, products, dps, out_shape, goal, side, name, after=(), hold=()):
    counts = [sum(g.count for g in rows) for rows, _ in products]
    widths = [slots[0].cols for _, slots in products]
    width = products[0][0][0].width
    block = width // dps
    parts = 1 if side else len(products)
    cols = sum(widths) if side else widths[0]
    step = max(slots_at_once(c) for c in widths)
    args, scratch, copies_needed = [], [vmem((parts, NZ, width, cols))], parts * NZ * dps
    for (rows, slots), count, own in zip(products, counts, widths):
        args += [a for g in rows + slots for a in g.args]
        scratch += [vmem((count, width)), vmem((NZ, count, own)), vmem((width, count))]
        copies_needed += sum(g.copies for g in rows + slots)

    def body(sc, ins, outs, scratch, copies):
        result = scratch[0]
        loaded = []
        for i, (rows, slots) in enumerate(products):
            x, y, flipped = scratch[1 + 3 * i : 4 + 3 * i]
            started, at = [], 0
            for g in rows:
                refs, ins = take(ins, len(g.args))
                started += g.load(copies, refs, x, sc, at)
                at += g.count
            by_slot, at = [[] for _ in range(NZ)], 0
            for g in slots:
                refs, ins = take(ins, len(g.args))
                for z, some in enumerate(g.load(copies, refs, y, sc, at)):
                    by_slot[z] += some
                at += g.count
            loaded.append((started, by_slot))
        leaving = []

        def send(part, z, ks=range(dps)):
            for k in ks:
                rows = pl.ds(k * block, block)
                leaving.append(copies.start(result.at[part, z, rows, :], goal(sc, outs, part, k, z)))

        def multiply(i, z, at, part, ks=range(dps)):
            y, flipped, own = scratch[2 + 3 * i], scratch[3 + 3 * i], widths[i]
            here = slice(ks[0] * block, (ks[-1] + 1) * block)
            if ks[0] == 0:
                for s in range(z, z + step):
                    wait(loaded[i][1][s])
            whole_y = jnp.concatenate([y[z + s] for s in range(step)], axis=1) if step > 1 else y[z]
            value = nn(flipped[here, :], whole_y)
            for s in range(step):
                result[part, z + s, here, at : at + own] = value[:, s * own : (s + 1) * own].astype(BF16)

        def flip(i):
            wait(loaded[i][0])
            scratch[3 + 3 * i][...] = scratch[1 + 3 * i][...].T

        if side:
            for i in range(len(products)):
                flip(i)
            for ks in (range(dps // 2), range(dps // 2, dps)):
                for z in range(0, NZ, step):
                    for i in range(len(products)):
                        multiply(i, z, sum(widths[:i]), 0, ks)
                    for s in range(z, z + step):
                        send(0, s, ks)
        else:
            for i in range(len(products)):
                flip(i)
                for z in range(0, NZ, step):
                    multiply(i, z, 0, i)
                    for s in range(z, z + step):
                        send(i, s)
        wait(leaving)

    return list(manual(body, name, scalars, args, out_shape, scratch, copies_needed, after, hold))


def gelu_and_slope(u):
    cdf = 0.5 + 0.5 * lax.erf(u * math.sqrt(0.5))
    return u * cdf, cdf + u * (jnp.exp(-0.5 * u * u) * (1.0 / math.sqrt(2.0 * math.pi)))


def feed_forward(scalars, rows, weights, bias_row, name, after=(), hold=()):
    count, cols = rows.count, weights.cols

    def body(sc, ins, outs, scratch, copies):
        x, w, b, hidden, slope = scratch
        row_refs, weight_refs = take(ins, len(rows.args))
        started = rows.load(copies, row_refs, x, sc)
        for z in range(NZ):
            started.append(copies.start(weight_refs[0].at[sc[3] ^ z, pl.ds(bias_row, BIAS_ROWS), :], b.at[z]))
        by_slot = weights.load(copies, weight_refs, w, sc)
        wait(started)
        leaving = []
        step = slots_at_once(cols)
        for z in range(0, NZ, step):
            for s in range(z, z + step):
                wait(by_slot[s])
            value = nn(x[...], weights.slots(w, z, step))
            for s in range(step):
                terms = b[z + s].astype(F32)
                act, steep = gelu_and_slope(value[:, s * cols : (s + 1) * cols] + (terms[0:1] + terms[1:2] + terms[2:3]))
                hidden[z + s] = act.astype(BF16)
                slope[z + s] = steep.astype(BF16)
                leaving.append(copies.start(hidden.at[z + s], outs[0].at[z + s]))
                leaving.append(copies.start(slope.at[z + s], outs[1].at[z + s]))
        wait(leaving)

    return manual(
        body, name, scalars, rows.args + weights.args, [shape((NZ, count, cols), BF16)] * 2,
        [vmem((count, rows.width)), weights.scratch, vmem((NZ, BIAS_ROWS, cols)), vmem((NZ, count, cols)), vmem((NZ, count, cols))],
        rows.copies + NZ + weights.copies + 2 * NZ, after, hold,
    )


def feed_back(scalars, rows, slope, down, up, nodes, swapped, name, after=(), hold=()):
    count, cols, width = rows.count, down.cols, rows.width

    def body(sc, ins, outs, scratch, copies):
        x, wd, wu, steep, du, gb, parts = scratch
        row_refs, ins = take(ins, len(rows.args))
        slope_ref, ins = ins[0], ins[1:]
        down_refs, up_refs = take(ins, len(down.args))
        started = rows.load(copies, row_refs, x, sc)
        down_slots = down.load(copies, down_refs, wd, sc)
        steep_slots = [copies.start(slope_ref.at[z], steep.at[z]) for z in range(NZ)]
        up_slots = up.load(copies, up_refs, wu, sc)
        wait(started)
        leaving = []
        step = slots_at_once(cols)
        for z in range(0, NZ, step):
            for s in range(z, z + step):
                wait(down_slots[s])
                steep_slots[s].wait()
            value = nn(x[...], down.slots(wd, z, step))
            for s in range(step):
                grad = value[:, s * cols : (s + 1) * cols] * steep[z + s].astype(F32)
                gb[z + s : z + s + 1, :] = jnp.sum(grad, axis=0, keepdims=True)
                du[z + s] = grad.astype(BF16)
                leaving.append(copies.start(du.at[z + s], outs[0].at[z + s]))
        leaving.append(copies.start(gb, outs[1]))
        for z in range(NZ):
            wait(up_slots[z])
        wait(leaving + multiply_parts(du, wu, True, parts, copies, outs[2:], sc, False, swapped))

    out = manual(
        body, name, scalars, rows.args + [slope] + down.args + up.args,
        [shape((NZ, count, cols), BF16), shape((NZ, cols), F32)] + [shape((count // nodes, width), BF16)] * nodes,
        [vmem((count, width)), down.scratch, up.scratch, vmem((NZ, count, cols)), vmem((NZ, count, cols)),
         vmem((NZ, cols), F32), vmem((nodes, count // nodes, width))],
        rows.copies + down.copies + up.copies + 2 * NZ + 1 + nodes, after, hold,
    )
    return out[0], out[1], list(out[2 : 2 + nodes]), out[2 + nodes :]


def feed_both(scalars, rows, grads, up, down, bias_row, nodes, swapped, name, after=(), hold=()):
    count, cols, width = rows.count, up.cols, rows.width

    def body(sc, ins, outs, scratch, copies):
        x, g, wu, wd, b, hidden, steep, du, gb, parts = scratch
        row_refs, ins = take(ins, len(rows.args))
        grad_refs, ins = take(ins, len(grads.args))
        up_refs, down_refs = take(ins, len(up.args))
        started = rows.load(copies, row_refs, x, sc)
        for z in range(NZ):
            started.append(copies.start(up_refs[0].at[sc[3] ^ z, pl.ds(bias_row, BIAS_ROWS), :], b.at[z]))
        up_slots = up.load(copies, up_refs, wu, sc)
        grads_started = grads.load(copies, grad_refs, g, sc)
        down_slots = down.load(copies, down_refs, wd, sc)
        wait(started)
        leaving = []
        step = slots_at_once(cols)
        for z in range(0, NZ, step):
            for s in range(z, z + step):
                wait(up_slots[s])
            value = nn(x[...], up.slots(wu, z, step))
            for s in range(step):
                terms = b[z + s].astype(F32)
                act, slope = gelu_and_slope(value[:, s * cols : (s + 1) * cols] + (terms[0:1] + terms[1:2] + terms[2:3]))
                hidden[z + s] = act.astype(BF16)
                steep[z + s] = slope.astype(BF16)
                leaving.append(copies.start(hidden.at[z + s], outs[0].at[z + s]))
        wait(grads_started)
        for z in range(0, NZ, step):
            for s in range(z, z + step):
                wait(down_slots[s])
            value = nn(g[...], down.slots(wd, z, step))
            for s in range(step):
                grad = value[:, s * cols : (s + 1) * cols] * steep[z + s].astype(F32)
                gb[z + s : z + s + 1, :] = jnp.sum(grad, axis=0, keepdims=True)
                du[z + s] = grad.astype(BF16)
                leaving.append(copies.start(du.at[z + s], outs[1].at[z + s]))
        leaving.append(copies.start(gb, outs[2]))
        wait(leaving + multiply_parts(du, wu, True, parts, copies, outs[3:], sc, False, swapped))

    out = manual(
        body, name, scalars, rows.args + grads.args + up.args + down.args,
        [shape((NZ, count, cols), BF16)] * 2 + [shape((NZ, cols), F32)] + [shape((count // nodes, width), BF16)] * nodes,
        [vmem((count, width)), vmem((count, width)), up.scratch, down.scratch, vmem((NZ, BIAS_ROWS, cols)),
         vmem((NZ, count, cols)), vmem((NZ, count, cols)), vmem((NZ, count, cols)), vmem((NZ, cols), F32),
         vmem((nodes, count // nodes, width))],
        rows.copies + grads.copies + up.copies + down.copies + 3 * NZ + 1 + nodes, after, hold,
    )
    return out[0], out[1], out[2], list(out[3 : 3 + nodes]), out[3 + nodes :]


def feed_out(scalars, hidden, down, nodes, swapped, name, after=(), hold=()):
    _, count, cols = hidden.shape
    width = down.depth

    def body(sc, ins, outs, scratch, copies):
        y, w, parts = scratch
        started = [copies.start(ins[0].at[z], y.at[z]) for z in range(NZ)]
        by_slot = down.load(copies, ins[1:], w, sc)
        wait(started)
        for z in range(NZ):
            wait(by_slot[z])
        wait(multiply_parts(y, w, True, parts, copies, outs, sc, False, swapped))

    return manual(
        body, name, scalars, [hidden] + down.args, [shape((count // nodes, width), BF16)] * nodes,
        [vmem((NZ, count, cols)), down.scratch, vmem((nodes, count // nodes, width))],
        NZ + down.copies + nodes, after, hold,
    )


def head_mask(cols, head):
    lane = lax.broadcasted_iota(jnp.int32, (1, cols), 1)
    return (lane >= head * HD) & (lane < (head + 1) * HD)


def by_head_rows(values):
    cols = values.shape[1]
    return jnp.concatenate(
        [jnp.where(head_mask(cols, h), values, 0).astype(BF16) for h in range(cols // HD)], axis=0
    )


def own_columns(stacked, cols):
    count = stacked.shape[0] // (cols // HD)
    total = None
    for h in range(cols // HD):
        piece = jnp.where(head_mask(cols, h), stacked[h * count : (h + 1) * count], 0.0)
        total = piece if total is None else total + piece
    return total


def attend(q, k, v):
    queries = by_head_rows((q * (1.0 / math.sqrt(HD))).astype(BF16))
    scores = nt(k, queries)
    raised = jnp.exp(scores - jnp.max(scores, axis=0, keepdims=True))
    soft = (raised * (1.0 / jnp.sum(raised, axis=0, keepdims=True))).astype(BF16)
    return own_columns(tn(soft, v), q.shape[1]).astype(BF16)


def attend_back(q, k, v, do):
    cols = q.shape[1]
    queries, grads = by_head_rows((q * (1.0 / math.sqrt(HD))).astype(BF16)), by_head_rows(do)
    scores = nt(k, queries)
    raised = jnp.exp(scores - jnp.max(scores, axis=0, keepdims=True))
    soft = raised * (1.0 / jnp.sum(raised, axis=0, keepdims=True))
    dsoft = nt(v, grads)
    dot = jnp.sum(dsoft * soft, axis=0, keepdims=True)
    dscores = (soft * (dsoft - dot)).astype(BF16)
    dv = nn(soft.astype(BF16), grads)
    dk = nn(dscores, queries)
    dq = own_columns(tn(dscores, k), cols) * (1.0 / math.sqrt(HD))
    return dq.astype(BF16), dk.astype(BF16), dv.astype(BF16)


def slots_together(cols):
    return 2 if 2 * cols == 256 else 1


def part_of(pieces, j, cols):
    return jnp.concatenate([p[:, j * cols : (j + 1) * cols] for p in pieces], axis=1) if len(pieces) > 1 else pieces[0][
        :, j * cols : (j + 1) * cols
    ]


def whole_image(sc):
    return pl.ds(pl.multiple_of(sc[2] * (SEQ // 2), 32), SEQ)


def split_rows(sc):
    return pl.ds(pl.multiple_of((1 - sc[2]) * SEQ, 32), SEQ // 2)


def pair_slots(dims, together):
    return pl.BlockSpec((together,) + dims, lambda s, *_: (s, 0, 0))


def own_slots(dims, together):
    return [pl.BlockSpec((1,) + dims, lambda s, *_, i=i: (2 * (s * together + i), 0, 0)) for i in range(together)]


def attend_whole(scalars, qkv, after=(), hold=()):
    slots, count, triple = qkv.shape
    cols = triple // 3
    together = slots_together(cols)

    def body(sc, qkv_ref, o_ref):
        rows = whole_image(sc)
        pieces = [qkv_ref[i, rows, :] for i in range(together)]
        mixed = attend(*(part_of(pieces, j, cols) for j in range(3)))
        for i in range(together):
            o_ref[i] = mixed[:, i * cols : (i + 1) * cols]

    return call(
        body, "attend_whole", (slots // together,), scalars, [pair_slots((count, triple), together)],
        pair_slots((SEQ, cols), together), shape((slots, SEQ, cols), BF16), [qkv],
        after=after, hold=hold, nbytes=2 * slots * count * 4 * cols,
    )


def attend_split(scalars, qkv, partner, after=(), hold=()):
    slots, half, triple = partner.shape
    count = qkv.shape[1]
    cols = triple // 3
    together = slots_together(cols)

    def body(sc, *refs):
        qkv_refs, (partner_ref, mine_ref, theirs_ref, joined) = refs[:together], refs[together:]
        for i, ref in enumerate(qkv_refs):
            joined[i, :half, :] = ref[0, split_rows(sc), :]
            joined[i, half:, :] = partner_ref[i]
        pieces = [joined[i] for i in range(together)]
        mixed = attend(*(part_of(pieces, j, cols) for j in range(3)))
        for i in range(together):
            mine_ref[i] = mixed[:half, i * cols : (i + 1) * cols]
            theirs_ref[i] = mixed[half:, i * cols : (i + 1) * cols]

    return call(
        body, "attend_split", (slots // together,), scalars,
        own_slots((count, triple), together) + [pair_slots((half, triple), together)],
        [pair_slots((half, cols), together)] * 2, [shape((slots, half, cols), BF16)] * 2, [qkv] * together + [partner],
        scratch=[vmem((together, 2 * half, triple))], after=after, hold=hold, nbytes=2 * slots * count * 4 * cols,
    )


def attend_whole_back(scalars, qkv, do, after=(), hold=()):
    slots, count, triple = qkv.shape
    cols = triple // 3
    together = slots_together(cols)

    def body(sc, qkv_ref, do_ref, out_ref):
        rows = whole_image(sc)
        pieces = [qkv_ref[i, rows, :] for i in range(together)]
        do = part_of([do_ref[i, rows, :] for i in range(together)], 0, cols)
        grads = attend_back(*(part_of(pieces, j, cols) for j in range(3)), do)
        for i in range(together):
            for j in range(3):
                out_ref[i, :, j * cols : (j + 1) * cols] = grads[j][:, i * cols : (i + 1) * cols]

    return call(
        body, "attend_whole_back", (slots // together,), scalars,
        [pair_slots((count, triple), together), pair_slots((count, cols), together)],
        pair_slots((SEQ, triple), together), shape((slots, SEQ, triple), BF16), [qkv, do],
        after=after, hold=hold, nbytes=2 * slots * count * 7 * cols,
    )


def attend_split_back(scalars, qkv, partner, do, do_partner, after=(), hold=()):
    slots, half, triple = partner.shape
    count = qkv.shape[1]
    cols = triple // 3
    together = slots_together(cols)

    def body(sc, *refs):
        qkv_refs, do_refs = refs[:together], refs[together : 2 * together]
        partner_ref, do_partner_ref, mine_ref, theirs_ref, joined, joined_do = refs[2 * together :]
        for i in range(together):
            joined[i, :half, :] = qkv_refs[i][0, split_rows(sc), :]
            joined[i, half:, :] = partner_ref[i]
            joined_do[i, :half, :] = do_refs[i][0, split_rows(sc), :]
            joined_do[i, half:, :] = do_partner_ref[i]
        pieces = [joined[i] for i in range(together)]
        do = part_of([joined_do[i] for i in range(together)], 0, cols)
        grads = attend_back(*(part_of(pieces, j, cols) for j in range(3)), do)
        for i in range(together):
            for j in range(3):
                mine_ref[i, :, j * cols : (j + 1) * cols] = grads[j][:half, i * cols : (i + 1) * cols]
                theirs_ref[i, :, j * cols : (j + 1) * cols] = grads[j][half:, i * cols : (i + 1) * cols]

    return call(
        body, "attend_split_back", (slots // together,), scalars,
        own_slots((count, triple), together) + own_slots((count, cols), together)
        + [pair_slots((half, triple), together), pair_slots((half, cols), together)],
        [pair_slots((half, triple), together)] * 2, [shape((slots, half, triple), BF16)] * 2,
        [qkv] * together + [do] * together + [partner, do_partner],
        scratch=[vmem((together, 2 * half, triple)), vmem((together, 2 * half, cols))],
        after=after, hold=hold, nbytes=2 * slots * count * 7 * cols,
    )


def by_rows(body, name, scalars, kinds, out_kinds, out_shape, args, after=(), hold=()):
    count = next(a for a, kind in zip(args, kinds) if kind == "r").shape[0]
    width = args[0].shape[1]
    steps = 3 if count % 48 == 0 else 1
    rows = count // steps
    made = len(out_shape)
    total = sum(steps if kind == "r" else 1 for kind in kinds + out_kinds)

    def part(ref, i):
        return ref.at[pl.ds(i * rows, rows), :]

    def run(sc, ins, outs, scratch, copies):
        here, results, work = scratch[: len(ins)], scratch[len(ins) : len(ins) + made], scratch[-1]
        first = [copies.start(r, h) for r, h, kind in zip(ins, here, kinds) if kind == "w"]
        arriving = [
            [copies.start(part(r, i), part(h, i)) for r, h, kind in zip(ins, here, kinds) if kind == "r"]
            for i in range(steps)
        ]
        wait(first)
        leaving = []
        for i in range(steps):
            wait(arriving[i])
            body(
                i, sc, [part(h, i) if kind == "r" else h for h, kind in zip(here, kinds)],
                [part(h, i) if kind == "r" else h for h, kind in zip(results, out_kinds)], work,
            )
            leaving += [copies.start(part(h, i), part(o, i)) for h, o, kind in zip(results, outs, out_kinds) if kind == "r"]
        leaving += [copies.start(h, o) for h, o, kind in zip(results, outs, out_kinds) if kind == "w"]
        wait(leaving)

    scratch = [vmem(a.shape, a.dtype) for a in list(args) + list(out_shape)] + [vmem((rows, width), F32)]
    return manual(run, name, scalars, args, out_shape, scratch, total, after, hold)


def to_relative(sc, scratch, out_ref, block):
    dps = scratch.shape[1] // block
    for k in range(dps):
        out_ref[:, k * block : (k + 1) * block] = scratch[
            :, pl.ds(pl.multiple_of((sc[0] ^ k) * block, block), block)
        ].astype(out_ref.dtype)


def from_relative(sc, refs, scratch, block):
    dps = scratch.shape[1] // block
    for k in range(dps):
        here = slice(k * block, (k + 1) * block)
        piece = refs[0][:, here].astype(F32)
        for ref in refs[1:]:
            piece += ref[:, here].astype(F32)
        scratch[:, pl.ds(pl.multiple_of((sc[0] ^ k) * block, block), block)] = piece


def normed(rows):
    centred = rows - jnp.mean(rows, axis=-1, keepdims=True)
    inverse = lax.rsqrt(jnp.mean(centred * centred, axis=-1, keepdims=True) + 1e-06)
    return centred * inverse, inverse


def norm_back(hat, inverse, grad, gain):
    scaled = grad * gain
    return inverse * (
        scaled - jnp.mean(scaled, axis=-1, keepdims=True) - hat * jnp.mean(scaled * hat, axis=-1, keepdims=True)
    )


def column(values):
    return jnp.sum(values, axis=0, keepdims=True)


def add_rows(step, ref, values):
    ref[...] = values if step == 0 else ref[...] + values


def first_norm(scalars, tokens, cotangent, vectors, dps, after=(), hold=()):
    count, width = tokens.shape
    block = width // dps

    def body(step, sc, ins, outs, work):
        x_ref, cot_ref, vec_ref = ins
        hat, _ = normed(x_ref[...])
        work[...] = hat * vec_ref[0:1] + vec_ref[1:2]
        to_relative(sc, work, outs[0], block)
        work[...] = cot_ref[...]
        to_relative(sc, work, outs[1], block)

    return by_rows(
        body, "first_norm", scalars, "rrw", "rr", [shape((count, width), BF16)] * 2, [tokens, cotangent, vectors], after, hold
    )


def second_norm(scalars, tokens, parts, vectors, dps, after=(), hold=()):
    count, width = tokens.shape
    block = width // dps

    def body(step, sc, ins, outs, work):
        x_ref, vec_ref, *part_refs = ins
        from_relative(sc, part_refs, work, block)
        h = x_ref[...] + work[...] + vec_ref[4:5]
        outs[0][...] = h
        hat, _ = normed(h)
        work[...] = hat * vec_ref[2:3] + vec_ref[3:4]
        to_relative(sc, work, outs[1], block)

    return by_rows(
        body, "second_norm", scalars, "rw" + "r" * len(parts), "rr",
        [shape((count, width), F32), shape((count, width), BF16)], [tokens, vectors] + list(parts), after, hold,
    )


def layer_output(scalars, middle, parts, vectors, dps, after=(), hold=()):
    count, width = middle.shape
    block = width // dps

    def body(step, sc, ins, outs, work):
        h_ref, vec_ref, *part_refs = ins
        from_relative(sc, part_refs, work, block)
        outs[0][...] = h_ref[...] + work[...] + vec_ref[5:6]

    return by_rows(
        body, "layer_output", scalars, "rw" + "r" * len(parts), "r", [shape((count, width), F32)],
        [middle, vectors] + list(parts), after, hold,
    )


def second_norm_back(scalars, middle, cotangent, parts, vectors, dps, after=(), hold=()):
    count, width = middle.shape
    block = width // dps

    def body(step, sc, ins, outs, work):
        h_ref, cot_ref, vec_ref, *part_refs = ins
        from_relative(sc, part_refs, work, block)
        dc = work[...]
        hat, inverse = normed(h_ref[...])
        cot = cot_ref[...]
        dh = cot + norm_back(hat, inverse, dc, vec_ref[2:3])
        outs[0][...] = dh
        work[...] = dh
        to_relative(sc, work, outs[1], block)
        add_rows(step, outs[2], jnp.concatenate([column(dc * hat), column(dc), column(dh), column(cot)], axis=0))

    return by_rows(
        body, "second_norm_back", scalars, "rrw" + "r" * len(parts), "rrw",
        [shape((count, width), F32), shape((count, width), BF16), shape((4, width), F32)],
        [middle, cotangent, vectors] + list(parts), after, hold,
    )


def first_norm_back(scalars, tokens, middle_grad, parts, vectors, dps, after=(), hold=()):
    count, width = tokens.shape
    block = width // dps

    def body(step, sc, ins, outs, work):
        x_ref, dh_ref, vec_ref, *part_refs = ins
        from_relative(sc, part_refs, work, block)
        da = work[...]
        hat, inverse = normed(x_ref[...])
        outs[0][...] = dh_ref[...] + norm_back(hat, inverse, da, vec_ref[0:1])
        add_rows(step, outs[1], jnp.concatenate([column(da * hat), column(da)], axis=0))

    return by_rows(
        body, "first_norm_back", scalars, "rrw" + "r" * len(parts), "rw",
        [shape((count, width), F32), shape((2, width), F32)], [tokens, middle_grad, vectors] + list(parts), after, hold,
    )


def adam_step(weight, gradient, first, second, rate, decay):
    first = 0.9 * first + 0.1 * gradient
    second = 0.999 * second + 0.001 * gradient * gradient
    first_fix = 1.0 - 0.9**STEP
    second_fix = 1.0 - 0.999**STEP
    update = first / first_fix / (jnp.sqrt(second / second_fix) + 1e-08) + decay * weight
    return (gradient, first, second, weight - rate * update)


def by_part(columns, heads):
    return jnp.concatenate([columns[:, (h * 3 + c) * HD : (h * 3 + c + 1) * HD] for c in range(3) for h in range(heads)], axis=1)


def by_head(columns, heads):
    return jnp.concatenate([columns[:, (c * heads + h) * HD : (c * heads + h + 1) * HD] for h in range(heads) for c in range(3)], axis=1)


def plain(body, name, args, out_shape, after=(), hold=()):
    given, extra = len(args), len(after) + len(hold)
    made = len(out_shape)
    nbytes = sum(math.prod(a.shape) * a.dtype.itemsize for a in list(args) + list(out_shape))

    def run(*refs):
        body(*refs[:given], *refs[given + extra : given + extra + made])

    anywhere = pl.BlockSpec(memory_space=pltpu.HBM)
    here = pl.BlockSpec(memory_space=pltpu.VMEM)
    first = given + len(after)
    return pl.pallas_call(
        run, name=name,
        out_shape=list(out_shape) + [shape(h.shape, h.dtype) for h in hold],
        in_specs=[pl.BlockSpec(memory_space=pltpu.SMEM)] + [here] * (given - 1) + [anywhere] * extra,
        out_specs=[here] * made + [anywhere] * len(hold),
        input_output_aliases={first + i: made + i for i in range(len(hold))},
        compiler_params=pltpu.CompilerParams(vmem_limit_bytes=VMEM_LIMIT), cost_estimate=cost(name, nbytes),
    )(*args, *after, *hold)


def weight_pieces(scalars, w_qkv, w_out, w_up, hidden_bias, w_down):
    block, cols = w_up.shape[0], w_up.shape[1] // 2
    heads, triple = w_qkv.shape[1] // (3 * HD), w_qkv.shape[1]

    def body(sc, qkv_ref, out_ref, up_ref, bias_ref, down_ref, attn_ref, my_up_ref, my_down_ref, theirs_ref):
        attn_ref[:, :triple] = by_part(qkv_ref[...], heads).astype(BF16)
        attn_ref[:, triple:] = out_ref[...].T.astype(BF16)
        mine, other = (pl.ds(pl.multiple_of(h * cols, cols), cols) for h in (sc[4], 1 - sc[4]))
        my_up_ref[:block, :] = up_ref[:, mine].astype(BF16)
        my_down_ref[...] = down_ref[mine, :].T.astype(BF16)
        theirs_ref[:block, :] = up_ref[:, other].astype(BF16)
        theirs_ref[block:, :] = down_ref[other, :].T.astype(BF16)
        rest = bias_ref[:, mine]
        row = lax.broadcasted_iota(jnp.int32, (BIAS_ROWS, cols), 0)
        terms = jnp.zeros((BIAS_ROWS, cols), F32)
        for i in range(3):
            term = rest.astype(BF16).astype(F32)
            terms = jnp.where(row == i, term, terms)
            rest = rest - term
        my_up_ref[block:, :] = terms.astype(BF16)

    return plain(
        body, "weight_pieces", [scalars, w_qkv, w_out, w_up, hidden_bias[None, :], w_down],
        [shape((block, triple + w_out.shape[0]), BF16), shape((block + BIAS_ROWS, cols), BF16),
         shape((block, cols), BF16), shape((2 * block, cols), BF16)],
    )


def attn_adam(scalars, near, far, w_qkv, qkv_m, qkv_v, w_out, out_m, out_v, after=()):
    heads, triple = w_qkv.shape[1] // (3 * HD), w_qkv.shape[1]
    block = far.shape[0]

    def body(sc, near_ref, far_ref, *refs):
        total = near_ref[:block, :].astype(F32) + far_ref[...].astype(F32)
        qw, qm, qv, ow, om, ov = (r[...] for r in refs[:6])
        new = adam_step(qw, by_head(total[:, :triple], heads), qm, qv, 0.1, 0.05)
        new += adam_step(ow, total[:, triple:].T, om, ov, 0.2, 0.05)
        for ref, value in zip(refs[6:], new):
            ref[...] = value

    out = plain(
        body, "attn_adam", [scalars, near, far, w_qkv, qkv_m, qkv_v, w_out, out_m, out_v],
        [shape(w_qkv.shape, F32)] * 4 + [shape(w_out.shape, F32)] * 4, after,
    )
    return tuple(out[:4]), tuple(out[4:])


def hidden_adam(scalars, total, far, up, down, after=(), hold=()):
    block, cols = far.shape[0] // 2, far.shape[1]

    def body(sc, total_ref, far_ref, *refs):
        ins, outs = take(refs, 6)
        up_grad, down_grad = outs[0], outs[4]
        for ref, half in ((total_ref, sc[4]), (far_ref, 1 - sc[4])):
            at = pl.ds(pl.multiple_of(half * cols, cols), cols)
            down_grad[at, :] = ref[:block, :].astype(F32).T
            up_grad[:, at] = ref[block : 2 * block, :].astype(F32)
        for (w, m, v), made, rate in ((ins[:3], outs[:4], 0.1), (ins[3:], outs[4:], 0.05)):
            new = adam_step(w[...], made[0][...], m[...], v[...], rate, 0.05)
            for ref, value in zip(made[1:], new[1:]):
                ref[...] = value

    out = plain(
        body, "hidden_adam", [scalars, total, far] + list(up) + list(down),
        [shape(up[0].shape, F32)] * 4 + [shape(down[0].shape, F32)] * 4, after, hold,
    )
    return tuple(out[:4]), tuple(out[4:8]), out[8:]


def solution(mesh):
    dps, tensor = mesh.shape["dp"], mesh.shape["tensor"]
    nodes = tensor // NZ
    devices = dps * tensor

    def snake(columns):
        return [(d, z) for i, d in enumerate(columns) for z in (range(NZ) if i % 2 == 0 else range(NZ - 1, -1, -1))]

    z_groups = [[d * tensor + z * nodes + c for z in range(NZ)] for d in range(dps) for c in range(nodes)]
    half_rings = [
        [d * tensor + z * nodes + c for d, z in snake(range(x, dps, 2))] for x in range(2) for c in range(nodes)
    ]

    def swap(value, flip):
        return lax.ppermute(value, AXES, [(i, i ^ flip) for i in range(devices)])

    def gather_ring(piece, groups):
        return lax.all_gather(piece, AXES, axis=0, axis_index_groups=groups)

    def scatter_ring(total, groups):
        return lax.psum_scatter(total, AXES, scatter_dimension=0, axis_index_groups=groups, tiled=True)[0]

    def by_weight(k):
        return (bin(k).count("1"), k)

    def gather(own, count, unit, low_first):
        bufs = [own] + [None] * (count - 1)
        for k in sorted(range(1, count), key=by_weight):
            last = k & -k if low_first else 1 << (k.bit_length() - 1)
            bufs[k] = swap(bufs[k ^ last], last * unit)
        return bufs

    def plus(left, right):
        return (left.astype(F32) + right.astype(F32)).astype(BF16)

    def add_up(sums):
        total = sums[0].astype(F32)
        for piece in sums[1:]:
            total = total + piece.astype(F32)
        return total.astype(BF16)

    def along_z(piece):
        return [piece] + [swap(piece, j * nodes) for j in range(1, NZ)]

    def relative(own):
        return [own] + [swap(own, j) for j in range(1, nodes)]

    def ordered_rows(parts, member):
        if parts[0].shape[0] % 16 == 0:
            return Rows(parts, True)
        flip = 1
        while len(parts) > 1:
            odd = (member // flip) % 2 == 1
            parts = [
                jnp.where(odd, jnp.concatenate([b, a], axis=0), jnp.concatenate([a, b], axis=0))
                for a, b in zip(parts[0::2], parts[1::2])
            ]
            flip *= 2
        return Rows(parts, True)

    def relative_rows(parts, swapped=0):
        if parts[0].shape[0] % 16:
            parts = [jnp.concatenate(parts, axis=0)]
        return Rows(parts, False, swapped)

    def send_parts(parts):
        return [parts[0]] + [swap(parts[j], j) for j in range(1, nodes)]

    def per_device(
        tokens, cotangent, vectors, vectors_m, vectors_v,
        w_qkv, qkv_m, qkv_v, w_out, out_m, out_v, w_up, up_m, up_v,
        hidden_bias, bias_m, bias_v, w_down, down_m, down_v,
    ):
        dp_index = lax.axis_index("dp")
        tensor_index = lax.axis_index("tensor")
        z_index, member = tensor_index // nodes, tensor_index % nodes
        odd_x = dp_index % 2
        scalars = jnp.stack([dp_index, member, z_index % 2, z_index, odd_x]).astype(jnp.int32)
        block = w_qkv.shape[0]
        triple, width = w_qkv.shape[1], w_out.shape[0]
        hidden_here = w_up.shape[1] // 2

        attn_own, my_up, my_down, theirs = weight_pieces(scalars, w_qkv, w_out, w_up, hidden_bias, w_down)
        attn_z = along_z(attn_own)
        arrived = swap(theirs, tensor)
        lower, upper = jnp.stack(attn_z[:2]), jnp.stack(attn_z[2:])
        up_piece = jnp.concatenate([my_up, arrived[:block]], axis=0)
        down_piece = jnp.concatenate([my_down, arrived[block:]], axis=0)
        early = attn_own
        if dps == 4:
            lowers, uppers = [swap(lower, tensor), swap(lower, 2 * tensor)], [swap(upper, tensor), swap(upper, 2 * tensor)]
            *lowers, up_piece, down_piece = gate(
                scalars, "gate_lower", [upper], lowers + [up_piece, down_piece]
            )
            early = up_piece
        a_own, g_own = first_norm(scalars, tokens, cotangent, vectors, dps, after=[early])
        a_parts = relative(a_own)
        if dps == 4:
            lowers[0], uppers[1], g_own = gate(
                scalars, "gate_gather", [lowers[1], uppers[0], a_own], [lowers[0], uppers[1], g_own]
            )
            lowers = [lower] + lowers + [swap(lowers[0], 2 * tensor)]
            uppers = [upper] + uppers + [swap(uppers[1], tensor)]
        else:
            lowers, uppers = gather(lower, dps, tensor, False), gather(upper, dps, tensor, True)
        up_z = gather_ring(up_piece, z_groups)
        halves = [(0, [(2 * k + z // 2, z % 2) for z in range(NZ)]) for k in range(dps)]
        attn_w = [half for pair in zip(lowers, uppers) for half in pair]
        qkv_w = Weights(attn_w, halves, block, 0, triple)
        out_w = Weights(attn_w, halves, block, triple, width)

        a_rows = ordered_rows(a_parts, member)
        qkv, qkv_theirs = project(scalars, a_rows, qkv_w, "qkv")
        qkv_partner = swap(qkv_theirs, nodes)
        g_far = swap(g_own, tensor)
        (up_z,) = gate(scalars, "gate_up", [qkv], [up_z])
        up_w = Weights(
            gather(up_z, dps // 2, 2 * tensor, False),
            [(k % 2 * (block + BIAS_ROWS), [(k // 2, lambda sc, z=z: sc[3] ^ z) for z in range(NZ)]) for k in range(dps)],
            block, 0, hidden_here,
        )
        mixed = attend_whole(scalars, qkv, after=[up_z])
        mixed_mine, mixed_theirs, down_piece = attend_split(scalars, qkv, qkv_partner, after=[mixed], hold=[down_piece])
        down_w = Weights(
            [gather_ring(down_piece, half_rings)],
            [(k % 2 * block, [(0, lambda sc, k=k, z=z: hidden_place(sc, k, z)) for z in range(NZ)]) for k in range(dps)],
            block, 0, hidden_here,
        )
        mixed = SplitSlots(mixed, mixed_mine, swap(mixed_theirs, nodes))
        *attn_parts, g_far = project_back(
            scalars, mixed, out_w, nodes, "attn_out", after=up_w.args[1:], hold=[g_far]
        )
        middle, c_own = second_norm(scalars, tokens, send_parts(attn_parts), vectors, dps)

        c_far = swap(c_own, tensor)
        g_rows, g_far = relative_rows(relative(g_own)), relative_rows(relative(g_far), dps)
        c_rows = relative_rows(relative(c_own))
        hidden, slope = feed_forward(scalars, c_rows, up_w, block, "feed_forward")
        du, bias_near, dc_near, _ = feed_back(
            scalars, g_rows, slope, down_w, up_w, nodes, 0, "feed_back", after=[hidden]
        )
        dc_near = send_parts(dc_near)
        (c_far,) = gate(scalars, "gate_rows", [du], [c_far])
        c_far = relative_rows(relative(c_far), dps)
        hidden_far, du_far, bias_far, dc_far, _ = feed_both(
            scalars, c_far, g_far, up_w, down_w, block, nodes, dps, "feed_both", after=[du] + dc_near[1:]
        )
        dc_sum = add_up(send_parts(dc_far))
        dc_arrived = swap(dc_sum, tensor)


        def hidden_goal(sc, outs, part, k, z):
            return outs[0].at[hidden_place(sc, k, z), pl.ds((2 * (k % 2) + part) * block, block), :]

        (hidden_part,) = weight_grads(
            scalars,
            [([g_rows, g_far], [Slots(hidden), Slots(hidden_far)]), ([c_rows, c_far], [Slots(du), Slots(du_far)])],
            dps, [shape((NZ * dps // 2, 4 * block, hidden_here), BF16)],
            hidden_goal, False, "hidden_grad", after=[dc_sum],
        )
        out_far = feed_out(scalars, hidden_far, down_w, nodes, dps, "feed_out_far", after=[hidden_part])
        hidden_total = scatter_ring(hidden_part, half_rings)
        middle_grad, e_own, sums_two = second_norm_back(
            scalars, middle, cotangent, dc_near + [dc_arrived], vectors, dps, after=[out_far[0]]
        )
        out_far = send_parts(out_far)

        e_rows = ordered_rows(relative(e_own), member)
        dmixed, dmixed_theirs = project(scalars, e_rows, out_w, "mixed_grad", after=out_far[1:])
        dmixed_partner = swap(dmixed_theirs, nodes)
        out_near = feed_out(scalars, hidden, down_w, nodes, 0, "feed_out", after=[dmixed])
        dqkv_mine, dqkv_theirs = attend_split_back(
            scalars, qkv, qkv_partner, dmixed, dmixed_partner, after=[out_near[0]]
        )
        dqkv_whole = attend_whole_back(scalars, qkv, dmixed, after=[dqkv_mine])
        dqkv = SplitSlots(dqkv_whole, dqkv_mine, swap(dqkv_theirs, nodes))

        def attn_goal(first, cols):
            def goal(sc, outs, part, k, z):
                place = outs[0].at[hidden_place(sc, k, z), pl.ds((k % 2) * block, block), :]
                return place if cols == triple + width else place.at[:, pl.ds(first, cols)]

            return goal

        attn_shape = [shape((NZ * dps // 2, 2 * block, triple + width), BF16)]
        if triple % 128 == 0 and width % 128 == 0:
            out_part = weight_grads(
                scalars, [([e_rows], [mixed])], dps, attn_shape, attn_goal(triple, width), True, "out_grad",
                after=[dqkv_whole],
            )
            attn_part, out_far[0] = weight_grads(
                scalars, [([a_rows], [dqkv])], dps, [], attn_goal(0, triple), True, "attn_grad",
                hold=out_part + [out_far[0]],
            )
        else:
            attn_part, out_far[0] = weight_grads(
                scalars, [([a_rows], [dqkv]), ([e_rows], [mixed])], dps, attn_shape, attn_goal(0, triple + width), True,
                "attn_grad", hold=[out_far[0]],
            )
        out_arrived = swap(add_up(out_far), tensor)
        da_parts = send_parts(project_back(scalars, dqkv, qkv_w, nodes, "first_back", after=[attn_part]))
        input_grad, sums_one, hidden_total = first_norm_back(
            scalars, tokens, middle_grad, da_parts, vectors, dps, hold=[hidden_total]
        )
        attn_part = scatter_ring(attn_part, half_rings)

        here = (jnp.arange(nodes)[:, None] == member) & (jnp.arange(2)[None, :] == odd_x)
        own_slot_of = (jnp.arange(NZ)[:, None] ^ z_index) == jnp.arange(NZ)[None, :]
        bias_here = jnp.sum(jnp.where(own_slot_of[:, :, None], (bias_near + bias_far)[None], 0.0), axis=1)
        bias_part = jnp.where(here[None, :, :, None], bias_here[:, None, None, :], 0.0)
        rows_two = sums_one.shape[0] + sums_two.shape[0]
        value = jnp.concatenate([sums_one, sums_two, bias_part.reshape(-1, sums_two.shape[1])], axis=0)
        for flip in [1 << i for i in range(devices.bit_length() - 1)]:
            value = value + swap(value, flip)
        all_sums = value
        (output,) = layer_output(scalars, middle, send_parts(out_near) + [out_arrived], vectors, dps, after=[input_grad])
        far = swap(hidden_total[2 * block :], tensor)
        up_res, down_res, _ = hidden_adam(
            scalars, hidden_total, far, (w_up, up_m, up_v), (w_down, down_m, down_v), after=[output]
        )
        attn_far = swap(attn_part[block:], tensor)
        qkv_res, out_res = attn_adam(scalars, attn_part, attn_far, w_qkv, qkv_m, qkv_v, w_out, out_m, out_v, after=[up_res[0]])
        vector_total = all_sums[:rows_two]
        bias_total = lax.dynamic_slice_in_dim(
            all_sums[rows_two:].reshape(-1), tensor_index * 2 * hidden_here, 2 * hidden_here, 0
        )

        vec_res = adam_step(vectors, vector_total, vectors_m, vectors_v, 0.3, 0.0)
        bias_res = adam_step(hidden_bias, bias_total, bias_m, bias_v, 0.3, 0.0)
        return (output, input_grad) + vec_res + qkv_res + out_res + up_res + bias_res + down_res

    rows, both = P(AXES, None), P("dp", "tensor")
    turned = P("tensor", "dp")
    in_specs = (
        (rows,) * 2 + (P(),) * 3 + (both,) * 3 + (turned,) * 3 + (both,) * 3 + (P("tensor"),) * 3 + (turned,) * 3
    )
    out_specs = (
        (rows,) * 2 + (P(),) * 4 + (both,) * 4 + (turned,) * 4 + (both,) * 4 + (P("tensor"),) * 4 + (turned,) * 4
    )
    return jax.shard_map(per_device, mesh=mesh, in_specs=in_specs, out_specs=out_specs, check_vma=False)
```

```python
import math

import jax
import jax.numpy as jnp
from jax import lax
from jax.experimental import pallas as pl
from jax.experimental.pallas import tpu as pltpu
from jax.sharding import PartitionSpec as P

HD = 64
SEQ = 576
STEP = 10
NZ = 4
BIAS_ROWS = 16
AXES = ("dp", "tensor")
F32 = jnp.float32
BF16 = jnp.bfloat16
VMEM_LIMIT = 63 * 1024 * 1024
ROWS_LIMIT = 24 * 1024 * 1024
TIMES = {"gate_lower": 1, "gate_gather": 1000, "attn_out": 1000, "feed_out_far": 1000, "feed_out": 5, "attend_whole_back": 20, "first_back": 1000}


def nn(left, right):
    return jnp.dot(left, right, preferred_element_type=F32)


def nt(left, right):
    return lax.dot_general(left, right, (((1,), (1,)), ((), ())), preferred_element_type=F32)


def tn(left, right):
    return lax.dot_general(left, right, (((0,), (0,)), ((), ())), preferred_element_type=F32)


def cost(name, nbytes):
    return pl.CostEstimate(flops=int(5e8 * TIMES.get(name, 0)), bytes_accessed=int(nbytes), transcendentals=0)


def call(body, name, grid, scalars, in_specs, out_specs, out_shape, args, scratch=(), after=(), hold=(), nbytes=0):
    given, extra = len(args), len(after) + len(hold)
    single = not isinstance(out_shape, (list, tuple))
    out_specs, out_shape = ([out_specs], [out_shape]) if single else (list(out_specs), list(out_shape))
    made = len(out_shape)

    def run(sc, *refs):
        rest = refs[given + extra :]
        body(sc, *refs[:given], *rest[:made], *rest[made + len(hold) :])

    anywhere = pl.BlockSpec(memory_space=pltpu.HBM)
    first = 1 + given + len(after)
    out = pl.pallas_call(
        run,
        name=name,
        grid_spec=pltpu.PrefetchScalarGridSpec(
            num_scalar_prefetch=1,
            grid=grid,
            in_specs=list(in_specs) + [anywhere] * extra,
            out_specs=out_specs + [anywhere] * len(hold),
            scratch_shapes=list(scratch),
        ),
        out_shape=out_shape + [shape(h.shape, h.dtype) for h in hold],
        input_output_aliases={first + i: made + i for i in range(len(hold))},
        compiler_params=pltpu.CompilerParams(vmem_limit_bytes=VMEM_LIMIT),
        cost_estimate=cost(name, nbytes),
    )(scalars, *args, *after, *hold)
    return out[0] if single and not hold else tuple(out)


def shape(dims, dtype):
    return jax.ShapeDtypeStruct(dims, dtype)


def whole(dims):
    return pl.BlockSpec(dims, lambda *_: (0,) * len(dims))


def slot(dims):
    return pl.BlockSpec((1,) + dims, lambda s, *_: (s, 0, 0))


def lower_slots(dims):
    return pl.BlockSpec((1,) + dims, lambda s, *_: (jnp.minimum(s, NZ // 2 - 1), 0, 0))


def upper_slots(dims):
    return pl.BlockSpec((1,) + dims, lambda s, *_: (jnp.maximum(s - NZ // 2, 0), 0, 0))


class Copies:
    def __init__(self, sems):
        self.sems, self.used = sems, 0

    def start(self, source, target):
        copy = pltpu.make_async_copy(source, target, self.sems.at[self.used])
        self.used += 1
        copy.start()
        return copy


def wait(copies):
    for copy in copies:
        copy.wait()


def manual(body, name, scalars, args, out_shape, scratch, copies, after=(), hold=(), limit=VMEM_LIMIT):
    given, extra = len(args), len(after) + len(hold)
    nbytes = sum(math.prod(a.shape) * a.dtype.itemsize for a in list(args) + list(out_shape))

    def run(sc, *refs):
        rest = refs[given + extra :]
        made = len(out_shape) + len(hold)
        body(sc, refs[:given], rest[:made], rest[made:-1], Copies(rest[-1]))

    anywhere = pl.BlockSpec(memory_space=pltpu.HBM if limit == VMEM_LIMIT else pl.ANY)
    first = 1 + given + len(after)
    return pl.pallas_call(
        run,
        name=name,
        in_specs=[pl.BlockSpec(memory_space=pltpu.SMEM)] + [anywhere] * (given + extra),
        out_specs=[anywhere] * (len(out_shape) + len(hold)),
        out_shape=list(out_shape) + [shape(h.shape, h.dtype) for h in hold],
        input_output_aliases={first + i: len(out_shape) + i for i in range(len(hold))},
        scratch_shapes=list(scratch) + [pltpu.SemaphoreType.DMA((copies,))],
        compiler_params=pltpu.CompilerParams(vmem_limit_bytes=limit),
        cost_estimate=cost(name, nbytes),
    )(scalars, *args, *after, *hold)


def vmem(dims, dtype=BF16):
    return pltpu.VMEM(dims, dtype)


class Weights:
    def __init__(self, arrays, blocks, block, col, cols):
        full = arrays[0].shape[2]
        if (col % 128 or cols % 128) and cols != full:
            arrays, col, full = [a[:, :, col : col + cols] for a in arrays], 0, cols
        self.args, self.blocks, self.block = list(arrays), blocks, block
        self.col, self.cols, self.full = col, cols, full
        self.depth = block * len(blocks)
        self.flat = cols % 128 == 0
        self.scratch = vmem((self.depth, NZ * cols) if self.flat else (NZ, self.depth, cols))
        self.copies = len(blocks) * NZ

    def load(self, copies, refs, target, sc):
        by_slot = [[] for _ in range(NZ)]
        for z in range(NZ):
            for k, (row, places) in enumerate(self.blocks):
                number, place = places[z]
                source = refs[number].at[place(sc) if callable(place) else place, pl.ds(row, self.block), :]
                if self.cols != self.full:
                    source = source.at[:, pl.ds(self.col, self.cols)]
                rows = pl.ds(k * self.block, self.block)
                goal = target.at[rows, pl.ds(z * self.cols, self.cols)] if self.flat else target.at[z, rows, :]
                by_slot[z].append(copies.start(source, goal))
        return by_slot

    def slots(self, target, first, count):
        if self.flat:
            return target[:, first * self.cols : (first + count) * self.cols]
        assert count == 1
        return target[first]


def slots_at_once(cols):
    for step in (1, 2, 4):
        if cols * step % 512 == 0 and cols % 128 == 0:
            return step
    return 1


class Rows:
    def __init__(self, parts, ordered, swapped=0):
        self.ordered, self.swapped = ordered, swapped
        self.part = parts[0].shape[0]
        self.args = list(parts)
        self.count = self.part * len(parts)
        self.width = parts[0].shape[1]
        self.copies = len(parts) * max(1, swapped)

    def load(self, copies, refs, target, sc, first=0):
        started = []
        for j, ref in enumerate(refs):
            at = first + j * self.part
            if self.ordered and len(refs) > 1:
                at = pl.multiple_of((sc[1] ^ j) * self.part, 16)
            rows = pl.ds(at, self.part)
            if not self.swapped:
                started.append(copies.start(ref, target.at[rows, :]))
                continue
            block = self.width // self.swapped
            for k in range(self.swapped):
                source = ref.at[:, pl.ds((k ^ 1) * block, block)]
                started.append(copies.start(source, target.at[rows, pl.ds(k * block, block)]))
        return started


class Slots:
    def __init__(self, array):
        self.args, self.copies = [array], NZ
        _, self.count, self.cols = array.shape

    def load(self, copies, refs, target, sc, first=0):
        return [[copies.start(refs[0].at[z], target.at[z, pl.ds(first, self.count), :])] for z in range(NZ)]


class SplitSlots:
    def __init__(self, full, mine, theirs):
        self.args, self.copies = [full, mine, theirs], 2 * NZ
        self.count, self.cols = full.shape[1] + mine.shape[1], full.shape[2]

    def load(self, copies, refs, target, sc, first=0):
        full, mine, theirs = refs
        by_slot = [[copies.start(full.at[z], target.at[z, whole_image(sc), :])] for z in range(NZ)]
        for z in range(NZ):
            source = (theirs if z % 2 else mine).at[z // 2]
            by_slot[z].append(copies.start(source, target.at[z, split_rows(sc), :]))
        return by_slot


def ring_place(column, z):
    return column * NZ + jnp.where(column % 2 == 0, z, NZ - 1 - z)


def hidden_place(sc, k, slot):
    return ring_place((sc[0] ^ k) >> 1, sc[3] ^ slot)


def take(items, count):
    return items[:count], items[count:]


def multiply_parts(y, w, flat, parts, copies, outs, sc, ordered, swapped):
    members, part, width = parts.shape

    def product(rows):
        if flat:
            return nt(jnp.concatenate([y[z, rows, :] for z in range(NZ)], axis=1), w[...])
        value = nt(y[0, rows, :], w[0])
        for z in range(1, NZ):
            value += nt(y[z, rows, :], w[z])
        return value

    together = None if part % 16 == 0 else product(slice(None))
    started = []
    for j in range(members):
        if together is not None:
            value = together[j * part : (j + 1) * part]
        else:
            value = product(pl.ds(pl.multiple_of((sc[1] ^ j) * part, 16) if ordered else j * part, part))
        block = width // swapped if swapped else width
        for k in range(width // block):
            to = k ^ 1 if swapped else k
            parts[j, :, to * block : (to + 1) * block] = value[:, k * block : (k + 1) * block].astype(BF16)
        goal = outs[j]
        started.append((j, goal))
        if together is None or not ordered:
            started[-1] = copies.start(parts.at[j], goal)
    if together is not None and ordered:
        started = [copies.start(parts.at[sc[1] ^ j], goal) for j, goal in started]
    return started


def gate(scalars, name, after, hold):
    def body(sc, ins, outs, scratch, copies):
        pass

    return manual(body, name, scalars, [], [], [], 1, after, hold)


def project(scalars, rows, weights, name, after=(), hold=()):
    count, cols = rows.count, weights.cols
    half = SEQ // 2
    chunks = 2 if count % 32 == 0 else 1

    def body(sc, ins, outs, scratch, copies):
        x, w, y = scratch
        row_refs, weight_refs = take(ins, len(rows.args))
        started = rows.load(copies, row_refs, x, sc)
        by_slot = weights.load(copies, weight_refs, w, sc)
        wait(started)
        step, leaving = slots_at_once(cols), []
        for c in range(chunks):
            here = pl.ds(c * (count // chunks), count // chunks)
            for z in range(0, NZ, step):
                if c == 0:
                    for s in range(z, z + step):
                        wait(by_slot[s])
                value = nn(x[here, :], weights.slots(w, z, step))
                for s in range(step):
                    y[z + s, here, :] = value[:, s * cols : (s + 1) * cols].astype(BF16)
                    leaving.append(copies.start(y.at[z + s, here, :], outs[0].at[z + s, here, :]))
        for z in range(1, NZ, 2):
            leaving.append(copies.start(y.at[z, split_rows(sc), :], outs[1].at[z // 2]))
        wait(leaving)

    return manual(
        body, name, scalars, rows.args + weights.args,
        [shape((NZ, count, cols), BF16), shape((NZ // 2, half, cols), BF16)],
        [vmem((count, rows.width)), weights.scratch, vmem((NZ, count, cols))],
        rows.copies + weights.copies + NZ * chunks + NZ // 2, after, hold,
    )


def project_back(scalars, slots, weights, nodes, name, after=(), hold=()):
    count, cols, width = slots.count, weights.cols, weights.depth

    def body(sc, ins, outs, scratch, copies):
        y, w, parts = scratch
        slot_refs, weight_refs = take(ins, len(slots.args))
        for started in slots.load(copies, slot_refs, y, sc) + weights.load(copies, weight_refs, w, sc):
            wait(started)
        wait(multiply_parts(y, w, weights.flat, parts, copies, outs, sc, True, 0))

    return manual(
        body, name, scalars, slots.args + weights.args, [shape((count // nodes, width), BF16)] * nodes,
        [vmem((NZ, count, cols)), weights.scratch, vmem((nodes, count // nodes, width))],
        slots.copies + weights.copies + nodes, after, hold,
    )


def weight_grads(scalars, products, dps, out_shape, goal, side, name, after=(), hold=()):
    counts = [sum(g.count for g in rows) for rows, _ in products]
    widths = [slots[0].cols for _, slots in products]
    width = products[0][0][0].width
    block = width // dps
    parts = 1 if side else len(products)
    cols = sum(widths) if side else widths[0]
    step = max(slots_at_once(c) for c in widths)
    args, scratch, copies_needed = [], [vmem((parts, NZ, width, cols))], parts * NZ * dps
    for (rows, slots), count, own in zip(products, counts, widths):
        args += [a for g in rows + slots for a in g.args]
        scratch += [vmem((count, width)), vmem((NZ, count, own)), vmem((width, count))]
        copies_needed += sum(g.copies for g in rows + slots)

    def body(sc, ins, outs, scratch, copies):
        result = scratch[0]
        loaded = []
        for i, (rows, slots) in enumerate(products):
            x, y, flipped = scratch[1 + 3 * i : 4 + 3 * i]
            started, at = [], 0
            for g in rows:
                refs, ins = take(ins, len(g.args))
                started += g.load(copies, refs, x, sc, at)
                at += g.count
            by_slot, at = [[] for _ in range(NZ)], 0
            for g in slots:
                refs, ins = take(ins, len(g.args))
                for z, some in enumerate(g.load(copies, refs, y, sc, at)):
                    by_slot[z] += some
                at += g.count
            loaded.append((started, by_slot))
        leaving = []

        def send(part, z, ks=range(dps)):
            for k in ks:
                rows = pl.ds(k * block, block)
                leaving.append(copies.start(result.at[part, z, rows, :], goal(sc, outs, part, k, z)))

        def multiply(i, z, at, part, ks=range(dps)):
            y, flipped, own = scratch[2 + 3 * i], scratch[3 + 3 * i], widths[i]
            here = slice(ks[0] * block, (ks[-1] + 1) * block)
            if ks[0] == 0:
                for s in range(z, z + step):
                    wait(loaded[i][1][s])
            whole_y = jnp.concatenate([y[z + s] for s in range(step)], axis=1) if step > 1 else y[z]
            value = nn(flipped[here, :], whole_y)
            for s in range(step):
                result[part, z + s, here, at : at + own] = value[:, s * own : (s + 1) * own].astype(BF16)

        def flip(i):
            wait(loaded[i][0])
            scratch[3 + 3 * i][...] = scratch[1 + 3 * i][...].T

        if side:
            for i in range(len(products)):
                flip(i)
            for ks in (range(dps // 2), range(dps // 2, dps)):
                for z in range(0, NZ, step):
                    for i in range(len(products)):
                        multiply(i, z, sum(widths[:i]), 0, ks)
                    for s in range(z, z + step):
                        send(0, s, ks)
        else:
            for i in range(len(products)):
                flip(i)
                for z in range(0, NZ, step):
                    multiply(i, z, 0, i)
                    for s in range(z, z + step):
                        send(i, s)
        wait(leaving)

    return list(manual(body, name, scalars, args, out_shape, scratch, copies_needed, after, hold))


def gelu_and_slope(u):
    cdf = 0.5 + 0.5 * lax.erf(u * math.sqrt(0.5))
    return u * cdf, cdf + u * (jnp.exp(-0.5 * u * u) * (1.0 / math.sqrt(2.0 * math.pi)))


def feed_forward(scalars, rows, weights, bias_row, name, after=(), hold=()):
    count, cols = rows.count, weights.cols

    def body(sc, ins, outs, scratch, copies):
        x, w, b, hidden, slope = scratch
        row_refs, weight_refs = take(ins, len(rows.args))
        started = rows.load(copies, row_refs, x, sc)
        for z in range(NZ):
            started.append(copies.start(weight_refs[0].at[sc[3] ^ z, pl.ds(bias_row, BIAS_ROWS), :], b.at[z]))
        by_slot = weights.load(copies, weight_refs, w, sc)
        wait(started)
        leaving = []
        step = slots_at_once(cols)
        for z in range(0, NZ, step):
            for s in range(z, z + step):
                wait(by_slot[s])
            value = nn(x[...], weights.slots(w, z, step))
            for s in range(step):
                terms = b[z + s].astype(F32)
                act, steep = gelu_and_slope(value[:, s * cols : (s + 1) * cols] + (terms[0:1] + terms[1:2] + terms[2:3]))
                hidden[z + s] = act.astype(BF16)
                slope[z + s] = steep.astype(BF16)
                leaving.append(copies.start(hidden.at[z + s], outs[0].at[z + s]))
                leaving.append(copies.start(slope.at[z + s], outs[1].at[z + s]))
        wait(leaving)

    return manual(
        body, name, scalars, rows.args + weights.args, [shape((NZ, count, cols), BF16)] * 2,
        [vmem((count, rows.width)), weights.scratch, vmem((NZ, BIAS_ROWS, cols)), vmem((NZ, count, cols)), vmem((NZ, count, cols))],
        rows.copies + NZ + weights.copies + 2 * NZ, after, hold,
    )


def feed_back(scalars, rows, slope, down, up, nodes, swapped, name, after=(), hold=()):
    count, cols, width = rows.count, down.cols, rows.width

    def body(sc, ins, outs, scratch, copies):
        x, wd, wu, steep, du, gb, parts = scratch
        row_refs, ins = take(ins, len(rows.args))
        slope_ref, ins = ins[0], ins[1:]
        down_refs, up_refs = take(ins, len(down.args))
        started = rows.load(copies, row_refs, x, sc)
        down_slots = down.load(copies, down_refs, wd, sc)
        steep_slots = [copies.start(slope_ref.at[z], steep.at[z]) for z in range(NZ)]
        up_slots = up.load(copies, up_refs, wu, sc)
        wait(started)
        leaving = []
        step = slots_at_once(cols)
        for z in range(0, NZ, step):
            for s in range(z, z + step):
                wait(down_slots[s])
                steep_slots[s].wait()
            value = nn(x[...], down.slots(wd, z, step))
            for s in range(step):
                grad = value[:, s * cols : (s + 1) * cols] * steep[z + s].astype(F32)
                gb[z + s : z + s + 1, :] = jnp.sum(grad, axis=0, keepdims=True)
                du[z + s] = grad.astype(BF16)
                leaving.append(copies.start(du.at[z + s], outs[0].at[z + s]))
        leaving.append(copies.start(gb, outs[1]))
        for z in range(NZ):
            wait(up_slots[z])
        wait(leaving + multiply_parts(du, wu, True, parts, copies, outs[2:], sc, False, swapped))

    out = manual(
        body, name, scalars, rows.args + [slope] + down.args + up.args,
        [shape((NZ, count, cols), BF16), shape((NZ, cols), F32)] + [shape((count // nodes, width), BF16)] * nodes,
        [vmem((count, width)), down.scratch, up.scratch, vmem((NZ, count, cols)), vmem((NZ, count, cols)),
         vmem((NZ, cols), F32), vmem((nodes, count // nodes, width))],
        rows.copies + down.copies + up.copies + 2 * NZ + 1 + nodes, after, hold,
    )
    return out[0], out[1], list(out[2 : 2 + nodes]), out[2 + nodes :]


def feed_both(scalars, rows, grads, up, down, bias_row, nodes, swapped, name, after=(), hold=()):
    count, cols, width = rows.count, up.cols, rows.width

    def body(sc, ins, outs, scratch, copies):
        x, g, wu, wd, b, hidden, steep, du, gb, parts = scratch
        row_refs, ins = take(ins, len(rows.args))
        grad_refs, ins = take(ins, len(grads.args))
        up_refs, down_refs = take(ins, len(up.args))
        started = rows.load(copies, row_refs, x, sc)
        for z in range(NZ):
            started.append(copies.start(up_refs[0].at[sc[3] ^ z, pl.ds(bias_row, BIAS_ROWS), :], b.at[z]))
        up_slots = up.load(copies, up_refs, wu, sc)
        grads_started = grads.load(copies, grad_refs, g, sc)
        down_slots = down.load(copies, down_refs, wd, sc)
        wait(started)
        leaving = []
        step = slots_at_once(cols)
        for z in range(0, NZ, step):
            for s in range(z, z + step):
                wait(up_slots[s])
            value = nn(x[...], up.slots(wu, z, step))
            for s in range(step):
                terms = b[z + s].astype(F32)
                act, slope = gelu_and_slope(value[:, s * cols : (s + 1) * cols] + (terms[0:1] + terms[1:2] + terms[2:3]))
                hidden[z + s] = act.astype(BF16)
                steep[z + s] = slope.astype(BF16)
                leaving.append(copies.start(hidden.at[z + s], outs[0].at[z + s]))
        wait(grads_started)
        for z in range(0, NZ, step):
            for s in range(z, z + step):
                wait(down_slots[s])
            value = nn(g[...], down.slots(wd, z, step))
            for s in range(step):
                grad = value[:, s * cols : (s + 1) * cols] * steep[z + s].astype(F32)
                gb[z + s : z + s + 1, :] = jnp.sum(grad, axis=0, keepdims=True)
                du[z + s] = grad.astype(BF16)
                leaving.append(copies.start(du.at[z + s], outs[1].at[z + s]))
        leaving.append(copies.start(gb, outs[2]))
        wait(leaving + multiply_parts(du, wu, True, parts, copies, outs[3:], sc, False, swapped))

    out = manual(
        body, name, scalars, rows.args + grads.args + up.args + down.args,
        [shape((NZ, count, cols), BF16)] * 2 + [shape((NZ, cols), F32)] + [shape((count // nodes, width), BF16)] * nodes,
        [vmem((count, width)), vmem((count, width)), up.scratch, down.scratch, vmem((NZ, BIAS_ROWS, cols)),
         vmem((NZ, count, cols)), vmem((NZ, count, cols)), vmem((NZ, count, cols)), vmem((NZ, cols), F32),
         vmem((nodes, count // nodes, width))],
        rows.copies + grads.copies + up.copies + down.copies + 3 * NZ + 1 + nodes, after, hold,
    )
    return out[0], out[1], out[2], list(out[3 : 3 + nodes]), out[3 + nodes :]


def feed_out(scalars, hidden, down, nodes, swapped, name, after=(), hold=()):
    _, count, cols = hidden.shape
    width = down.depth

    def body(sc, ins, outs, scratch, copies):
        y, w, parts = scratch
        started = [copies.start(ins[0].at[z], y.at[z]) for z in range(NZ)]
        by_slot = down.load(copies, ins[1:], w, sc)
        wait(started)
        for z in range(NZ):
            wait(by_slot[z])
        wait(multiply_parts(y, w, True, parts, copies, outs, sc, False, swapped))

    return manual(
        body, name, scalars, [hidden] + down.args, [shape((count // nodes, width), BF16)] * nodes,
        [vmem((NZ, count, cols)), down.scratch, vmem((nodes, count // nodes, width))],
        NZ + down.copies + nodes, after, hold,
    )


def head_mask(cols, head):
    lane = lax.broadcasted_iota(jnp.int32, (1, cols), 1)
    return (lane >= head * HD) & (lane < (head + 1) * HD)


def by_head_rows(values):
    cols = values.shape[1]
    return jnp.concatenate(
        [jnp.where(head_mask(cols, h), values, 0).astype(BF16) for h in range(cols // HD)], axis=0
    )


def own_columns(stacked, cols):
    count = stacked.shape[0] // (cols // HD)
    total = None
    for h in range(cols // HD):
        piece = jnp.where(head_mask(cols, h), stacked[h * count : (h + 1) * count], 0.0)
        total = piece if total is None else total + piece
    return total


def attend(q, k, v):
    queries = by_head_rows((q * (1.0 / math.sqrt(HD))).astype(BF16))
    scores = nt(k, queries)
    raised = jnp.exp(scores - jnp.max(scores, axis=0, keepdims=True))
    soft = (raised * (1.0 / jnp.sum(raised, axis=0, keepdims=True))).astype(BF16)
    return own_columns(tn(soft, v), q.shape[1]).astype(BF16)


def attend_back(q, k, v, do):
    cols = q.shape[1]
    queries, grads = by_head_rows((q * (1.0 / math.sqrt(HD))).astype(BF16)), by_head_rows(do)
    scores = nt(k, queries)
    raised = jnp.exp(scores - jnp.max(scores, axis=0, keepdims=True))
    soft = raised * (1.0 / jnp.sum(raised, axis=0, keepdims=True))
    dsoft = nt(v, grads)
    dot = jnp.sum(dsoft * soft, axis=0, keepdims=True)
    dscores = (soft * (dsoft - dot)).astype(BF16)
    dv = nn(soft.astype(BF16), grads)
    dk = nn(dscores, queries)
    dq = own_columns(tn(dscores, k), cols) * (1.0 / math.sqrt(HD))
    return dq.astype(BF16), dk.astype(BF16), dv.astype(BF16)


def slots_together(cols):
    return 2 if 2 * cols == 256 else 1


def part_of(pieces, j, cols):
    return jnp.concatenate([p[:, j * cols : (j + 1) * cols] for p in pieces], axis=1) if len(pieces) > 1 else pieces[0][
        :, j * cols : (j + 1) * cols
    ]


def whole_image(sc):
    return pl.ds(pl.multiple_of(sc[2] * (SEQ // 2), 32), SEQ)


def split_rows(sc):
    return pl.ds(pl.multiple_of((1 - sc[2]) * SEQ, 32), SEQ // 2)


def pair_slots(dims, together):
    return pl.BlockSpec((together,) + dims, lambda s, *_: (s, 0, 0))


def own_slots(dims, together):
    return [pl.BlockSpec((1,) + dims, lambda s, *_, i=i: (2 * (s * together + i), 0, 0)) for i in range(together)]


def attend_whole(scalars, qkv, after=(), hold=()):
    slots, count, triple = qkv.shape
    cols = triple // 3
    together = slots_together(cols)

    def body(sc, qkv_ref, o_ref):
        rows = whole_image(sc)
        pieces = [qkv_ref[i, rows, :] for i in range(together)]
        mixed = attend(*(part_of(pieces, j, cols) for j in range(3)))
        for i in range(together):
            o_ref[i] = mixed[:, i * cols : (i + 1) * cols]

    return call(
        body, "attend_whole", (slots // together,), scalars, [pair_slots((count, triple), together)],
        pair_slots((SEQ, cols), together), shape((slots, SEQ, cols), BF16), [qkv],
        after=after, hold=hold, nbytes=2 * slots * count * 4 * cols,
    )


def attend_split(scalars, qkv, partner, after=(), hold=()):
    slots, half, triple = partner.shape
    count = qkv.shape[1]
    cols = triple // 3
    together = slots_together(cols)

    def body(sc, *refs):
        qkv_refs, (partner_ref, mine_ref, theirs_ref, joined) = refs[:together], refs[together:]
        for i, ref in enumerate(qkv_refs):
            joined[i, :half, :] = ref[0, split_rows(sc), :]
            joined[i, half:, :] = partner_ref[i]
        pieces = [joined[i] for i in range(together)]
        mixed = attend(*(part_of(pieces, j, cols) for j in range(3)))
        for i in range(together):
            mine_ref[i] = mixed[:half, i * cols : (i + 1) * cols]
            theirs_ref[i] = mixed[half:, i * cols : (i + 1) * cols]

    return call(
        body, "attend_split", (slots // together,), scalars,
        own_slots((count, triple), together) + [pair_slots((half, triple), together)],
        [pair_slots((half, cols), together)] * 2, [shape((slots, half, cols), BF16)] * 2, [qkv] * together + [partner],
        scratch=[vmem((together, 2 * half, triple))], after=after, hold=hold, nbytes=2 * slots * count * 4 * cols,
    )


def attend_whole_back(scalars, qkv, do, after=(), hold=()):
    slots, count, triple = qkv.shape
    cols = triple // 3
    together = slots_together(cols)

    def body(sc, qkv_ref, do_ref, out_ref):
        rows = whole_image(sc)
        pieces = [qkv_ref[i, rows, :] for i in range(together)]
        do = part_of([do_ref[i, rows, :] for i in range(together)], 0, cols)
        grads = attend_back(*(part_of(pieces, j, cols) for j in range(3)), do)
        for i in range(together):
            for j in range(3):
                out_ref[i, :, j * cols : (j + 1) * cols] = grads[j][:, i * cols : (i + 1) * cols]

    return call(
        body, "attend_whole_back", (slots // together,), scalars,
        [pair_slots((count, triple), together), pair_slots((count, cols), together)],
        pair_slots((SEQ, triple), together), shape((slots, SEQ, triple), BF16), [qkv, do],
        after=after, hold=hold, nbytes=2 * slots * count * 7 * cols,
    )


def attend_split_back(scalars, qkv, partner, do, do_partner, after=(), hold=()):
    slots, half, triple = partner.shape
    count = qkv.shape[1]
    cols = triple // 3
    together = slots_together(cols)

    def body(sc, *refs):
        qkv_refs, do_refs = refs[:together], refs[together : 2 * together]
        partner_ref, do_partner_ref, mine_ref, theirs_ref, joined, joined_do = refs[2 * together :]
        for i in range(together):
            joined[i, :half, :] = qkv_refs[i][0, split_rows(sc), :]
            joined[i, half:, :] = partner_ref[i]
            joined_do[i, :half, :] = do_refs[i][0, split_rows(sc), :]
            joined_do[i, half:, :] = do_partner_ref[i]
        pieces = [joined[i] for i in range(together)]
        do = part_of([joined_do[i] for i in range(together)], 0, cols)
        grads = attend_back(*(part_of(pieces, j, cols) for j in range(3)), do)
        for i in range(together):
            for j in range(3):
                mine_ref[i, :, j * cols : (j + 1) * cols] = grads[j][:half, i * cols : (i + 1) * cols]
                theirs_ref[i, :, j * cols : (j + 1) * cols] = grads[j][half:, i * cols : (i + 1) * cols]

    return call(
        body, "attend_split_back", (slots // together,), scalars,
        own_slots((count, triple), together) + own_slots((count, cols), together)
        + [pair_slots((half, triple), together), pair_slots((half, cols), together)],
        [pair_slots((half, triple), together)] * 2, [shape((slots, half, triple), BF16)] * 2,
        [qkv] * together + [do] * together + [partner, do_partner],
        scratch=[vmem((together, 2 * half, triple)), vmem((together, 2 * half, cols))],
        after=after, hold=hold, nbytes=2 * slots * count * 7 * cols,
    )


def by_rows(body, name, scalars, kinds, out_kinds, out_shape, args, after=(), hold=()):
    count = next(a for a, kind in zip(args, kinds) if kind == "r").shape[0]
    width = args[0].shape[1]
    steps = 3 if count % 48 == 0 else 1
    rows = count // steps
    made = len(out_shape)
    total = sum(steps if kind == "r" else 1 for kind in kinds + out_kinds)

    def part(ref, i):
        return ref.at[pl.ds(i * rows, rows), :]

    def run(sc, ins, outs, scratch, copies):
        here, results, work = scratch[: len(ins)], scratch[len(ins) : len(ins) + made], scratch[-1]
        first = [copies.start(r, h) for r, h, kind in zip(ins, here, kinds) if kind == "w"]
        arriving = [
            [copies.start(part(r, i), part(h, i)) for r, h, kind in zip(ins, here, kinds) if kind == "r"]
            for i in range(steps)
        ]
        wait(first)
        leaving = []
        for i in range(steps):
            wait(arriving[i])
            body(
                i, sc, [part(h, i) if kind == "r" else h for h, kind in zip(here, kinds)],
                [part(h, i) if kind == "r" else h for h, kind in zip(results, out_kinds)], work,
            )
            leaving += [copies.start(part(h, i), part(o, i)) for h, o, kind in zip(results, outs, out_kinds) if kind == "r"]
        leaving += [copies.start(h, o) for h, o, kind in zip(results, outs, out_kinds) if kind == "w"]
        wait(leaving)

    scratch = [vmem(a.shape, a.dtype) for a in list(args) + list(out_shape)] + [vmem((rows, width), F32)]
    return manual(run, name, scalars, args, out_shape, scratch, total, after, hold, ROWS_LIMIT)


def to_relative(sc, scratch, out_ref, block):
    dps = scratch.shape[1] // block
    for k in range(dps):
        out_ref[:, k * block : (k + 1) * block] = scratch[
            :, pl.ds(pl.multiple_of((sc[0] ^ k) * block, block), block)
        ].astype(out_ref.dtype)


def from_relative(sc, refs, scratch, block):
    dps = scratch.shape[1] // block
    for k in range(dps):
        here = slice(k * block, (k + 1) * block)
        piece = refs[0][:, here].astype(F32)
        for ref in refs[1:]:
            piece += ref[:, here].astype(F32)
        scratch[:, pl.ds(pl.multiple_of((sc[0] ^ k) * block, block), block)] = piece


def normed(rows):
    centred = rows - jnp.mean(rows, axis=-1, keepdims=True)
    inverse = lax.rsqrt(jnp.mean(centred * centred, axis=-1, keepdims=True) + 1e-06)
    return centred * inverse, inverse


def norm_back(hat, inverse, grad, gain):
    scaled = grad * gain
    return inverse * (
        scaled - jnp.mean(scaled, axis=-1, keepdims=True) - hat * jnp.mean(scaled * hat, axis=-1, keepdims=True)
    )


def column(values):
    return jnp.sum(values, axis=0, keepdims=True)


def add_rows(step, ref, values):
    ref[...] = values if step == 0 else ref[...] + values


def first_norm(scalars, tokens, cotangent, vectors, dps, after=(), hold=()):
    count, width = tokens.shape
    block = width // dps

    def body(step, sc, ins, outs, work):
        x_ref, cot_ref, vec_ref = ins
        hat, _ = normed(x_ref[...])
        work[...] = hat * vec_ref[0:1] + vec_ref[1:2]
        to_relative(sc, work, outs[0], block)
        work[...] = cot_ref[...]
        to_relative(sc, work, outs[1], block)

    return by_rows(
        body, "first_norm", scalars, "rrw", "rr", [shape((count, width), BF16)] * 2, [tokens, cotangent, vectors], after, hold
    )


def second_norm(scalars, tokens, parts, vectors, dps, after=(), hold=()):
    count, width = tokens.shape
    block = width // dps

    def body(step, sc, ins, outs, work):
        x_ref, vec_ref, *part_refs = ins
        from_relative(sc, part_refs, work, block)
        h = x_ref[...] + work[...] + vec_ref[4:5]
        outs[0][...] = h
        hat, _ = normed(h)
        work[...] = hat * vec_ref[2:3] + vec_ref[3:4]
        to_relative(sc, work, outs[1], block)

    return by_rows(
        body, "second_norm", scalars, "rw" + "r" * len(parts), "rr",
        [shape((count, width), F32), shape((count, width), BF16)], [tokens, vectors] + list(parts), after, hold,
    )


def layer_output(scalars, middle, parts, vectors, dps, after=(), hold=()):
    count, width = middle.shape
    block = width // dps

    def body(step, sc, ins, outs, work):
        h_ref, vec_ref, *part_refs = ins
        from_relative(sc, part_refs, work, block)
        outs[0][...] = h_ref[...] + work[...] + vec_ref[5:6]

    return by_rows(
        body, "layer_output", scalars, "rw" + "r" * len(parts), "r", [shape((count, width), F32)],
        [middle, vectors] + list(parts), after, hold,
    )


def second_norm_back(scalars, middle, cotangent, parts, vectors, dps, after=(), hold=()):
    count, width = middle.shape
    block = width // dps

    def body(step, sc, ins, outs, work):
        h_ref, cot_ref, vec_ref, *part_refs = ins
        from_relative(sc, part_refs, work, block)
        dc = work[...]
        hat, inverse = normed(h_ref[...])
        cot = cot_ref[...]
        dh = cot + norm_back(hat, inverse, dc, vec_ref[2:3])
        outs[0][...] = dh
        work[...] = dh
        to_relative(sc, work, outs[1], block)
        add_rows(step, outs[2], jnp.concatenate([column(dc * hat), column(dc), column(dh), column(cot)], axis=0))

    return by_rows(
        body, "second_norm_back", scalars, "rrw" + "r" * len(parts), "rrw",
        [shape((count, width), F32), shape((count, width), BF16), shape((4, width), F32)],
        [middle, cotangent, vectors] + list(parts), after, hold,
    )


def first_norm_back(scalars, tokens, middle_grad, parts, vectors, dps, after=(), hold=()):
    count, width = tokens.shape
    block = width // dps

    def body(step, sc, ins, outs, work):
        x_ref, dh_ref, vec_ref, *part_refs = ins
        from_relative(sc, part_refs, work, block)
        da = work[...]
        hat, inverse = normed(x_ref[...])
        outs[0][...] = dh_ref[...] + norm_back(hat, inverse, da, vec_ref[0:1])
        add_rows(step, outs[1], jnp.concatenate([column(da * hat), column(da)], axis=0))

    return by_rows(
        body, "first_norm_back", scalars, "rrw" + "r" * len(parts), "rw",
        [shape((count, width), F32), shape((2, width), F32)], [tokens, middle_grad, vectors] + list(parts), after, hold,
    )


def adam_step(weight, gradient, first, second, rate, decay):
    first = 0.9 * first + 0.1 * gradient
    second = 0.999 * second + 0.001 * gradient * gradient
    first_fix = 1.0 - 0.9**STEP
    second_fix = 1.0 - 0.999**STEP
    update = first / first_fix / (jnp.sqrt(second / second_fix) + 1e-08) + decay * weight
    return (gradient, first, second, weight - rate * update)


def by_part(columns, heads):
    return jnp.concatenate([columns[:, (h * 3 + c) * HD : (h * 3 + c + 1) * HD] for c in range(3) for h in range(heads)], axis=1)


def by_head(columns, heads):
    return jnp.concatenate([columns[:, (c * heads + h) * HD : (c * heads + h + 1) * HD] for h in range(heads) for c in range(3)], axis=1)


def plain(body, name, args, out_shape, after=(), hold=()):
    given, extra = len(args), len(after) + len(hold)
    made = len(out_shape)
    nbytes = sum(math.prod(a.shape) * a.dtype.itemsize for a in list(args) + list(out_shape))

    def run(*refs):
        body(*refs[:given], *refs[given + extra : given + extra + made])

    anywhere = pl.BlockSpec(memory_space=pltpu.HBM)
    here = pl.BlockSpec(memory_space=pltpu.VMEM)
    first = given + len(after)
    return pl.pallas_call(
        run, name=name,
        out_shape=list(out_shape) + [shape(h.shape, h.dtype) for h in hold],
        in_specs=[pl.BlockSpec(memory_space=pltpu.SMEM)] + [here] * (given - 1) + [anywhere] * extra,
        out_specs=[here] * made + [anywhere] * len(hold),
        input_output_aliases={first + i: made + i for i in range(len(hold))},
        compiler_params=pltpu.CompilerParams(vmem_limit_bytes=VMEM_LIMIT), cost_estimate=cost(name, nbytes),
    )(*args, *after, *hold)


def weight_pieces(scalars, w_qkv, w_out, w_up, hidden_bias, w_down):
    block, cols = w_up.shape[0], w_up.shape[1] // 2
    heads, triple = w_qkv.shape[1] // (3 * HD), w_qkv.shape[1]

    def body(sc, qkv_ref, out_ref, up_ref, bias_ref, down_ref, attn_ref, my_up_ref, my_down_ref, theirs_ref):
        attn_ref[:, :triple] = by_part(qkv_ref[...], heads).astype(BF16)
        attn_ref[:, triple:] = out_ref[...].T.astype(BF16)
        mine, other = (pl.ds(pl.multiple_of(h * cols, cols), cols) for h in (sc[4], 1 - sc[4]))
        my_up_ref[:block, :] = up_ref[:, mine].astype(BF16)
        my_down_ref[...] = down_ref[mine, :].T.astype(BF16)
        theirs_ref[:block, :] = up_ref[:, other].astype(BF16)
        theirs_ref[block:, :] = down_ref[other, :].T.astype(BF16)
        rest = bias_ref[:, mine]
        row = lax.broadcasted_iota(jnp.int32, (BIAS_ROWS, cols), 0)
        terms = jnp.zeros((BIAS_ROWS, cols), F32)
        for i in range(3):
            term = rest.astype(BF16).astype(F32)
            terms = jnp.where(row == i, term, terms)
            rest = rest - term
        my_up_ref[block:, :] = terms.astype(BF16)

    return plain(
        body, "weight_pieces", [scalars, w_qkv, w_out, w_up, hidden_bias[None, :], w_down],
        [shape((block, triple + w_out.shape[0]), BF16), shape((block + BIAS_ROWS, cols), BF16),
         shape((block, cols), BF16), shape((2 * block, cols), BF16)],
    )


def attn_adam(scalars, near, far, w_qkv, qkv_m, qkv_v, w_out, out_m, out_v, after=()):
    heads, triple = w_qkv.shape[1] // (3 * HD), w_qkv.shape[1]
    block = far.shape[0]

    def body(sc, near_ref, far_ref, *refs):
        total = near_ref[:block, :].astype(F32) + far_ref[...].astype(F32)
        qw, qm, qv, ow, om, ov = (r[...] for r in refs[:6])
        new = adam_step(qw, by_head(total[:, :triple], heads), qm, qv, 0.1, 0.05)
        new += adam_step(ow, total[:, triple:].T, om, ov, 0.2, 0.05)
        for ref, value in zip(refs[6:], new):
            ref[...] = value

    out = plain(
        body, "attn_adam", [scalars, near, far, w_qkv, qkv_m, qkv_v, w_out, out_m, out_v],
        [shape(w_qkv.shape, F32)] * 4 + [shape(w_out.shape, F32)] * 4, after,
    )
    return tuple(out[:4]), tuple(out[4:])


def hidden_adam(scalars, total, far, up, down, after=(), hold=()):
    block, cols = far.shape[0] // 2, far.shape[1]

    def body(sc, total_ref, far_ref, *refs):
        ins, outs = take(refs, 6)
        up_grad, down_grad = outs[0], outs[4]
        for ref, half in ((total_ref, sc[4]), (far_ref, 1 - sc[4])):
            at = pl.ds(pl.multiple_of(half * cols, cols), cols)
            down_grad[at, :] = ref[:block, :].astype(F32).T
            up_grad[:, at] = ref[block : 2 * block, :].astype(F32)
        for (w, m, v), made, rate in ((ins[:3], outs[:4], 0.1), (ins[3:], outs[4:], 0.05)):
            new = adam_step(w[...], made[0][...], m[...], v[...], rate, 0.05)
            for ref, value in zip(made[1:], new[1:]):
                ref[...] = value

    out = plain(
        body, "hidden_adam", [scalars, total, far] + list(up) + list(down),
        [shape(up[0].shape, F32)] * 4 + [shape(down[0].shape, F32)] * 4, after, hold,
    )
    return tuple(out[:4]), tuple(out[4:8]), out[8:]


def solution(mesh):
    dps, tensor = mesh.shape["dp"], mesh.shape["tensor"]
    nodes = tensor // NZ
    devices = dps * tensor

    def snake(columns):
        return [(d, z) for i, d in enumerate(columns) for z in (range(NZ) if i % 2 == 0 else range(NZ - 1, -1, -1))]

    z_groups = [[d * tensor + z * nodes + c for z in range(NZ)] for d in range(dps) for c in range(nodes)]
    half_rings = [
        [d * tensor + z * nodes + c for d, z in snake(range(x, dps, 2))] for x in range(2) for c in range(nodes)
    ]

    def swap(value, flip):
        return lax.ppermute(value, AXES, [(i, i ^ flip) for i in range(devices)])

    def gather_ring(piece, groups):
        return lax.all_gather(piece, AXES, axis=0, axis_index_groups=groups)

    def scatter_ring(total, groups):
        return lax.psum_scatter(total, AXES, scatter_dimension=0, axis_index_groups=groups, tiled=True)[0]

    def by_weight(k):
        return (bin(k).count("1"), k)

    def gather(own, count, unit, low_first):
        bufs = [own] + [None] * (count - 1)
        for k in sorted(range(1, count), key=by_weight):
            last = k & -k if low_first else 1 << (k.bit_length() - 1)
            bufs[k] = swap(bufs[k ^ last], last * unit)
        return bufs

    def plus(left, right):
        return (left.astype(F32) + right.astype(F32)).astype(BF16)

    def add_up(sums):
        total = sums[0].astype(F32)
        for piece in sums[1:]:
            total = total + piece.astype(F32)
        return total.astype(BF16)

    def along_z(piece):
        return [piece] + [swap(piece, j * nodes) for j in range(1, NZ)]

    def relative(own):
        return [own] + [swap(own, j) for j in range(1, nodes)]

    def ordered_rows(parts, member):
        if parts[0].shape[0] % 16 == 0:
            return Rows(parts, True)
        flip = 1
        while len(parts) > 1:
            odd = (member // flip) % 2 == 1
            parts = [
                jnp.where(odd, jnp.concatenate([b, a], axis=0), jnp.concatenate([a, b], axis=0))
                for a, b in zip(parts[0::2], parts[1::2])
            ]
            flip *= 2
        return Rows(parts, True)

    def relative_rows(parts, swapped=0):
        if parts[0].shape[0] % 16:
            parts = [jnp.concatenate(parts, axis=0)]
        return Rows(parts, False, swapped)

    def send_parts(parts):
        return [parts[0]] + [swap(parts[j], j) for j in range(1, nodes)]

    def per_device(
        tokens, cotangent, vectors, vectors_m, vectors_v,
        w_qkv, qkv_m, qkv_v, w_out, out_m, out_v, w_up, up_m, up_v,
        hidden_bias, bias_m, bias_v, w_down, down_m, down_v,
    ):
        dp_index = lax.axis_index("dp")
        tensor_index = lax.axis_index("tensor")
        z_index, member = tensor_index // nodes, tensor_index % nodes
        odd_x = dp_index % 2
        scalars = jnp.stack([dp_index, member, z_index % 2, z_index, odd_x]).astype(jnp.int32)
        block = w_qkv.shape[0]
        triple, width = w_qkv.shape[1], w_out.shape[0]
        hidden_here = w_up.shape[1] // 2

        attn_own, my_up, my_down, theirs = weight_pieces(scalars, w_qkv, w_out, w_up, hidden_bias, w_down)
        attn_z = along_z(attn_own)
        arrived = swap(theirs, tensor)
        lower, upper = jnp.stack(attn_z[:2]), jnp.stack(attn_z[2:])
        up_piece = jnp.concatenate([my_up, arrived[:block]], axis=0)
        down_piece = jnp.concatenate([my_down, arrived[block:]], axis=0)
        early = attn_own
        if dps == 4:
            lowers, uppers = [swap(lower, tensor), swap(lower, 2 * tensor)], [swap(upper, tensor), swap(upper, 2 * tensor)]
            *lowers, up_piece, down_piece = gate(
                scalars, "gate_lower", [upper], lowers + [up_piece, down_piece]
            )
            early = up_piece
        a_own, g_own = first_norm(scalars, tokens, cotangent, vectors, dps, after=[early])
        a_parts = relative(a_own)
        if dps == 4:
            lowers[0], uppers[1], g_own = gate(
                scalars, "gate_gather", [lowers[1], uppers[0], a_own], [lowers[0], uppers[1], g_own]
            )
            lowers = [lower] + lowers + [swap(lowers[0], 2 * tensor)]
            uppers = [upper] + uppers + [swap(uppers[1], tensor)]
        else:
            lowers, uppers = gather(lower, dps, tensor, False), gather(upper, dps, tensor, True)
        up_z = gather_ring(up_piece, z_groups)
        halves = [(0, [(2 * k + z // 2, z % 2) for z in range(NZ)]) for k in range(dps)]
        attn_w = [half for pair in zip(lowers, uppers) for half in pair]
        qkv_w = Weights(attn_w, halves, block, 0, triple)
        out_w = Weights(attn_w, halves, block, triple, width)

        a_rows = ordered_rows(a_parts, member)
        qkv, qkv_theirs = project(scalars, a_rows, qkv_w, "qkv")
        qkv_partner = swap(qkv_theirs, nodes)
        g_far = swap(g_own, tensor)
        (up_z,) = gate(scalars, "gate_up", [qkv], [up_z])
        up_w = Weights(
            gather(up_z, dps // 2, 2 * tensor, False),
            [(k % 2 * (block + BIAS_ROWS), [(k // 2, lambda sc, z=z: sc[3] ^ z) for z in range(NZ)]) for k in range(dps)],
            block, 0, hidden_here,
        )
        mixed = attend_whole(scalars, qkv, after=[up_z])
        mixed_mine, mixed_theirs, down_piece = attend_split(scalars, qkv, qkv_partner, after=[mixed], hold=[down_piece])
        down_w = Weights(
            [gather_ring(down_piece, half_rings)],
            [(k % 2 * block, [(0, lambda sc, k=k, z=z: hidden_place(sc, k, z)) for z in range(NZ)]) for k in range(dps)],
            block, 0, hidden_here,
        )
        mixed = SplitSlots(mixed, mixed_mine, swap(mixed_theirs, nodes))
        *attn_parts, g_far = project_back(
            scalars, mixed, out_w, nodes, "attn_out", after=up_w.args[1:], hold=[g_far]
        )
        middle, c_own = second_norm(scalars, tokens, send_parts(attn_parts), vectors, dps)

        c_far = swap(c_own, tensor)
        g_rows, g_far = relative_rows(relative(g_own)), relative_rows(relative(g_far), dps)
        c_rows = relative_rows(relative(c_own))
        hidden, slope = feed_forward(scalars, c_rows, up_w, block, "feed_forward")
        du, bias_near, dc_near, _ = feed_back(
            scalars, g_rows, slope, down_w, up_w, nodes, 0, "feed_back", after=[hidden]
        )
        dc_near = send_parts(dc_near)
        (c_far,) = gate(scalars, "gate_rows", [du], [c_far])
        c_far = relative_rows(relative(c_far), dps)
        hidden_far, du_far, bias_far, dc_far, _ = feed_both(
            scalars, c_far, g_far, up_w, down_w, block, nodes, dps, "feed_both", after=[du] + dc_near[1:]
        )
        dc_sum = add_up(send_parts(dc_far))
        dc_arrived = swap(dc_sum, tensor)


        def hidden_goal(sc, outs, part, k, z):
            return outs[0].at[hidden_place(sc, k, z), pl.ds((2 * (k % 2) + part) * block, block), :]

        (hidden_part,) = weight_grads(
            scalars,
            [([g_rows, g_far], [Slots(hidden), Slots(hidden_far)]), ([c_rows, c_far], [Slots(du), Slots(du_far)])],
            dps, [shape((NZ * dps // 2, 4 * block, hidden_here), BF16)],
            hidden_goal, False, "hidden_grad", after=[dc_sum],
        )
        out_far = feed_out(scalars, hidden_far, down_w, nodes, dps, "feed_out_far", after=[hidden_part])
        hidden_total = scatter_ring(hidden_part, half_rings)
        middle_grad, e_own, sums_two = second_norm_back(
            scalars, middle, cotangent, dc_near + [dc_arrived], vectors, dps, after=[out_far[0]]
        )
        out_far = send_parts(out_far)

        e_rows = ordered_rows(relative(e_own), member)
        dmixed, dmixed_theirs = project(scalars, e_rows, out_w, "mixed_grad", after=out_far[1:])
        dmixed_partner = swap(dmixed_theirs, nodes)
        out_near = feed_out(scalars, hidden, down_w, nodes, 0, "feed_out", after=[dmixed])
        dqkv_mine, dqkv_theirs = attend_split_back(
            scalars, qkv, qkv_partner, dmixed, dmixed_partner, after=[out_near[0]]
        )
        dqkv_whole = attend_whole_back(scalars, qkv, dmixed, after=[dqkv_mine])
        dqkv = SplitSlots(dqkv_whole, dqkv_mine, swap(dqkv_theirs, nodes))

        def attn_goal(first, cols):
            def goal(sc, outs, part, k, z):
                place = outs[0].at[hidden_place(sc, k, z), pl.ds((k % 2) * block, block), :]
                return place if cols == triple + width else place.at[:, pl.ds(first, cols)]

            return goal

        attn_shape = [shape((NZ * dps // 2, 2 * block, triple + width), BF16)]
        if triple % 128 == 0 and width % 128 == 0:
            out_part = weight_grads(
                scalars, [([e_rows], [mixed])], dps, attn_shape, attn_goal(triple, width), True, "out_grad",
                after=[dqkv_whole],
            )
            attn_part, out_far[0] = weight_grads(
                scalars, [([a_rows], [dqkv])], dps, [], attn_goal(0, triple), True, "attn_grad",
                hold=out_part + [out_far[0]],
            )
        else:
            attn_part, out_far[0] = weight_grads(
                scalars, [([a_rows], [dqkv]), ([e_rows], [mixed])], dps, attn_shape, attn_goal(0, triple + width), True,
                "attn_grad", hold=[out_far[0]],
            )
        out_arrived = swap(add_up(out_far), tensor)
        da_parts = send_parts(project_back(scalars, dqkv, qkv_w, nodes, "first_back", after=[attn_part]))
        input_grad, sums_one, hidden_total = first_norm_back(
            scalars, tokens, middle_grad, da_parts, vectors, dps, hold=[hidden_total]
        )
        attn_part = scatter_ring(attn_part, half_rings)

        here = (jnp.arange(nodes)[:, None] == member) & (jnp.arange(2)[None, :] == odd_x)
        own_slot_of = (jnp.arange(NZ)[:, None] ^ z_index) == jnp.arange(NZ)[None, :]
        bias_here = jnp.sum(jnp.where(own_slot_of[:, :, None], (bias_near + bias_far)[None], 0.0), axis=1)
        bias_part = jnp.where(here[None, :, :, None], bias_here[:, None, None, :], 0.0)
        rows_two = sums_one.shape[0] + sums_two.shape[0]
        value = jnp.concatenate([sums_one, sums_two, bias_part.reshape(-1, sums_two.shape[1])], axis=0)
        for flip in [1 << i for i in range(devices.bit_length() - 1)]:
            value = value + swap(value, flip)
        all_sums = value
        (output,) = layer_output(scalars, middle, send_parts(out_near) + [out_arrived], vectors, dps, after=[input_grad])
        far = swap(hidden_total[2 * block :], tensor)
        up_res, down_res, _ = hidden_adam(
            scalars, hidden_total, far, (w_up, up_m, up_v), (w_down, down_m, down_v), after=[output]
        )
        attn_far = swap(attn_part[block:], tensor)
        qkv_res, out_res = attn_adam(scalars, attn_part, attn_far, w_qkv, qkv_m, qkv_v, w_out, out_m, out_v, after=[up_res[0]])
        vector_total = all_sums[:rows_two]
        bias_total = lax.dynamic_slice_in_dim(
            all_sums[rows_two:].reshape(-1), tensor_index * 2 * hidden_here, 2 * hidden_here, 0
        )

        vec_res = adam_step(vectors, vector_total, vectors_m, vectors_v, 0.3, 0.0)
        bias_res = adam_step(hidden_bias, bias_total, bias_m, bias_v, 0.3, 0.0)
        return (output, input_grad) + vec_res + qkv_res + out_res + up_res + bias_res + down_res

    rows, both = P(AXES, None), P("dp", "tensor")
    turned = P("tensor", "dp")
    in_specs = (
        (rows,) * 2 + (P(),) * 3 + (both,) * 3 + (turned,) * 3 + (both,) * 3 + (P("tensor"),) * 3 + (turned,) * 3
    )
    out_specs = (
        (rows,) * 2 + (P(),) * 4 + (both,) * 4 + (turned,) * 4 + (both,) * 4 + (P("tensor"),) * 4 + (turned,) * 4
    )
    return jax.shard_map(per_device, mesh=mesh, in_specs=in_specs, out_specs=out_specs, check_vma=False)
```
